512 devices in a mesh: space: 64 (over x, z, core), freq: 8 (over y).
Axes of the slice: x: 4, y: 8, z: 8, core: 2. Of those that a mesh axis runs over, the one named last changes fastest.
Arguments:
- sketch: bfloat16 [16, 64, 5, 512, 128], P('freq', None, None, 'space'), may hold values from -160 to 160
- coupling: float32 [5, 5, 512, 128], P(None, None, 'space'), may hold values from -2.5 to 2.5
- velocity: float32 [512, 128], P('space'), may hold values from 0.5 to 2
- freq_index: int32 [8], replicated, may hold values from 1 to 15, as said below
Outputs:
- basis: float32 [8, 128, 5, 512, 128], P('freq', None, None, 'space')
- factor: float32 [8, 128, 128], P('freq')
The draws below stay inside these ranges and needn't reach their ends.
Inputs may be any that keep to these rules, and one draw needn't show every extreme that they name: `freq_index`: 8 distinct indices, none equal to 0 or to half of 16.
All inputs are finite; a program needn't handle non-finite values.
Results may differ from the reference program's by a relative error of at most 0.0003.
Values may be sent and summed in bfloat16 or wider, within the bound.
No kernel may reach another device: no remote copies, remote signals or barrier semaphores. Data moves between devices by JAX's collectives and lax.ppermute only.
A program may use at most 128 MiB of HBM per device.

```python
import math
import jax
import jax.numpy as jnp
from jax import lax

CR = 128
K = 64
FIELDS = 5
NT = 16
F = 8
NX = 512


def draw_sketch(key, part):
    key = jax.random.fold_in(key, 7)
    k_noise, k_common, k_cols, k_cells = jax.random.split(key, 4)
    full_shape = (NT, K, FIELDS, NX, CR)
    column_scale = jnp.exp(jax.random.uniform(k_cols, (1, K, 1, 1, 1)) * math.log(10.0))
    cell_scale = jnp.exp(jax.random.uniform(k_cells, (1, 1, FIELDS, NX, CR)) * math.log(10.0))
    noise_part = jnp.clip(jax.random.normal(k_noise, full_shape), -4.0, 4.0)
    common = 0.6 * jnp.clip(jax.random.normal(k_common, (NT, 1, FIELDS, NX, CR)), -4.0, 4.0)
    return ((noise_part + common) * column_scale * cell_scale * 0.25).astype(jnp.bfloat16)


def draw_freq_index(key, part):
    key = jax.random.fold_in(key, 11)
    k_middle, k_order = jax.random.split(key, 2)
    middle = jax.random.permutation(k_middle, NT - 4)[:F - 2].astype(jnp.int32) + 1
    chosen = jnp.concatenate([jnp.array([0, NT - 3], dtype=jnp.int32), middle])
    chosen = chosen[jax.random.permutation(k_order, F)]
    return (chosen + 1 + (chosen >= NT // 2 - 1).astype(jnp.int32)).astype(jnp.int32)


def steps_of(rng, dims, pieces, low, largest):
    def one(position, parts):
        draws = jax.random.uniform(jax.random.fold_in(jax.random.fold_in(rng, 6), position), (parts,), jnp.float32, low / len(pieces), largest / len(pieces))
        return jnp.repeat(jnp.exp(draws), dims[position] // parts).reshape((-1,) + (1,) * (len(dims) - position - 1))

    level = one(*pieces[0])
    for cut in pieces[1:]:
        level = level * one(*cut)
    return level


def bell_draw(key, dims, spread, bound, pieces=(), kind=jnp.bfloat16):
    gain = steps_of(key, dims, pieces, -0.22, 0.18) if pieces else 1.0
    values = jax.random.normal(key, dims, jnp.float32) * spread * gain
    return jnp.minimum(jnp.maximum(values, -bound), bound).astype(kind)


def setup_inputs(seed: int = 0) -> dict:
    seeds = jax.random.split(jax.random.key(seed), 5)
    return {
        "sketch": draw_sketch(jax.random.fold_in(seeds[4], 71), 0),
        "coupling": bell_draw(seeds[1], (FIELDS, FIELDS, NX, CR), FIELDS ** -0.5, 2.5, ((2, 64),), jnp.float32),
        "velocity": jnp.clip(jnp.exp(math.log(2.0) - 1.3862944 * jax.random.uniform(seeds[2], (NX, CR), jnp.float32) ** steps_of(seeds[2], (NX, CR), ((0, 64),), -0.2, 0.2)), 0.5, 2.0),
        "freq_index": draw_freq_index(jax.random.fold_in(seeds[4], 71), 0),
    }


STEP_DT = 0.25
VISCOSITY = 0.5

def make_table(indices, slots):
    times = jnp.arange(slots, dtype=jnp.int32)
    phases = indices[:, None].astype(jnp.int32) * times[None, :] % slots
    angles = phases.astype(jnp.float32) * (2.0 * math.pi / slots)
    return jnp.stack([jnp.cos(angles), -jnp.sin(angles)], axis=1).reshape(2 * indices.shape[0], slots)

def advance(padded, velocity, coupling, angular):
    centre = padded[..., 2:-2, :]
    far_plus = padded[..., 4:, :]
    near_plus = padded[..., 3:-1, :]
    near_minus = padded[..., 1:-3, :]
    far_minus = padded[..., :-4, :]
    slope_x = (8.0 * (near_plus - near_minus) - (far_plus - far_minus)) / 12.0
    curve_x = (16.0 * (near_plus + near_minus) - (far_plus + far_minus) - 30.0 * centre) / 12.0
    radial_pad = jnp.pad(centre, [(0, 0)] * (centre.ndim - 1) + [(1, 1)])
    radial = radial_pad[..., 2:] + radial_pad[..., :-2] - 2.0 * centre
    coupled = coupling[0] * centre[:, :, :, 0:1]
    for source in range(1, coupling.shape[0]):
        coupled = coupled + coupling[source] * centre[:, :, :, source:source + 1]
    tendency = velocity * slope_x + VISCOSITY * (curve_x + radial) + coupled
    rotation = jnp.stack([centre[:, 1], -centre[:, 0]], axis=1) * angular[:, None, None, None, None, None]
    return centre + STEP_DT * (tendency + rotation)

def reference(sketch, coupling, velocity, freq_index):
    sketch_float = sketch.astype(jnp.float32)
    row_scale = math.sqrt(FIELDS * NX * CR)

    def one_frequency(index_one):
        cosines = make_table(index_one[None], NT)
        spectra = jnp.einsum('ct,tkvxr->ckvxr', cosines, sketch_float, precision=lax.Precision.HIGHEST)
        fields = spectra.reshape(1, 2, K, FIELDS, NX, CR)
        angular = math.pi / NT * index_one[None].astype(jnp.float32)
        for repeat in range(2):
            padded = jnp.pad(fields, [(0, 0)] * 4 + [(2, 2), (0, 0)])
            fields = advance(padded, velocity, coupling, angular)
        columns = fields.reshape(2 * K, FIELDS * NX * CR)
        gram_total = jnp.dot(columns.astype(jnp.float32), columns.T.astype(jnp.float32), precision=lax.Precision.HIGHEST, preferred_element_type=jnp.float32)
        chol_factor = jnp.linalg.cholesky(gram_total)
        basis_one = jax.scipy.linalg.solve_triangular(chol_factor, columns, lower=True) * row_scale
        return (basis_one.reshape(2 * K, FIELDS, NX, CR), chol_factor / row_scale)
    basis_all, factor_all = lax.map(one_frequency, freq_index)
    return (basis_all, factor_all)
```

```python
from functools import partial
import math

import jax
import jax.numpy as jnp
from jax import lax
from jax.sharding import PartitionSpec as P

K = 64
FIELDS = 5
NT = 16
F = 8


STEP_DT = 0.25
VISCOSITY = 0.5


def with_halo(value, sides, width):
    for axis, dim in sides:
        count, length = (lax.axis_size(axis), value.shape[dim])
        up = [(i, (i + 1) % count) for i in range(count - 1)]
        down = [(j, i) for i, j in up]
        last = lax.slice_in_dim(value, length - width, length, axis=dim)
        leading = lax.slice_in_dim(value, 0, width, axis=dim)
        before = lax.ppermute(last, axis, up)
        after = lax.ppermute(leading, axis, down)
        value = jnp.concatenate([before, value, after], axis=dim)
    return value


def butterfly_sum(value, axis):
    count = lax.axis_size(axis)
    stride = 1
    while stride < count:
        value = value + lax.ppermute(value, axis, [(i, i ^ stride) for i in range(count)])
        stride *= 2
    return value


def make_table(indices, slots):
    times = jnp.arange(slots, dtype=jnp.int32)
    phases = indices[:, None] * times[None, :] % slots
    angles = phases.astype(jnp.float32) * (2.0 * math.pi / slots)
    return jnp.stack([jnp.cos(angles), -jnp.sin(angles)], axis=1).reshape(
        2 * indices.shape[0], slots
    )


def advance(padded, velocity, coupling, angular):
    centre = padded[..., 2:-2, :]
    far_plus = padded[..., 4:, :]
    near_plus = padded[..., 3:-1, :]
    near_minus = padded[..., 1:-3, :]
    far_minus = padded[..., :-4, :]
    slope_x = (8.0 * (near_plus - near_minus) - (far_plus - far_minus)) / 12.0
    curve_x = (16.0 * (near_plus + near_minus) - (far_plus + far_minus) - 30.0 * centre) / 12.0
    radial_pad = jnp.pad(centre, [(0, 0)] * (centre.ndim - 1) + [(1, 1)])
    radial = radial_pad[..., 2:] + radial_pad[..., :-2] - 2.0 * centre
    coupled = coupling[0] * centre[:, :, :, 0:1]
    for source in range(1, coupling.shape[0]):
        coupled = coupled + coupling[source] * centre[:, :, :, source : source + 1]
    tendency = velocity * slope_x + VISCOSITY * (curve_x + radial) + coupled
    rotation = (
        jnp.stack([centre[:, 1], -centre[:, 0]], axis=1) * angular[:, None, None, None, None, None]
    )
    return centre + STEP_DT * (tendency + rotation)


def local(sketch, coupling, velocity, freq_index):
    group_size = lax.axis_size("freq")
    per_group = F // group_size
    row_count = sketch.shape[3]
    radial_count = sketch.shape[4]
    own_index = lax.dynamic_slice_in_dim(freq_index, lax.axis_index("freq") * per_group, per_group)
    angular = math.pi / NT * own_index.astype(jnp.float32)
    cosines = make_table(freq_index, NT)
    spectra = jnp.einsum(
        "ct,tkvxr->ckvxr",
        cosines,
        lax.all_to_all(sketch, "freq", split_axis=3, concat_axis=0, tiled=True).astype(jnp.float32),
        precision=lax.Precision.HIGHEST,
    )
    fields = lax.all_to_all(spectra, "freq", split_axis=0, concat_axis=3, tiled=True)
    fields = fields.reshape(per_group, 2, K, FIELDS, row_count, radial_count)
    for repeat in range(2):
        padded = with_halo(fields, (("space", 4),), 2)
        fields = advance(padded, velocity, coupling, angular)
    columns = fields.reshape(per_group, 2 * K, FIELDS * row_count * radial_count)
    partial_gram = jnp.einsum("fir,fjr->fij", columns, columns, precision=lax.Precision.HIGHEST)
    gram_total = butterfly_sum(partial_gram, "space")
    chol_factor = jnp.linalg.cholesky(gram_total)
    row_scale = math.sqrt(FIELDS * row_count * lax.axis_size("space") * radial_count)
    solved = jax.vmap(partial(jax.scipy.linalg.solve_triangular, lower=True))(chol_factor, columns)
    basis_out = (solved * row_scale).reshape(per_group, 2 * K, FIELDS, row_count, radial_count)
    return (basis_out, chol_factor / row_scale)


def solution(mesh):
    return jax.shard_map(
        local,
        mesh=mesh,
        in_specs=(
            P("freq", None, None, "space", None),
            P(None, None, "space", None),
            P("space", None),
            P(),
        ),
        out_specs=(P("freq", None, None, "space", None), P("freq", None, None)),
        check_vma=False,
    )
```

```python
from functools import partial
import math

import jax
import jax.numpy as jnp
from jax import lax
from jax.experimental import pallas as pl
from jax.experimental.pallas import tpu as pltpu
from jax.sharding import PartitionSpec as P

K = 64
FIELDS = 5
NT = 16
F = 8
STEP_DT = 0.25
VISCOSITY = 0.5
LANES = 2 * K
HALF = 4
RH = 2
VMEM_LIMIT = 50 * 1024 * 1024


def butterfly_sum(value, axis):
    count = lax.axis_size(axis)
    stride = 1
    while stride < count:
        value = value + lax.ppermute(value, axis, [(i, i ^ stride) for i in range(count)])
        stride *= 2
    return value


def spread_body(sketch_ref, low_ref, high_ref, rows_ref, turned_ref):
    groups = low_ref.shape[0]
    radial = sketch_ref.shape[4]
    per = radial // groups
    rows_ref[...] = sketch_ref[...].astype(jnp.float32).reshape(LANES * 8, radial)
    edge = jnp.zeros((RH * HALF, LANES), jnp.float32)
    for half in range(2):
        turned_ref[half, 0 : RH * HALF, :] = edge
        turned_ref[half, (radial + RH) * HALF :, :] = edge
    for x in range(8):
        block = rows_ref[pl.ds(x, LANES, stride=8), :]
        turned_ref[x // HALF, pl.ds(RH * HALF + x % HALF, radial, stride=HALF), :] = block.T
    count = (per + 2 * RH) * HALF
    for half, ref in ((0, low_ref), (1, high_ref)):
        for group in range(groups):
            start = group * per * HALF
            ref[group] = turned_ref[half, start : start + count, :].astype(jnp.bfloat16)


def spread(sketch, groups):
    radial = sketch.shape[4]
    rows = (radial // groups + 2 * RH) * HALF
    shape = jax.ShapeDtypeStruct((groups, FIELDS * rows, LANES), jnp.bfloat16)
    return pl.pallas_call(
        spread_body,
        grid=(FIELDS,),
        in_specs=[pl.BlockSpec((2, K, 1, 8, radial), lambda i: (0, 0, i, 0, 0))],
        out_specs=[pl.BlockSpec((groups, rows, LANES), lambda i: (0, i, 0))] * 2,
        out_shape=[shape, shape],
        scratch_shapes=[
            pltpu.VMEM((LANES * 8, radial), jnp.float32),
            pltpu.VMEM((2, (radial + 2 * RH) * HALF, LANES), jnp.float32),
        ],
        compiler_params=pltpu.CompilerParams(vmem_limit_bytes=VMEM_LIMIT),
        name="spread",
    )(sketch)


def evolve_body(
    parity_ref, low_ref, high_ref, right_ref, left_ref, table_ref, coef_ref, mask_ref, turn_ref,
    out_ref, gram_ref, pair_ref, z_ref, s_ref,
):
    per = z_ref.shape[2] - 2 * RH
    rows = FIELDS * (per + 2 * RH) * HALF
    lane = lax.broadcasted_iota(jnp.int32, (16, LANES), 1)
    first = lane < K

    for quarter, ref in enumerate((low_ref, high_ref, right_ref, left_ref)):

        @pl.loop(0, rows // 16)
        def _(step):
            start = pl.multiple_of(step * 16, 16)
            for d in range(4):
                a = ref[d, pl.ds(start, 16), :].astype(jnp.float32)
                b = ref[d + 4, pl.ds(start, 16), :].astype(jnp.float32)
                pair_ref[0, d] = a + b
                pair_ref[1, d] = a - b
            line = step * 4
            field = line // (per + 2 * RH)
            cell = line % (per + 2 * RH)
            for f in range(F):
                parity = parity_ref[f]
                p = [pair_ref[parity, d] for d in range(4)]
                u = p[0] * table_ref[f, 0, 0:1]
                v = p[0] * table_ref[f, 1, 0:1]
                for d in range(1, 4):
                    u = u + p[d] * table_ref[f, 0, d : d + 1]
                    v = v + p[d] * table_ref[f, 1, d : d + 1]
                z = jnp.where(first, u, v) + pltpu.roll(jnp.where(first, v, u), K, 1)
                for c in range(4):
                    z_ref[f, field, cell + c, quarter * HALF : (quarter + 1) * HALF, :] = z[
                        c * HALF : (c + 1) * HALF
                    ]

    def advance(q, before, after, f, r):
        turn = turn_ref[f]
        values = []
        for i in range(FIELDS):
            value = coef_ref[i, r] * q[0]
            for j in range(1, FIELDS):
                value = value + coef_ref[j * FIELDS + i, r] * q[j]
            here = q[i]
            value = value + coef_ref[25, r] * pltpu.roll(here, 15, 0)
            value = value + coef_ref[26, r] * pltpu.roll(here, 1, 0)
            value = value + coef_ref[27, r] * pltpu.roll(here, 14, 0)
            value = value + coef_ref[28, r] * pltpu.roll(here, 2, 0)
            value = value + (STEP_DT * VISCOSITY) * (before[i] + after[i])
            value = value + turn * pltpu.roll(here, K, 1)
            values.append(value)
        return values

    @pl.loop(0, per + 2)
    def _(r):
        mask = mask_ref[r]

        @pl.loop(0, F)
        def _(f):
            q = [z_ref[f, i, r + 1] for i in range(FIELDS)]
            before = [z_ref[f, i, r] for i in range(FIELDS)]
            after = [z_ref[f, i, r + 2] for i in range(FIELDS)]
            for i, value in enumerate(advance(q, before, after, f, r)):
                s_ref[f, i, r] = value * mask

    @pl.loop(0, per)
    def _(r):
        @pl.loop(0, F)
        def _(f):
            q = [s_ref[f, i, r + 1] for i in range(FIELDS)]
            before = [s_ref[f, i, r] for i in range(FIELDS)]
            after = [s_ref[f, i, r + 2] for i in range(FIELDS)]
            for i, value in enumerate(advance(q, before, after, f, r + 1)):
                out_ref[f, pl.ds(i * 8 * per + r, 8, stride=per), :] = value[0:8]

    @pl.loop(0, F)
    def _(f):
        block = out_ref[f]
        gram_ref[f] = lax.dot_general(
            block, block, (((0,), (0,)), ((), ())),
            precision=lax.Precision.HIGHEST, preferred_element_type=jnp.float32,
        )


def evolve(parity, low, high, right, left, table, coef, mask, turn):
    per = coef.shape[1] - 2
    vmem = pl.BlockSpec(memory_space=pltpu.VMEM)
    return pl.pallas_call(
        evolve_body,
        in_specs=[pl.BlockSpec(memory_space=pltpu.SMEM)] + [vmem] * 8,
        out_specs=[vmem, vmem],
        out_shape=[
            jax.ShapeDtypeStruct((F, FIELDS * 8 * per, LANES), jnp.float32),
            jax.ShapeDtypeStruct((F, LANES, LANES), jnp.float32),
        ],
        scratch_shapes=[
            pltpu.VMEM((2, 4, 16, LANES), jnp.float32),
            pltpu.VMEM((F, FIELDS, per + 2 * RH, 16, LANES), jnp.float32),
            pltpu.VMEM((F, FIELDS, per + 2, 16, LANES), jnp.float32),
        ],
        compiler_params=pltpu.CompilerParams(vmem_limit_bytes=VMEM_LIMIT),
        name="evolve",
    )(parity, low, high, right, left, table, coef, mask, turn)


def apply_body(place_ref, inverse_ref, *refs):
    chunks = refs[:F]
    out_ref, rows_ref, all_ref = refs[F:]
    per = chunks[0].shape[0] // 8
    radial = per * F
    inverse = inverse_ref[...]
    for x in range(8):
        for d in range(F):
            spot = pl.multiple_of(place_ref[d] * per, per)
            all_ref[x, pl.ds(spot, per), :] = chunks[d][x * per : (x + 1) * per, :]
    for x in range(8):
        rows_ref[pl.ds(x, LANES, stride=8), :] = lax.dot_general(
            inverse, all_ref[x], (((1,), (1,)), ((), ())),
            precision=lax.Precision.HIGHEST, preferred_element_type=jnp.float32,
        )
    out_ref[...] = rows_ref[...].reshape(out_ref.shape)


def apply(place, inverse, chunks):
    per = chunks[0].shape[0] // (8 * FIELDS)
    radial = per * F
    return pl.pallas_call(
        apply_body,
        grid=(FIELDS,),
        in_specs=[
            pl.BlockSpec(memory_space=pltpu.SMEM),
            pl.BlockSpec((LANES, LANES), lambda i: (0, 0)),
        ]
        + [pl.BlockSpec((8 * per, LANES), lambda i: (i, 0))] * F,
        out_specs=pl.BlockSpec((1, LANES, 1, 8, radial), lambda i: (0, 0, i, 0, 0)),
        out_shape=jax.ShapeDtypeStruct((1, LANES, FIELDS, 8, radial), jnp.float32),
        scratch_shapes=[
            pltpu.VMEM((LANES * 8, radial), jnp.float32),
            pltpu.VMEM((8, radial, LANES), jnp.float32),
        ],
        compiler_params=pltpu.CompilerParams(vmem_limit_bytes=VMEM_LIMIT),
        name="apply",
    )(place, inverse, *chunks)


def make_table(indices, slots):
    times = jnp.arange(slots, dtype=jnp.int32)
    phases = indices[:, None] * times[None, :] % slots
    angles = phases.astype(jnp.float32) * (2.0 * math.pi / slots)
    return jnp.stack([jnp.cos(angles), -jnp.sin(angles)], axis=1)


def stencil(coupling, velocity, per):
    count = lax.axis_size("space")
    mine = lax.axis_index("space")
    start = lax.axis_index("freq") * per
    radial = velocity.shape[1]
    up = [(i, i + 1) for i in range(count - 1)]
    down = [(i + 1, i) for i in range(count - 1)]
    both = jnp.concatenate([coupling.reshape(FIELDS * FIELDS, 8, radial), velocity[None]], axis=0)
    right = lax.ppermute(both[:, :2], "space", down)
    left = lax.ppermute(both[:, 6:], "space", up)
    gap = jnp.zeros((both.shape[0], 4, radial), jnp.float32)
    full = jnp.concatenate([both, right, gap, left], axis=1)
    full = jnp.pad(full, ((0, 0), (0, 0), (1, 1)))
    full = lax.dynamic_slice_in_dim(full, start, per + 2, axis=2).transpose(0, 2, 1)
    speed = full[FIELDS * FIELDS]
    coupled = STEP_DT * full[: FIELDS * FIELDS]
    centre = 1.0 - STEP_DT * VISCOSITY * (30.0 / 12.0 + 2.0)
    diagonal = jnp.eye(FIELDS, dtype=jnp.float32).reshape(-1) * centre
    coupled = coupled + diagonal[:, None, None]
    near_d, near_c = STEP_DT * 8.0 / 12.0, STEP_DT * VISCOSITY * 16.0 / 12.0
    far_d, far_c = STEP_DT / 12.0, STEP_DT * VISCOSITY / 12.0
    shifts = jnp.stack(
        [near_d * speed + near_c, near_c - near_d * speed, -far_d * speed - far_c, far_d * speed - far_c]
    )
    coef = jnp.concatenate([coupled, shifts], axis=0)
    coef = jnp.broadcast_to(coef[..., None], coef.shape + (LANES,))
    r = start - 1 + jnp.arange(per + 2)
    place = jnp.arange(16)
    inside = (place < 8) | ((place < 12) & (mine < count - 1)) | ((place >= 12) & (mine > 0))
    mask = ((r >= 0) & (r < radial))[:, None] & inside[None, :]
    mask = jnp.broadcast_to(mask.astype(jnp.float32)[..., None], mask.shape + (LANES,))
    return coef, mask


def local(sketch, coupling, velocity, freq_index):
    groups = lax.axis_size("freq")
    count = lax.axis_size("space")
    radial = sketch.shape[4]
    per = radial // groups
    mine = lax.axis_index("freq")
    low, high = spread(sketch, groups)
    low = lax.all_to_all(low, "freq", split_axis=0, concat_axis=0, tiled=True)
    high = lax.all_to_all(high, "freq", split_axis=0, concat_axis=0, tiled=True)
    right = lax.ppermute(low, "space", [(i + 1, i) for i in range(count - 1)])
    left = lax.ppermute(high, "space", [(i, i + 1) for i in range(count - 1)])

    waves = make_table(freq_index, NT)[:, :, : NT // 2].reshape(F, 2, 4, 2)
    waves = jnp.repeat(waves, K, axis=3)
    coef, mask = stencil(coupling, velocity, per)
    angular = math.pi / NT * STEP_DT * freq_index.astype(jnp.float32)
    sign = jnp.where(jnp.arange(LANES) < K, 1.0, -1.0).astype(jnp.float32)
    turn = jnp.broadcast_to((angular[:, None] * sign)[:, None, :], (F, 16, LANES))
    columns, grams = evolve(freq_index % 2, low, high, right, left, waves, coef, mask, turn)

    parts = lax.all_to_all(grams, "freq", split_axis=0, concat_axis=0, tiled=True)
    gram = jnp.sum(parts, axis=0)
    columns, gram = lax.optimization_barrier((columns, gram))
    chunks = []
    for shift in range(groups):
        chunk = lax.dynamic_index_in_dim(columns, (mine + shift) % groups, 0, keepdims=False)
        if shift:
            chunk = lax.ppermute(chunk, "freq", [(i, (i + shift) % groups) for i in range(groups)])
        chunks.append(chunk)
    gram = butterfly_sum(gram, "space")
    chol = jnp.linalg.cholesky(gram)
    row_scale = math.sqrt(FIELDS * 8 * count * radial)
    inverse = jax.scipy.linalg.solve_triangular(chol, row_scale * jnp.eye(LANES, dtype=jnp.float32), lower=True)
    place = (mine - jnp.arange(groups)) % groups
    basis = apply(place.astype(jnp.int32), inverse, chunks)
    return basis, (chol / row_scale)[None]


def solution(mesh):
    return jax.shard_map(
        local,
        mesh=mesh,
        in_specs=(
            P("freq", None, None, "space", None),
            P(None, None, "space", None),
            P("space", None),
            P(),
        ),
        out_specs=(P("freq", None, None, "space", None), P("freq", None, None)),
        check_vma=False,
    )
```

```python
from functools import partial
import math

import jax
import jax.numpy as jnp
from jax import lax
from jax.experimental import pallas as pl
from jax.experimental.pallas import tpu as pltpu
from jax.sharding import PartitionSpec as P

K = 64
FIELDS = 5
NT = 16
F = 8
STEP_DT = 0.25
VISCOSITY = 0.5
LANES = 2 * K
HALF = 4
RH = 2
VMEM_LIMIT = 50 * 1024 * 1024


def quad_sum(value, axis, bit):
    count = lax.axis_size(axis)
    others = [m << bit for m in (2, 3, 1)]
    return [value] + [lax.ppermute(value, axis, [(i, i ^ m) for i in range(count)]) for m in others]


def spread_body(sketch_ref, out_ref, rows_ref, turned_ref):
    groups = out_ref.shape[0]
    radial = sketch_ref.shape[4]
    per = radial // groups
    rows_ref[...] = sketch_ref[...].astype(jnp.float32).reshape(LANES * 8, radial)
    edge = jnp.zeros((RH * HALF, LANES), jnp.float32)
    for half in range(2):
        turned_ref[half, 0 : RH * HALF, :] = edge
        turned_ref[half, (radial + RH) * HALF :, :] = edge
    for x in range(8):
        block = rows_ref[pl.ds(x, LANES, stride=8), :]
        turned_ref[x // HALF, pl.ds(RH * HALF + x % HALF, radial, stride=HALF), :] = block.T
    count = (per + 2 * RH) * HALF
    for half in range(2):
        for group in range(groups):
            start = group * per * HALF
            out_ref[group, half] = turned_ref[half, start : start + count, :].astype(jnp.bfloat16)


def spread(sketch, groups):
    radial = sketch.shape[4]
    rows = (radial // groups + 2 * RH) * HALF
    return pl.pallas_call(
        spread_body,
        grid=(FIELDS,),
        in_specs=[pl.BlockSpec((2, K, 1, 8, radial), lambda i: (0, 0, i, 0, 0))],
        out_specs=pl.BlockSpec((groups, 2, rows, LANES), lambda i: (0, 0, i, 0)),
        out_shape=jax.ShapeDtypeStruct((groups, 2, FIELDS * rows, LANES), jnp.bfloat16),
        scratch_shapes=[
            pltpu.VMEM((LANES * 8, radial), jnp.float32),
            pltpu.VMEM((2, (radial + 2 * RH) * HALF, LANES), jnp.float32),
        ],
        compiler_params=pltpu.CompilerParams(vmem_limit_bytes=VMEM_LIMIT),
        name="spread",
    )(sketch)


def fourier_body(parity_ref, rows_ref, table_ref, z_ref, pair_ref):
    size = pair_ref.shape[2]
    first = lax.broadcasted_iota(jnp.int32, (8, LANES), 1) < K

    @pl.loop(0, rows_ref.shape[2] // size)
    def _(step):
        start = pl.multiple_of(step * size, size)
        for d in range(4):
            a = rows_ref[d, 0, pl.ds(start, size), :].astype(jnp.float32)
            b = rows_ref[d + 4, 0, pl.ds(start, size), :].astype(jnp.float32)
            pair_ref[0, d] = a + b
            pair_ref[1, d] = a - b
        for f in range(F):
            parity = parity_ref[f]
            wave = [[jnp.broadcast_to(table_ref[f, c, d : d + 1], (8, LANES)) for d in range(4)] for c in range(2)]
            for line in range(0, size, 8):
                p = [pair_ref[parity, d, line : line + 8] for d in range(4)]
                u = (p[0] * wave[0][0] + p[1] * wave[0][1]) + (p[2] * wave[0][2] + p[3] * wave[0][3])
                v = (p[0] * wave[1][0] + p[1] * wave[1][1]) + (p[2] * wave[1][2] + p[3] * wave[1][3])
                z_ref[f, pl.ds(start + line, 8), :] = jnp.where(first, u, v) + pltpu.roll(
                    jnp.where(first, v, u), K, 1
                )


def fourier(parity, rows, part, table):
    slots, _, count, _ = rows.shape
    return pl.pallas_call(
        fourier_body,
        grid=(1,),
        in_specs=[
            pl.BlockSpec(memory_space=pltpu.SMEM),
            pl.BlockSpec((slots, 1, count, LANES), lambda i: (0, part, 0, 0)),
            pl.BlockSpec(table.shape, lambda i: (0, 0, 0, 0)),
        ],
        out_specs=pl.BlockSpec((F, count, LANES), lambda i: (0, 0, 0)),
        out_shape=jax.ShapeDtypeStruct((F, count, LANES), jnp.float32),
        scratch_shapes=[pltpu.VMEM((2, 4, count // 5, LANES), jnp.float32)],
        compiler_params=pltpu.CompilerParams(vmem_limit_bytes=VMEM_LIMIT),
        name="fourier",
    )(parity, rows, table)


def evolve_body(order_ref, *refs):
    layers, (coef_ref, mask_ref, turn_a, turn_b, out_ref, gram_ref, z_ref, s_ref) = refs[:8], refs[8:]
    wide = z_ref.shape[2]
    per = wide - 2 * RH
    sub = lax.broadcasted_iota(jnp.int32, (8, LANES), 0)

    @pl.loop(0, layers[0].shape[1] // 8, unroll=5)
    def _(step):
        here = pl.ds(pl.multiple_of(step * 8, 8), 8)
        line = step * 2
        field = line // wide
        cell = line % wide
        for n in range(2):
            for tile in range(2):
                a = layers[4 * n + 2 * tile][0, here, :]
                b = layers[4 * n + 2 * tile + 1][0, here, :]
                z_ref[n, field, cell, tile] = jnp.where(sub < HALF, a, pltpu.roll(b, HALF, 0))
                z_ref[n, field, cell + 1, tile] = jnp.where(sub < HALF, pltpu.roll(a, HALF, 0), b)

    turns = [turn_a[0], turn_b[0]]

    def shifted(tiles, shift, t):
        keep = (sub < 8 - shift) if shift > 0 else (sub >= -shift)
        turned = [pltpu.roll(v, (-shift) % 8, 0) for v in tiles]
        return jnp.where(keep, turned[t], turned[1 - t])

    def advance(ref, r, place, t, store):
        q = [[ref[n, j, r, t] for j in range(FIELDS)] for n in range(2)]
        for i in range(FIELDS):
            coupled = [coef_ref[j * FIELDS + i, place, t] for j in range(FIELDS)]
            moves = [coef_ref[FIELDS * FIELDS + m, place, t] for m in range(4)]
            for n in range(2):
                value = coupled[0] * q[n][0]
                for j in range(1, FIELDS):
                    value = value + coupled[j] * q[n][j]
                pair = [None, None]
                pair[t] = q[n][i]
                pair[1 - t] = ref[n, i, r, 1 - t]
                for m, shift in enumerate((1, -1, 2, -2)):
                    value = value + moves[m] * shifted(pair, shift, t)
                value = value + (STEP_DT * VISCOSITY) * (ref[n, i, r - 1, t] + ref[n, i, r + 1, t])
                store(n, i, value + turns[n] * pltpu.roll(q[n][i], K, 1))

    @pl.loop(0, per + 2)
    def _(r):
        for t in range(2):
            mask = mask_ref[r, t]

            def store(n, i, value):
                s_ref[n, i, r, t] = value * mask

            advance(z_ref, r + 1, r, t, store)

    @pl.loop(0, per, unroll=2)
    def _(r):
        def store(n, i, value):
            out_ref[n, pl.ds(i * 8 * per + r, 8, stride=per), :] = value

        advance(s_ref, r + 1, r + 1, 0, store)

    for n in range(2):
        block = out_ref[n]
        gram_ref[n] = lax.dot_general(
            block, block, (((0,), (0,)), ((), ())),
            precision=lax.Precision.HIGHEST, preferred_element_type=jnp.float32,
        )


def evolve(order, low, high, right, left, coef, mask, turn):
    count = order.shape[0]
    per = coef.shape[1] - 2
    rows = low.shape[1]
    whole = lambda shape: pl.BlockSpec(shape, lambda i, order: (0,) * len(shape))
    pick = lambda shape, n: pl.BlockSpec((1,) + shape, lambda i, order: (order[2 * i + n], 0, 0))
    layers = [pick((rows, LANES), n) for n in range(2) for _ in range(4)]
    return pl.pallas_call(
        evolve_body,
        grid_spec=pltpu.PrefetchScalarGridSpec(
            num_scalar_prefetch=1,
            grid=(count // 2,),
            in_specs=layers
            + [whole(coef.shape), whole(mask.shape), pick((8, LANES), 0), pick((8, LANES), 1)],
            out_specs=[
                pl.BlockSpec((2, FIELDS * 8 * per, LANES), lambda i, order: (i, 0, 0)),
                pl.BlockSpec((2, LANES, LANES), lambda i, order: (i, 0, 0)),
            ],
            scratch_shapes=[
                pltpu.VMEM((2, FIELDS, per + 2 * RH, 2, 8, LANES), jnp.float32),
                pltpu.VMEM((2, FIELDS, per + 2, 2, 8, LANES), jnp.float32),
            ],
        ),
        out_shape=[
            jax.ShapeDtypeStruct((count, FIELDS * 8 * per, LANES), jnp.float32),
            jax.ShapeDtypeStruct((count, LANES, LANES), jnp.float32),
        ],
        compiler_params=pltpu.CompilerParams(vmem_limit_bytes=VMEM_LIMIT),
        name="evolve",
    )(order, *([low, high, right, left] * 2), coef, mask, turn, turn)


def factor_body(scale, *refs):
    parts = refs[:-2]
    inverse_ref, factor_ref = refs[-2:]
    blocks = LANES // 8
    lane = lax.broadcasted_iota(jnp.int32, (8, LANES), 1)
    sub = lax.broadcasted_iota(jnp.int32, (8, LANES), 0)
    w = []
    for b in range(blocks):
        here = slice(8 * b, 8 * b + 8)
        w.append(sum(ref[here, :] for ref in parts))
    full = lambda v: jnp.broadcast_to(v, (8, LANES))
    for b in range(blocks):
        columns = [[full(w[i][:, 8 * b + k : 8 * b + k + 1]) for k in range(8)] for i in range(b, blocks)]
        rows = [full(w[b][k : k + 1, :]) for k in range(8)]
        a = [[full(columns[0][k][i : i + 1, :]) for k in range(i + 1)] for i in range(8)]
        low = [[None] * 8 for _ in range(8)]
        m = [[None] * 8 for _ in range(8)]
        for j in range(8):
            root = lax.rsqrt(a[j][j])
            root = root * (1.5 - 0.5 * (a[j][j] * root) * root)
            m[j][j] = root
            for i in range(j + 1, 8):
                low[i][j] = a[i][j] * root
            for i in range(j + 1, 8):
                for k in range(j + 1, i + 1):
                    a[i][k] = a[i][k] - low[i][j] * low[k][j]
            for k in range(j):
                total = low[j][k] * m[k][k]
                for n in range(k + 1, j):
                    total = total + low[j][n] * m[n][k]
                m[j][k] = -(total * root)
        inside = (lane >= 8 * b) & (lane < 8 * b + 8)
        ones = [jnp.where(inside, jnp.where(lane == 8 * b + k, 1.0, 0.0), rows[k]) for k in range(8)]
        final = [None] * 8
        upper = None
        lower = None
        for i in range(8):
            top = m[i][0] * rows[0]
            final[i] = m[i][0] * ones[0]
            for k in range(1, i + 1):
                top = top + m[i][k] * rows[k]
                final[i] = final[i] + m[i][k] * ones[k]
            upper = top if i == 0 else jnp.where(sub == i, top, upper)
            lower = final[i] if i == 0 else jnp.where(sub == i, final[i], lower)
        inverse_ref[8 * b : 8 * b + 8, :] = jnp.where(lane <= sub + 8 * b, lower * scale, 0.0)
        factor_ref[8 * b : 8 * b + 8, :] = jnp.where(lane >= sub + 8 * b, upper * (1.0 / scale), 0.0)
        if b + 1 < blocks:
            solved = []
            for k in range(8):
                total = m[k][k] * final[k]
                for i in range(k + 1, 8):
                    total = total + m[i][k] * final[i]
                solved.append(total)
            for i in range(b + 1, blocks):
                c = columns[i - b]
                products = [c[k] * solved[k] for k in range(8)]
                while len(products) > 1:
                    products = [products[n] + products[n + 1] for n in range(0, len(products), 2)]
                w[i] = jnp.where(inside, 0.0, w[i]) - products[0]
    factor_ref[...] = factor_ref[...].T


def factorize(parts, scale):
    vmem = pl.BlockSpec(memory_space=pltpu.VMEM)
    shape = jax.ShapeDtypeStruct((LANES, LANES), jnp.float32)
    return pl.pallas_call(
        partial(factor_body, scale),
        in_specs=[vmem] * len(parts),
        out_specs=[vmem, vmem],
        out_shape=[shape, shape],
        name="factorize",
    )(*parts)


def split(value):
    one = value.astype(jnp.bfloat16)
    rest = value - one.astype(jnp.float32)
    two = rest.astype(jnp.bfloat16)
    three = (rest - two.astype(jnp.float32)).astype(jnp.bfloat16)
    return one, two, three


def apply_body(inverse_ref, columns_ref, out_ref, rows_ref, all_ref):
    per = columns_ref.shape[1] // 8
    one, two, three = split(inverse_ref[...].T)
    main = jnp.concatenate([jnp.concatenate([one, two], axis=1)] * 2, axis=0)
    rest = jnp.concatenate([one, three], axis=0)
    for x in range(8):
        for d in range(F):
            all_ref[x, d * per : (d + 1) * per, :] = columns_ref[d, x * per : (x + 1) * per, :]
    for x in range(8):
        a, b, c = split(all_ref[x])
        wide = jnp.dot(jnp.concatenate([a, b], axis=1), main, preferred_element_type=jnp.float32)
        tail = jnp.dot(jnp.concatenate([c, a], axis=1), rest, preferred_element_type=jnp.float32)
        value = wide[:, :LANES] + (wide[:, LANES:] + tail)
        rows_ref[pl.ds(x, LANES, stride=8), :] = value.T
    out_ref[...] = rows_ref[...].reshape(out_ref.shape)


def apply(inverse, columns):
    per = columns.shape[1] // (8 * FIELDS)
    radial = per * F
    return pl.pallas_call(
        apply_body,
        grid=(FIELDS,),
        in_specs=[
            pl.BlockSpec((LANES, LANES), lambda i: (0, 0)),
            pl.BlockSpec((F, 8 * per, LANES), lambda i: (0, i, 0)),
        ],
        out_specs=pl.BlockSpec((1, LANES, 1, 8, radial), lambda i: (0, 0, i, 0, 0)),
        out_shape=jax.ShapeDtypeStruct((1, LANES, FIELDS, 8, radial), jnp.float32),
        scratch_shapes=[
            pltpu.VMEM((LANES * 8, radial), jnp.float32),
            pltpu.VMEM((8, radial, LANES), jnp.float32),
        ],
        compiler_params=pltpu.CompilerParams(vmem_limit_bytes=VMEM_LIMIT),
        name="apply",
    )(inverse, columns)


def make_table(indices, slots):
    times = jnp.arange(slots, dtype=jnp.int32)
    phases = indices[:, None] * times[None, :] % slots
    angles = phases.astype(jnp.float32) * (2.0 * math.pi / slots)
    return jnp.stack([jnp.cos(angles), -jnp.sin(angles)], axis=1)


def stencil(coupling, velocity, per):
    count = lax.axis_size("space")
    mine = lax.axis_index("space")
    start = lax.axis_index("freq") * per
    radial = velocity.shape[1]
    up = [(i, i + 1) for i in range(count - 1)]
    down = [(i + 1, i) for i in range(count - 1)]
    both = jnp.concatenate([coupling.reshape(FIELDS * FIELDS, 8, radial), velocity[None]], axis=0)
    right = lax.ppermute(both[:, :2], "space", down)
    left = lax.ppermute(both[:, 6:], "space", up)
    gap = jnp.zeros((both.shape[0], 4, radial), jnp.float32)
    full = jnp.concatenate([both, right, gap, left], axis=1)
    full = jnp.pad(full, ((0, 0), (0, 0), (1, 1)))
    full = lax.dynamic_slice_in_dim(full, start, per + 2, axis=2).transpose(0, 2, 1)
    speed = full[FIELDS * FIELDS]
    coupled = STEP_DT * full[: FIELDS * FIELDS]
    centre = 1.0 - STEP_DT * VISCOSITY * (30.0 / 12.0 + 2.0)
    diagonal = jnp.eye(FIELDS, dtype=jnp.float32).reshape(-1) * centre
    coupled = coupled + diagonal[:, None, None]
    near_d, near_c = STEP_DT * 8.0 / 12.0, STEP_DT * VISCOSITY * 16.0 / 12.0
    far_d, far_c = STEP_DT / 12.0, STEP_DT * VISCOSITY / 12.0
    shifts = jnp.stack(
        [near_d * speed + near_c, near_c - near_d * speed, -far_d * speed - far_c, far_d * speed - far_c]
    )
    coef = jnp.concatenate([coupled, shifts], axis=0)
    coef = jnp.broadcast_to(coef.reshape(-1, per + 2, 2, 8)[..., None], (coef.shape[0], per + 2, 2, 8, LANES))
    r = start - 1 + jnp.arange(per + 2)
    place = jnp.arange(16)
    inside = (place < 8) | ((place < 12) & (mine < count - 1)) | ((place >= 12) & (mine > 0))
    mask = ((r >= 0) & (r < radial))[:, None] & inside[None, :]
    mask = mask.astype(jnp.float32).reshape(per + 2, 2, 8)
    mask = jnp.broadcast_to(mask[..., None], mask.shape + (LANES,))
    return coef, mask


def local(sketch, coupling, velocity, freq_index):
    groups = lax.axis_size("freq")
    count = lax.axis_size("space")
    radial = sketch.shape[4]
    per = radial // groups
    mine = lax.axis_index("freq")

    rows = spread(sketch, groups)
    coupling, velocity, rows = lax.optimization_barrier((coupling, velocity, rows))
    rows = lax.all_to_all(rows, "freq", split_axis=0, concat_axis=0, tiled=True)

    parity = freq_index % 2
    waves = make_table(freq_index, NT)[:, :, : NT // 2].reshape(F, 2, 4, 2)
    waves = jnp.repeat(waves, K, axis=3)
    angular = math.pi / NT * STEP_DT * freq_index.astype(jnp.float32)
    sign = jnp.where(jnp.arange(LANES) < K, 1.0, -1.0).astype(jnp.float32)
    turn = jnp.broadcast_to((angular[:, None] * sign)[:, None, :], (F, 8, LANES))
    coef, mask = stencil(coupling, velocity, per)

    right = lax.ppermute(rows[:, 0], "space", [(i + 1, i) for i in range(count - 1)])
    left = lax.ppermute(rows[:, 1], "space", [(i, i + 1) for i in range(count - 1)])
    low, high = fourier(parity, rows, 0, waves), fourier(parity, rows, 1, waves)
    right, left = fourier(parity, right[:, None], 0, waves), fourier(parity, left[:, None], 0, waves)

    columns, grams = evolve(jnp.arange(F, dtype=jnp.int32), low, high, right, left, coef, mask, turn)
    parts = lax.all_to_all(grams, "freq", split_axis=0, concat_axis=0, tiled=True)
    gram = jnp.sum(parts, axis=0)
    columns, gram = lax.optimization_barrier((columns, gram))
    columns = lax.all_to_all(columns, "freq", split_axis=0, concat_axis=0, tiled=True)
    for bit in (0, 2, 4):
        parts = quad_sum(gram, "space", bit)
        gram = sum(parts)
    row_scale = math.sqrt(FIELDS * 8 * count * radial)
    inverse, factor = factorize(parts, row_scale)
    return apply(inverse, columns), factor[None]


def solution(mesh):
    return jax.shard_map(
        local,
        mesh=mesh,
        in_specs=(
            P("freq", None, None, "space", None),
            P(None, None, "space", None),
            P("space", None),
            P(),
        ),
        out_specs=(P("freq", None, None, "space", None), P("freq", None, None)),
        check_vma=False,
    )
```

```python
from functools import partial
import math

import jax
import jax.numpy as jnp
from jax import lax
from jax.experimental import pallas as pl
from jax.experimental.pallas import tpu as pltpu
from jax.sharding import PartitionSpec as P

K = 64
FIELDS = 5
NT = 16
F = 8
STEP_DT = 0.25
VISCOSITY = 0.5
LANES = 2 * K
HALF = 4
RH = 2
VMEM_LIMIT = 50 * 1024 * 1024


def quad_sum(value, axis, bit):
    count = lax.axis_size(axis)
    others = [m << bit for m in (2, 3, 1)]
    return [value] + [lax.ppermute(value, axis, [(i, i ^ m) for i in range(count)]) for m in others]


def spread_body(sketch_ref, out_ref, rows_ref, turned_ref):
    groups = out_ref.shape[0]
    radial = sketch_ref.shape[4]
    per = radial // groups
    rows_ref[...] = sketch_ref[...].astype(jnp.float32).reshape(LANES * 8, radial)
    edge = jnp.zeros((RH * HALF, LANES), jnp.float32)
    for half in range(2):
        turned_ref[half, 0 : RH * HALF, :] = edge
        turned_ref[half, (radial + RH) * HALF :, :] = edge
    for x in range(8):
        block = rows_ref[pl.ds(x, LANES, stride=8), :]
        turned_ref[x // HALF, pl.ds(RH * HALF + x % HALF, radial, stride=HALF), :] = block.T
    count = (per + 2 * RH) * HALF
    for half in range(2):
        for group in range(groups):
            start = group * per * HALF
            out_ref[group, half] = turned_ref[half, start : start + count, :].astype(jnp.bfloat16)


def spread(sketch, groups):
    radial = sketch.shape[4]
    rows = (radial // groups + 2 * RH) * HALF
    return pl.pallas_call(
        spread_body,
        grid=(FIELDS,),
        in_specs=[pl.BlockSpec((2, K, 1, 8, radial), lambda i: (0, 0, i, 0, 0))],
        out_specs=pl.BlockSpec((groups, 2, rows, LANES), lambda i: (0, 0, i, 0)),
        out_shape=jax.ShapeDtypeStruct((groups, 2, FIELDS * rows, LANES), jnp.bfloat16),
        scratch_shapes=[
            pltpu.VMEM((LANES * 8, radial), jnp.float32),
            pltpu.VMEM((2, (radial + 2 * RH) * HALF, LANES), jnp.float32),
        ],
        compiler_params=pltpu.CompilerParams(vmem_limit_bytes=VMEM_LIMIT),
        name="spread",
    )(sketch)


def fourier_body(parity_ref, rows_ref, table_ref, z_ref, pair_ref):
    size = pair_ref.shape[2]
    first = lax.broadcasted_iota(jnp.int32, (8, LANES), 1) < K

    @pl.loop(0, rows_ref.shape[2] // size)
    def _(step):
        start = pl.multiple_of(step * size, size)
        for d in range(4):
            a = rows_ref[d, 0, pl.ds(start, size), :].astype(jnp.float32)
            b = rows_ref[d + 4, 0, pl.ds(start, size), :].astype(jnp.float32)
            pair_ref[0, d] = a + b
            pair_ref[1, d] = a - b
        for f in range(F):
            parity = parity_ref[f]
            wave = [[jnp.broadcast_to(table_ref[f, c, d : d + 1], (8, LANES)) for d in range(4)] for c in range(2)]
            for line in range(0, size, 8):
                p = [pair_ref[parity, d, line : line + 8] for d in range(4)]
                u = (p[0] * wave[0][0] + p[1] * wave[0][1]) + (p[2] * wave[0][2] + p[3] * wave[0][3])
                v = (p[0] * wave[1][0] + p[1] * wave[1][1]) + (p[2] * wave[1][2] + p[3] * wave[1][3])
                z_ref[f, pl.ds(start + line, 8), :] = jnp.where(first, u, v) + pltpu.roll(
                    jnp.where(first, v, u), K, 1
                )


def fourier(parity, rows, part, table):
    slots, _, count, _ = rows.shape
    return pl.pallas_call(
        fourier_body,
        grid=(1,),
        in_specs=[
            pl.BlockSpec(memory_space=pltpu.SMEM),
            pl.BlockSpec((slots, 1, count, LANES), lambda i: (0, part, 0, 0)),
            pl.BlockSpec(table.shape, lambda i: (0, 0, 0, 0)),
        ],
        out_specs=pl.BlockSpec((F, count, LANES), lambda i: (0, 0, 0)),
        out_shape=jax.ShapeDtypeStruct((F, count, LANES), jnp.float32),
        scratch_shapes=[pltpu.VMEM((2, 4, count // 5, LANES), jnp.float32)],
        compiler_params=pltpu.CompilerParams(vmem_limit_bytes=VMEM_LIMIT),
        name="fourier",
    )(parity, rows, table)


def pack(gram, ref, n):
    line = lax.broadcasted_iota(jnp.int32, (K, LANES), 0)
    lane = lax.broadcasted_iota(jnp.int32, (K, LANES), 1)
    last = pltpu.roll(gram[K:], K, 1)
    ref[n, 0:K, :] = jnp.where(lane >= line, gram[:K], last)
    diagonal = jnp.sum(jnp.where(lane == line, last, 0.0), axis=0, keepdims=True)
    ref[n, K : K + 8, :] = jnp.broadcast_to(diagonal, (8, LANES))


def unpack(packed):
    line = lax.broadcasted_iota(jnp.int32, (K, LANES), 0)
    lane = lax.broadcasted_iota(jnp.int32, (K, LANES), 1)
    top = packed[:K]
    last = pltpu.roll(jnp.where(lane < line, top, 0.0), K, 1)
    half = jnp.concatenate([jnp.where(lane >= line, top, 0.0), last], axis=0)
    diagonal = pltpu.roll(packed[K : K + 8], K, 1)
    diagonal = jnp.concatenate([top] + [diagonal] * (K // 8), axis=0)
    line = lax.broadcasted_iota(jnp.int32, (LANES, LANES), 0)
    lane = lax.broadcasted_iota(jnp.int32, (LANES, LANES), 1)
    return jnp.where(line == lane, diagonal, half + half.T)


def evolve_body(order_ref, *refs):
    layers, (coef_ref, mask_ref, turn_a, turn_b, out_ref, gram_ref, z_ref, s_ref) = refs[:8], refs[8:]
    wide = z_ref.shape[2]
    per = wide - 2 * RH
    sub = lax.broadcasted_iota(jnp.int32, (8, LANES), 0)

    @pl.loop(0, layers[0].shape[1] // 8, unroll=5)
    def _(step):
        here = pl.ds(pl.multiple_of(step * 8, 8), 8)
        line = step * 2
        field = line // wide
        cell = line % wide
        for n in range(2):
            for tile in range(2):
                a = layers[4 * n + 2 * tile][0, here, :]
                b = layers[4 * n + 2 * tile + 1][0, here, :]
                z_ref[n, field, cell, tile] = jnp.where(sub < HALF, a, pltpu.roll(b, HALF, 0))
                z_ref[n, field, cell + 1, tile] = jnp.where(sub < HALF, pltpu.roll(a, HALF, 0), b)

    turns = [turn_a[0], turn_b[0]]

    def shifted(tiles, shift, t):
        keep = (sub < 8 - shift) if shift > 0 else (sub >= -shift)
        turned = [pltpu.roll(v, (-shift) % 8, 0) for v in tiles]
        return jnp.where(keep, turned[t], turned[1 - t])

    def advance(ref, r, place, t, store):
        q = [[ref[n, j, r, t] for j in range(FIELDS)] for n in range(2)]
        for i in range(FIELDS):
            coupled = [coef_ref[j * FIELDS + i, place, t] for j in range(FIELDS)]
            moves = [coef_ref[FIELDS * FIELDS + m, place, t] for m in range(4)]
            for n in range(2):
                value = coupled[0] * q[n][0]
                for j in range(1, FIELDS):
                    value = value + coupled[j] * q[n][j]
                pair = [None, None]
                pair[t] = q[n][i]
                pair[1 - t] = ref[n, i, r, 1 - t]
                for m, shift in enumerate((1, -1, 2, -2)):
                    value = value + moves[m] * shifted(pair, shift, t)
                value = value + (STEP_DT * VISCOSITY) * (ref[n, i, r - 1, t] + ref[n, i, r + 1, t])
                store(n, i, value + turns[n] * pltpu.roll(q[n][i], K, 1))

    @pl.loop(0, per + 2)
    def _(r):
        for t in range(2):
            mask = mask_ref[r, t]

            def store(n, i, value):
                s_ref[n, i, r, t] = value * mask

            advance(z_ref, r + 1, r, t, store)

    @pl.loop(0, per, unroll=2)
    def _(r):
        def store(n, i, value):
            out_ref[n, pl.ds(i * 8 * per + r, 8, stride=per), :] = value

        advance(s_ref, r + 1, r + 1, 0, store)

    for n in range(2):
        block = out_ref[n]
        gram = lax.dot_general(
            block, block, (((0,), (0,)), ((), ())),
            precision=lax.Precision.HIGHEST, preferred_element_type=jnp.float32,
        )
        pack(gram, gram_ref, n)


def evolve(order, low, high, right, left, coef, mask, turn):
    count = order.shape[0]
    per = coef.shape[1] - 2
    rows = low.shape[1]
    whole = lambda shape: pl.BlockSpec(shape, lambda i, order: (0,) * len(shape))
    pick = lambda shape, n: pl.BlockSpec((1,) + shape, lambda i, order: (order[2 * i + n], 0, 0))
    layers = [pick((rows, LANES), n) for n in range(2) for _ in range(4)]
    return pl.pallas_call(
        evolve_body,
        grid_spec=pltpu.PrefetchScalarGridSpec(
            num_scalar_prefetch=1,
            grid=(count // 2,),
            in_specs=layers
            + [whole(coef.shape), whole(mask.shape), pick((8, LANES), 0), pick((8, LANES), 1)],
            out_specs=[
                pl.BlockSpec((2, FIELDS * 8 * per, LANES), lambda i, order: (i, 0, 0)),
                pl.BlockSpec((2, K + 8, LANES), lambda i, order: (i, 0, 0)),
            ],
            scratch_shapes=[
                pltpu.VMEM((2, FIELDS, per + 2 * RH, 2, 8, LANES), jnp.float32),
                pltpu.VMEM((2, FIELDS, per + 2, 2, 8, LANES), jnp.float32),
            ],
        ),
        out_shape=[
            jax.ShapeDtypeStruct((count, FIELDS * 8 * per, LANES), jnp.float32),
            jax.ShapeDtypeStruct((count, K + 8, LANES), jnp.float32),
        ],
        compiler_params=pltpu.CompilerParams(vmem_limit_bytes=VMEM_LIMIT),
        name="evolve",
    )(order, *([low, high, right, left] * 2), coef, mask, turn, turn)


def factor_body(scale, *refs):
    parts = refs[:-2]
    inverse_ref, factor_ref = refs[-2:]
    blocks = LANES // 8
    lane = lax.broadcasted_iota(jnp.int32, (8, LANES), 1)
    sub = lax.broadcasted_iota(jnp.int32, (8, LANES), 0)
    gram = unpack(sum(ref[...] for ref in parts))
    w = [gram[8 * b : 8 * b + 8] for b in range(blocks)]
    full = lambda v: jnp.broadcast_to(v, (8, LANES))
    for b in range(blocks):
        columns = [[full(w[i][:, 8 * b + k : 8 * b + k + 1]) for k in range(8)] for i in range(b, blocks)]
        rows = [full(w[b][k : k + 1, :]) for k in range(8)]
        a = [[full(columns[0][k][i : i + 1, :]) for k in range(i + 1)] for i in range(8)]
        low = [[None] * 8 for _ in range(8)]
        m = [[None] * 8 for _ in range(8)]
        for j in range(8):
            root = lax.rsqrt(a[j][j])
            root = root * (1.5 - 0.5 * (a[j][j] * root) * root)
            m[j][j] = root
            for i in range(j + 1, 8):
                low[i][j] = a[i][j] * root
            for i in range(j + 1, 8):
                for k in range(j + 1, i + 1):
                    a[i][k] = a[i][k] - low[i][j] * low[k][j]
            for k in range(j):
                total = low[j][k] * m[k][k]
                for n in range(k + 1, j):
                    total = total + low[j][n] * m[n][k]
                m[j][k] = -(total * root)
        inside = (lane >= 8 * b) & (lane < 8 * b + 8)
        ones = [jnp.where(inside, jnp.where(lane == 8 * b + k, 1.0, 0.0), rows[k]) for k in range(8)]
        final = [None] * 8
        upper = None
        lower = None
        for i in range(8):
            top = m[i][0] * rows[0]
            final[i] = m[i][0] * ones[0]
            for k in range(1, i + 1):
                top = top + m[i][k] * rows[k]
                final[i] = final[i] + m[i][k] * ones[k]
            upper = top if i == 0 else jnp.where(sub == i, top, upper)
            lower = final[i] if i == 0 else jnp.where(sub == i, final[i], lower)
        inverse_ref[8 * b : 8 * b + 8, :] = jnp.where(lane <= sub + 8 * b, lower * scale, 0.0)
        factor_ref[8 * b : 8 * b + 8, :] = jnp.where(lane >= sub + 8 * b, upper * (1.0 / scale), 0.0)
        if b + 1 < blocks:
            solved = []
            for k in range(8):
                total = m[k][k] * final[k]
                for i in range(k + 1, 8):
                    total = total + m[i][k] * final[i]
                solved.append(total)
            for i in range(b + 1, blocks):
                c = columns[i - b]
                products = [c[k] * solved[k] for k in range(8)]
                while len(products) > 1:
                    products = [products[n] + products[n + 1] for n in range(0, len(products), 2)]
                w[i] = jnp.where(inside, 0.0, w[i]) - products[0]
    factor_ref[...] = factor_ref[...].T


def factorize(parts, scale):
    vmem = pl.BlockSpec(memory_space=pltpu.VMEM)
    shape = jax.ShapeDtypeStruct((LANES, LANES), jnp.float32)
    return pl.pallas_call(
        partial(factor_body, scale),
        in_specs=[vmem] * len(parts),
        out_specs=[vmem, vmem],
        out_shape=[shape, shape],
        name="factorize",
    )(*parts)


def split(value):
    one = value.astype(jnp.bfloat16)
    rest = value - one.astype(jnp.float32)
    two = rest.astype(jnp.bfloat16)
    three = (rest - two.astype(jnp.float32)).astype(jnp.bfloat16)
    return one, two, three


def apply_body(inverse_ref, columns_ref, out_ref, rows_ref, all_ref):
    per = columns_ref.shape[1] // 8
    one, two, three = split(inverse_ref[...].T)
    main = jnp.concatenate([jnp.concatenate([one, two], axis=1)] * 2, axis=0)
    rest = jnp.concatenate([one, three], axis=0)
    for x in range(8):
        for d in range(F):
            all_ref[x, d * per : (d + 1) * per, :] = columns_ref[d, x * per : (x + 1) * per, :]
    for x in range(8):
        a, b, c = split(all_ref[x])
        wide = jnp.dot(jnp.concatenate([a, b], axis=1), main, preferred_element_type=jnp.float32)
        tail = jnp.dot(jnp.concatenate([c, a], axis=1), rest, preferred_element_type=jnp.float32)
        value = wide[:, :LANES] + (wide[:, LANES:] + tail)
        rows_ref[pl.ds(x, LANES, stride=8), :] = value.T
    out_ref[...] = rows_ref[...].reshape(out_ref.shape)


def apply(inverse, columns):
    per = columns.shape[1] // (8 * FIELDS)
    radial = per * F
    return pl.pallas_call(
        apply_body,
        grid=(FIELDS,),
        in_specs=[
            pl.BlockSpec((LANES, LANES), lambda i: (0, 0)),
            pl.BlockSpec((F, 8 * per, LANES), lambda i: (0, i, 0)),
        ],
        out_specs=pl.BlockSpec((1, LANES, 1, 8, radial), lambda i: (0, 0, i, 0, 0)),
        out_shape=jax.ShapeDtypeStruct((1, LANES, FIELDS, 8, radial), jnp.float32),
        scratch_shapes=[
            pltpu.VMEM((LANES * 8, radial), jnp.float32),
            pltpu.VMEM((8, radial, LANES), jnp.float32),
        ],
        compiler_params=pltpu.CompilerParams(vmem_limit_bytes=VMEM_LIMIT),
        name="apply",
    )(inverse, columns)


def make_table(indices, slots):
    times = jnp.arange(slots, dtype=jnp.int32)
    phases = indices[:, None] * times[None, :] % slots
    angles = phases.astype(jnp.float32) * (2.0 * math.pi / slots)
    return jnp.stack([jnp.cos(angles), -jnp.sin(angles)], axis=1)


def stencil(coupling, velocity, per):
    count = lax.axis_size("space")
    mine = lax.axis_index("space")
    start = lax.axis_index("freq") * per
    radial = velocity.shape[1]
    up = [(i, i + 1) for i in range(count - 1)]
    down = [(i + 1, i) for i in range(count - 1)]
    both = jnp.concatenate([coupling.reshape(FIELDS * FIELDS, 8, radial), velocity[None]], axis=0)
    right = lax.ppermute(both[:, :2], "space", down)
    left = lax.ppermute(both[:, 6:], "space", up)
    gap = jnp.zeros((both.shape[0], 4, radial), jnp.float32)
    full = jnp.concatenate([both, right, gap, left], axis=1)
    full = jnp.pad(full, ((0, 0), (0, 0), (1, 1)))
    full = lax.dynamic_slice_in_dim(full, start, per + 2, axis=2).transpose(0, 2, 1)
    speed = full[FIELDS * FIELDS]
    coupled = STEP_DT * full[: FIELDS * FIELDS]
    centre = 1.0 - STEP_DT * VISCOSITY * (30.0 / 12.0 + 2.0)
    diagonal = jnp.eye(FIELDS, dtype=jnp.float32).reshape(-1) * centre
    coupled = coupled + diagonal[:, None, None]
    near_d, near_c = STEP_DT * 8.0 / 12.0, STEP_DT * VISCOSITY * 16.0 / 12.0
    far_d, far_c = STEP_DT / 12.0, STEP_DT * VISCOSITY / 12.0
    shifts = jnp.stack(
        [near_d * speed + near_c, near_c - near_d * speed, -far_d * speed - far_c, far_d * speed - far_c]
    )
    coef = jnp.concatenate([coupled, shifts], axis=0)
    coef = jnp.broadcast_to(coef.reshape(-1, per + 2, 2, 8)[..., None], (coef.shape[0], per + 2, 2, 8, LANES))
    r = start - 1 + jnp.arange(per + 2)
    place = jnp.arange(16)
    inside = (place < 8) | ((place < 12) & (mine < count - 1)) | ((place >= 12) & (mine > 0))
    mask = ((r >= 0) & (r < radial))[:, None] & inside[None, :]
    mask = mask.astype(jnp.float32).reshape(per + 2, 2, 8)
    mask = jnp.broadcast_to(mask[..., None], mask.shape + (LANES,))
    return coef, mask


def local(sketch, coupling, velocity, freq_index):
    groups = lax.axis_size("freq")
    count = lax.axis_size("space")
    radial = sketch.shape[4]
    per = radial // groups
    mine = lax.axis_index("freq")

    rows = spread(sketch, groups)
    coupling, velocity, rows = lax.optimization_barrier((coupling, velocity, rows))
    rows = lax.all_to_all(rows, "freq", split_axis=0, concat_axis=0, tiled=True)

    parity = freq_index % 2
    waves = make_table(freq_index, NT)[:, :, : NT // 2].reshape(F, 2, 4, 2)
    waves = jnp.repeat(waves, K, axis=3)
    angular = math.pi / NT * STEP_DT * freq_index.astype(jnp.float32)
    sign = jnp.where(jnp.arange(LANES) < K, 1.0, -1.0).astype(jnp.float32)
    turn = jnp.broadcast_to((angular[:, None] * sign)[:, None, :], (F, 8, LANES))
    coef, mask = stencil(coupling, velocity, per)

    rows, coef, mask, turn, waves, parity = lax.optimization_barrier((rows, coef, mask, turn, waves, parity))
    right = lax.ppermute(rows[:, 0], "space", [(i + 1, i) for i in range(count - 1)])
    left = lax.ppermute(rows[:, 1], "space", [(i, i + 1) for i in range(count - 1)])
    low, high = fourier(parity, rows, 0, waves), fourier(parity, rows, 1, waves)
    right, left = fourier(parity, right[:, None], 0, waves), fourier(parity, left[:, None], 0, waves)

    columns, grams = evolve(jnp.arange(F, dtype=jnp.int32), low, high, right, left, coef, mask, turn)
    parts = lax.all_to_all(grams, "freq", split_axis=0, concat_axis=0, tiled=True)
    gram = jnp.sum(parts, axis=0)
    columns, gram = lax.optimization_barrier((columns, gram))
    columns = lax.all_to_all(columns, "freq", split_axis=0, concat_axis=0, tiled=True)
    for bit in (0, 2, 4):
        parts = quad_sum(gram, "space", bit)
        gram = sum(parts)
    row_scale = math.sqrt(FIELDS * 8 * count * radial)
    inverse, factor = factorize(parts, row_scale)
    return apply(inverse, columns), factor[None]


def solution(mesh):
    return jax.shard_map(
        local,
        mesh=mesh,
        in_specs=(
            P("freq", None, None, "space", None),
            P(None, None, "space", None),
            P("space", None),
            P(),
        ),
        out_specs=(P("freq", None, None, "space", None), P("freq", None, None)),
        check_vma=False,
    )
```

```python
from functools import partial
import math

import jax
import jax.numpy as jnp
from jax import lax
from jax.experimental import pallas as pl
from jax.experimental.pallas import tpu as pltpu
from jax.sharding import PartitionSpec as P

K = 64
FIELDS = 5
NT = 16
F = 8
STEP_DT = 0.25
VISCOSITY = 0.5
LANES = 2 * K
HALF = 4
RH = 2
VMEM_LIMIT = 50 * 1024 * 1024


def quad_sum(value, axis, bit):
    count = lax.axis_size(axis)
    others = [m << bit for m in (2, 3, 1)]
    return [value] + [lax.ppermute(value, axis, [(i, i ^ m) for i in range(count)]) for m in others]


def spread_body(sketch_ref, out_ref, rows_ref, turned_ref):
    groups = out_ref.shape[0]
    radial = sketch_ref.shape[4]
    per = radial // groups
    rows_ref[...] = sketch_ref[...].astype(jnp.float32).reshape(LANES * 8, radial)
    edge = jnp.zeros((RH * HALF, LANES), jnp.float32)
    for half in range(2):
        turned_ref[half, 0 : RH * HALF, :] = edge
        turned_ref[half, (radial + RH) * HALF :, :] = edge
    for x in range(8):
        block = rows_ref[pl.ds(x, LANES, stride=8), :]
        turned_ref[x // HALF, pl.ds(RH * HALF + x % HALF, radial, stride=HALF), :] = block.T
    count = (per + 2 * RH) * HALF
    for half in range(2):
        for group in range(groups):
            start = group * per * HALF
            out_ref[group, half] = turned_ref[half, start : start + count, :].astype(jnp.bfloat16)


def spread(sketch, groups):
    radial = sketch.shape[4]
    rows = (radial // groups + 2 * RH) * HALF
    return pl.pallas_call(
        spread_body,
        grid=(FIELDS,),
        in_specs=[pl.BlockSpec((2, K, 1, 8, radial), lambda i: (0, 0, i, 0, 0))],
        out_specs=pl.BlockSpec((groups, 2, rows, LANES), lambda i: (0, 0, i, 0)),
        out_shape=jax.ShapeDtypeStruct((groups, 2, FIELDS * rows, LANES), jnp.bfloat16),
        scratch_shapes=[
            pltpu.VMEM((LANES * 8, radial), jnp.float32),
            pltpu.VMEM((2, (radial + 2 * RH) * HALF, LANES), jnp.float32),
        ],
        compiler_params=pltpu.CompilerParams(vmem_limit_bytes=VMEM_LIMIT),
        name="spread",
    )(sketch)


def fourier_body(parity_ref, one_ref, two_ref, table_ref, z_one, z_two, pair_ref):
    size = pair_ref.shape[2]
    first = lax.broadcasted_iota(jnp.int32, (8, LANES), 1) < K
    for rows_ref, z_ref in ((one_ref, z_one), (two_ref, z_two)):
        for d in range(4):
            a = rows_ref[d, 0].astype(jnp.float32)
            b = rows_ref[d + 4, 0].astype(jnp.float32)
            pair_ref[0, d] = a + b
            pair_ref[1, d] = a - b
        for f in range(F):
            parity = parity_ref[f]
            wave = [[jnp.broadcast_to(table_ref[f, c, d : d + 1], (8, LANES)) for d in range(4)] for c in range(2)]
            for line in range(0, size, 8):
                p = [pair_ref[parity, d, line : line + 8] for d in range(4)]
                u = (p[0] * wave[0][0] + p[1] * wave[0][1]) + (p[2] * wave[0][2] + p[3] * wave[0][3])
                v = (p[0] * wave[1][0] + p[1] * wave[1][1]) + (p[2] * wave[1][2] + p[3] * wave[1][3])
                z_ref[f, line : line + 8, :] = jnp.where(first, u, v) + pltpu.roll(jnp.where(first, v, u), K, 1)


def fourier(parity, one, two, table, parts):
    slots, _, count, _ = one.shape
    size = count // FIELDS
    z_spec = pl.BlockSpec((F, size, LANES), lambda i: (0, i, 0))
    z_shape = jax.ShapeDtypeStruct((F, count, LANES), jnp.float32)
    return pl.pallas_call(
        fourier_body,
        grid=(FIELDS,),
        in_specs=[
            pl.BlockSpec(memory_space=pltpu.SMEM),
            pl.BlockSpec((slots, 1, size, LANES), lambda i: (0, parts[0], i, 0)),
            pl.BlockSpec((slots, 1, size, LANES), lambda i: (0, parts[1], i, 0)),
            pl.BlockSpec(table.shape, lambda i: (0, 0, 0, 0)),
        ],
        out_specs=[z_spec, z_spec],
        out_shape=[z_shape, z_shape],
        scratch_shapes=[pltpu.VMEM((2, 4, size, LANES), jnp.float32)],
        compiler_params=pltpu.CompilerParams(vmem_limit_bytes=VMEM_LIMIT),
        name="fourier",
    )(parity, one, two, table)


CODE = 8388000.0


def encode(block, scale):
    number = jnp.round(block * (CODE / scale)).astype(jnp.int32)
    half = block.shape[0] // 2
    low = number & 255
    both = (low[:half] << 8) + low[half:] - 32768
    return (number >> 8).astype(jnp.int16), both.astype(jnp.int16)


def pack(gram, ref, n):
    line = lax.broadcasted_iota(jnp.int32, (K, LANES), 0)
    lane = lax.broadcasted_iota(jnp.int32, (K, LANES), 1)
    last = pltpu.roll(gram[K:], K, 1)
    ref[n, 0:K, :] = jnp.where(lane >= line, gram[:K], last)
    diagonal = jnp.sum(jnp.where(lane == line, last, 0.0), axis=0, keepdims=True)
    ref[n, K : K + 8, :] = jnp.broadcast_to(diagonal, (8, LANES))


def unpack(packed):
    line = lax.broadcasted_iota(jnp.int32, (K, LANES), 0)
    lane = lax.broadcasted_iota(jnp.int32, (K, LANES), 1)
    top = packed[:K]
    last = pltpu.roll(jnp.where(lane < line, top, 0.0), K, 1)
    half = jnp.concatenate([jnp.where(lane >= line, top, 0.0), last], axis=0)
    diagonal = pltpu.roll(jnp.broadcast_to(packed[K : K + 1], (8, LANES)), K, 1)
    diagonal = jnp.concatenate([top] + [diagonal] * (K // 8), axis=0)
    line = lax.broadcasted_iota(jnp.int32, (LANES, LANES), 0)
    lane = lax.broadcasted_iota(jnp.int32, (LANES, LANES), 1)
    return jnp.where(line == lane, diagonal, half + half.T)


def evolve_body(order_ref, *refs):
    layers, (coef_ref, mask_ref, turn_a, turn_b, code_ref, gram_ref, z_ref, s_ref, out_ref) = refs[:8], refs[8:]
    wide = z_ref.shape[2]
    per = wide - 2 * RH
    sub = lax.broadcasted_iota(jnp.int32, (8, LANES), 0)

    @pl.loop(0, layers[0].shape[1] // 8, unroll=5)
    def _(step):
        here = pl.ds(pl.multiple_of(step * 8, 8), 8)
        line = step * 2
        field = line // wide
        cell = line % wide
        for n in range(2):
            for tile in range(2):
                a = layers[4 * n + 2 * tile][0, here, :]
                b = layers[4 * n + 2 * tile + 1][0, here, :]
                z_ref[n, field, cell, tile] = jnp.where(sub < HALF, a, pltpu.roll(b, HALF, 0))
                z_ref[n, field, cell + 1, tile] = jnp.where(sub < HALF, pltpu.roll(a, HALF, 0), b)

    turns = [turn_a[0], turn_b[0]]

    def shifted(tiles, shift, t):
        keep = (sub < 8 - shift) if shift > 0 else (sub >= -shift)
        turned = [pltpu.roll(v, (-shift) % 8, 0) for v in tiles]
        return jnp.where(keep, turned[t], turned[1 - t])

    def advance(ref, r, place, t, store):
        q = [[ref[n, j, r, t] for j in range(FIELDS)] for n in range(2)]
        for i in range(FIELDS):
            coupled = [coef_ref[j * FIELDS + i, place, t] for j in range(FIELDS)]
            moves = [coef_ref[FIELDS * FIELDS + m, place, t] for m in range(4)]
            for n in range(2):
                value = coupled[0] * q[n][0]
                for j in range(1, FIELDS):
                    value = value + coupled[j] * q[n][j]
                pair = [None, None]
                pair[t] = q[n][i]
                pair[1 - t] = ref[n, i, r, 1 - t]
                for m, shift in enumerate((1, -1, 2, -2)):
                    value = value + moves[m] * shifted(pair, shift, t)
                value = value + (STEP_DT * VISCOSITY) * (ref[n, i, r - 1, t] + ref[n, i, r + 1, t])
                store(n, i, value + turns[n] * pltpu.roll(q[n][i], K, 1))

    @pl.loop(0, per + 2)
    def _(r):
        for t in range(2):
            mask = mask_ref[r, t]

            def store(n, i, value):
                s_ref[n, i, r, t] = value * mask

            advance(z_ref, r + 1, r, t, store)

    @pl.loop(0, per, unroll=2)
    def _(r):
        def store(n, i, value):
            out_ref[n, pl.ds(i * 8 * per + r, 8, stride=per), :] = value

        advance(s_ref, r + 1, r + 1, 0, store)

    for n in range(2):
        block = out_ref[n]
        gram = lax.dot_general(
            block, block, (((0,), (0,)), ((), ())),
            precision=lax.Precision.HIGHEST, preferred_element_type=jnp.float32,
        )
        pack(gram, gram_ref, n)
        scale = jnp.maximum(jnp.max(jnp.abs(block), axis=0, keepdims=True), 1e-30)
        gram_ref[n, K + 1 : K + 2, :] = scale
        count = block.shape[0]
        code_ref[n, 0:count, :], code_ref[n, count : count + count // 2, :] = encode(block, scale)


def evolve(order, low, high, right, left, coef, mask, turn):
    count = order.shape[0]
    per = coef.shape[1] - 2
    rows = low.shape[1]
    whole = lambda shape: pl.BlockSpec(shape, lambda i, order: (0,) * len(shape))
    pick = lambda shape, n: pl.BlockSpec((1,) + shape, lambda i, order: (order[2 * i + n], 0, 0))
    layers = [pick((rows, LANES), n) for n in range(2) for _ in range(4)]
    return pl.pallas_call(
        evolve_body,
        grid_spec=pltpu.PrefetchScalarGridSpec(
            num_scalar_prefetch=1,
            grid=(count // 2,),
            in_specs=layers
            + [whole(coef.shape), whole(mask.shape), pick((8, LANES), 0), pick((8, LANES), 1)],
            out_specs=[
                pl.BlockSpec((2, FIELDS * 12 * per, LANES), lambda i, order: (i, 0, 0)),
                pl.BlockSpec((2, K + 8, LANES), lambda i, order: (i, 0, 0)),
            ],
            scratch_shapes=[
                pltpu.VMEM((2, FIELDS, per + 2 * RH, 2, 8, LANES), jnp.float32),
                pltpu.VMEM((2, FIELDS, per + 2, 2, 8, LANES), jnp.float32),
                pltpu.VMEM((2, FIELDS * 8 * per, LANES), jnp.float32),
            ],
        ),
        out_shape=[
            jax.ShapeDtypeStruct((count, FIELDS * 12 * per, LANES), jnp.int16),
            jax.ShapeDtypeStruct((count, K + 8, LANES), jnp.float32),
        ],
        compiler_params=pltpu.CompilerParams(vmem_limit_bytes=VMEM_LIMIT),
        name="evolve",
    )(order, *([low, high, right, left] * 2), coef, mask, turn, turn)


def factor_body(scale, *refs):
    parts = refs[:-2]
    inverse_ref, factor_ref = refs[-2:]
    blocks = LANES // 8
    lane = lax.broadcasted_iota(jnp.int32, (8, LANES), 1)
    sub = lax.broadcasted_iota(jnp.int32, (8, LANES), 0)
    gram = unpack(sum(ref[...] for ref in parts))
    w = [gram[8 * b : 8 * b + 8] for b in range(blocks)]
    full = lambda v: jnp.broadcast_to(v, (8, LANES))
    for b in range(blocks):
        columns = [[full(w[i][:, 8 * b + k : 8 * b + k + 1]) for k in range(8)] for i in range(b, blocks)]
        rows = [full(w[b][k : k + 1, :]) for k in range(8)]
        a = [[full(columns[0][k][i : i + 1, :]) for k in range(i + 1)] for i in range(8)]
        low = [[None] * 8 for _ in range(8)]
        m = [[None] * 8 for _ in range(8)]
        for j in range(8):
            root = lax.rsqrt(a[j][j])
            root = root * (1.5 - 0.5 * (a[j][j] * root) * root)
            m[j][j] = root
            for i in range(j + 1, 8):
                low[i][j] = a[i][j] * root
            for i in range(j + 1, 8):
                for k in range(j + 1, i + 1):
                    a[i][k] = a[i][k] - low[i][j] * low[k][j]
            for k in range(j):
                total = low[j][k] * m[k][k]
                for n in range(k + 1, j):
                    total = total + low[j][n] * m[n][k]
                m[j][k] = -(total * root)
        inside = (lane >= 8 * b) & (lane < 8 * b + 8)
        ones = [jnp.where(inside, jnp.where(lane == 8 * b + k, 1.0, 0.0), rows[k]) for k in range(8)]
        final = [None] * 8
        upper = None
        lower = None
        for i in range(8):
            top = m[i][0] * rows[0]
            final[i] = m[i][0] * ones[0]
            for k in range(1, i + 1):
                top = top + m[i][k] * rows[k]
                final[i] = final[i] + m[i][k] * ones[k]
            upper = top if i == 0 else jnp.where(sub == i, top, upper)
            lower = final[i] if i == 0 else jnp.where(sub == i, final[i], lower)
        inverse_ref[8 * b : 8 * b + 8, :] = jnp.where(lane <= sub + 8 * b, lower * scale, 0.0)
        factor_ref[8 * b : 8 * b + 8, :] = jnp.where(lane >= sub + 8 * b, upper * (1.0 / scale), 0.0)
        if b + 1 < blocks:
            solved = []
            for k in range(8):
                total = m[k][k] * final[k]
                for i in range(k + 1, 8):
                    total = total + m[i][k] * final[i]
                solved.append(total)
            for i in range(b + 1, blocks):
                c = columns[i - b]
                products = [c[k] * solved[k] for k in range(8)]
                while len(products) > 1:
                    products = [products[n] + products[n + 1] for n in range(0, len(products), 2)]
                w[i] = jnp.where(inside, 0.0, w[i]) - products[0]
    factor_ref[...] = factor_ref[...].T


def factorize(parts, scale):
    vmem = pl.BlockSpec(memory_space=pltpu.VMEM)
    shape = jax.ShapeDtypeStruct((LANES, LANES), jnp.float32)
    return pl.pallas_call(
        partial(factor_body, scale),
        in_specs=[vmem] * len(parts),
        out_specs=[vmem, vmem],
        out_shape=[shape, shape],
        name="factorize",
    )(*parts)


def split(value):
    one = value.astype(jnp.bfloat16)
    rest = value - one.astype(jnp.float32)
    two = rest.astype(jnp.bfloat16)
    three = (rest - two.astype(jnp.float32)).astype(jnp.bfloat16)
    return one, two, three


def apply_body(inverse_ref, scale_ref, code_ref, out_ref, rows_ref, all_ref):
    per = code_ref.shape[1] // (12 * FIELDS)
    total = 8 * FIELDS * per
    field = pl.program_id(0)
    one, two, three = split(inverse_ref[...].T)
    main = jnp.concatenate([jnp.concatenate([one, two], axis=1)] * 2, axis=0)
    rest = jnp.concatenate([one, three], axis=0)
    for x in range(8):
        line = (field * 8 + x) * per
        late = line >= total // 2
        other = jnp.where(late, line - total // 2, line)
        shift = jnp.where(late, 0, 8)
        for d in range(F):
            high = code_ref[d, pl.ds(pl.multiple_of(line, 16), per), :].astype(jnp.int32)
            low = code_ref[d, pl.ds(pl.multiple_of(total + other, 16), per), :].astype(jnp.int32) + 32768
            low = lax.shift_right_logical(low, jnp.full(low.shape, shift, jnp.int32)) & 255
            value = ((high << 8) + low).astype(jnp.float32) * (scale_ref[d : d + 1, :] * (1.0 / CODE))
            all_ref[x, d * per : (d + 1) * per, :] = value
    for x in range(8):
        a, b, c = split(all_ref[x])
        wide = jnp.dot(jnp.concatenate([a, b], axis=1), main, preferred_element_type=jnp.float32)
        tail = jnp.dot(jnp.concatenate([c, a], axis=1), rest, preferred_element_type=jnp.float32)
        value = wide[:, :LANES] + (wide[:, LANES:] + tail)
        rows_ref[pl.ds(x, LANES, stride=8), :] = value.T
    out_ref[...] = rows_ref[...].reshape(out_ref.shape)


def apply(inverse, scales, columns):
    per = columns.shape[1] // (12 * FIELDS)
    radial = per * F
    vmem = pl.BlockSpec(memory_space=pltpu.VMEM)
    return pl.pallas_call(
        apply_body,
        grid=(FIELDS,),
        in_specs=[vmem, vmem, vmem],
        out_specs=pl.BlockSpec((1, LANES, 1, 8, radial), lambda i: (0, 0, i, 0, 0)),
        out_shape=jax.ShapeDtypeStruct((1, LANES, FIELDS, 8, radial), jnp.float32),
        scratch_shapes=[
            pltpu.VMEM((LANES * 8, radial), jnp.float32),
            pltpu.VMEM((8, radial, LANES), jnp.float32),
        ],
        compiler_params=pltpu.CompilerParams(vmem_limit_bytes=VMEM_LIMIT),
        name="apply",
    )(inverse, scales, columns)


def make_table(indices, slots):
    times = jnp.arange(slots, dtype=jnp.int32)
    phases = indices[:, None] * times[None, :] % slots
    angles = phases.astype(jnp.float32) * (2.0 * math.pi / slots)
    return jnp.stack([jnp.cos(angles), -jnp.sin(angles)], axis=1)


def stencil_body(place_ref, coupling_ref, velocity_ref, right_ref, left_ref, coef_ref, mask_ref):
    cells, radial = coef_ref.shape[1], velocity_ref.shape[1]
    start = place_ref[0]
    turn = lax.rem(radial + 1 - start, radial)
    sub = lax.broadcasted_iota(jnp.int32, (8, LANES), 0)

    def tiles(index, own):
        gap = jnp.zeros((4, radial), jnp.float32)
        other = jnp.concatenate([right_ref[index], gap, left_ref[index]], axis=0)
        return [pltpu.roll(value, turn, 1) for value in (own, other)]

    def spread_lanes(index, t, value):
        for r in range(cells):
            coef_ref[index, r, t] = jnp.broadcast_to(value[:, r : r + 1], (8, LANES))

    centre = 1.0 - STEP_DT * VISCOSITY * (30.0 / 12.0 + 2.0)

    @pl.loop(0, FIELDS * FIELDS)
    def _(index):
        diagonal = jnp.where(lax.rem(index, FIELDS + 1) == 0, centre, 0.0)
        for t, value in enumerate(tiles(index, coupling_ref[index])):
            spread_lanes(index, t, STEP_DT * value + diagonal)

    near_d, near_c = STEP_DT * 8.0 / 12.0, STEP_DT * VISCOSITY * 16.0 / 12.0
    far_d, far_c = STEP_DT / 12.0, STEP_DT * VISCOSITY / 12.0
    for t, speed in enumerate(tiles(FIELDS * FIELDS, velocity_ref[...])):
        spread_lanes(FIELDS * FIELDS, t, near_d * speed + near_c)
        spread_lanes(FIELDS * FIELDS + 1, t, near_c - near_d * speed)
        spread_lanes(FIELDS * FIELDS + 2, t, -far_d * speed - far_c)
        spread_lanes(FIELDS * FIELDS + 3, t, far_d * speed - far_c)
    sides = jnp.where(sub < HALF, place_ref[2], place_ref[1])
    for r in range(cells):
        here = start - 1 + r
        inside = jnp.where((here >= 0) & (here < radial), 1, 0)
        mask_ref[r, 0] = jnp.full((8, LANES), inside, jnp.int32).astype(jnp.float32)
        mask_ref[r, 1] = (sides * inside).astype(jnp.float32)


def stencil(coupling, velocity, per):
    count = lax.axis_size("space")
    mine = lax.axis_index("space")
    radial = velocity.shape[1]
    up = [(i, i + 1) for i in range(count - 1)]
    down = [(i + 1, i) for i in range(count - 1)]
    coupling = coupling.reshape(FIELDS * FIELDS, 8, radial)
    edges = [jnp.concatenate([coupling[:, s], velocity[None, s]], axis=0) for s in (slice(0, 2), slice(6, 8))]
    right = lax.ppermute(edges[0], "space", down)
    left = lax.ppermute(edges[1], "space", up)
    place = jnp.stack([lax.axis_index("freq") * per, (mine > 0).astype(jnp.int32), (mine < count - 1).astype(jnp.int32)])
    vmem = pl.BlockSpec(memory_space=pltpu.VMEM)
    return pl.pallas_call(
        stencil_body,
        in_specs=[pl.BlockSpec(memory_space=pltpu.SMEM)] + [vmem] * 4,
        out_specs=[vmem, vmem],
        out_shape=[
            jax.ShapeDtypeStruct((FIELDS * FIELDS + 4, per + 2, 2, 8, LANES), jnp.float32),
            jax.ShapeDtypeStruct((per + 2, 2, 8, LANES), jnp.float32),
        ],
        compiler_params=pltpu.CompilerParams(vmem_limit_bytes=VMEM_LIMIT),
        name="stencil",
    )(place, coupling, velocity, right, left)


def local(sketch, coupling, velocity, freq_index):
    groups = lax.axis_size("freq")
    count = lax.axis_size("space")
    radial = sketch.shape[4]
    per = radial // groups
    mine = lax.axis_index("freq")

    rows = spread(sketch, groups)
    coupling, velocity, rows = lax.optimization_barrier((coupling, velocity, rows))
    rows = lax.all_to_all(rows, "freq", split_axis=0, concat_axis=0, tiled=True)

    parity = freq_index % 2
    waves = make_table(freq_index, NT)[:, :, : NT // 2].reshape(F, 2, 4, 2)
    waves = jnp.repeat(waves, K, axis=3)
    angular = math.pi / NT * STEP_DT * freq_index.astype(jnp.float32)
    sign = jnp.where(jnp.arange(LANES) < K, 1.0, -1.0).astype(jnp.float32)
    turn = jnp.broadcast_to((angular[:, None] * sign)[:, None, :], (F, 8, LANES))
    coef, mask = stencil(coupling, velocity, per)

    rows, coef, mask, turn, waves, parity = lax.optimization_barrier((rows, coef, mask, turn, waves, parity))
    right = lax.ppermute(rows[:, 0], "space", [(i + 1, i) for i in range(count - 1)])
    left = lax.ppermute(rows[:, 1], "space", [(i, i + 1) for i in range(count - 1)])
    low, high = fourier(parity, rows, rows, waves, (0, 1))
    right, left = fourier(parity, right[:, None], left[:, None], waves, (0, 0))

    columns, grams = evolve(jnp.arange(F, dtype=jnp.int32), low, high, right, left, coef, mask, turn)
    parts = lax.all_to_all(grams, "freq", split_axis=0, concat_axis=0, tiled=True)
    gram = jnp.sum(parts, axis=0)
    scales = parts[:, K + 1]
    columns, gram = lax.optimization_barrier((columns, gram))
    columns = lax.all_to_all(columns, "freq", split_axis=0, concat_axis=0, tiled=True)
    for bit in (0, 2, 4):
        parts = quad_sum(gram, "space", bit)
        gram = sum(parts)
    row_scale = math.sqrt(FIELDS * 8 * count * radial)
    inverse, factor = factorize(parts, row_scale)
    return apply(inverse, scales, columns), factor[None]


def solution(mesh):
    return jax.shard_map(
        local,
        mesh=mesh,
        in_specs=(
            P("freq", None, None, "space", None),
            P(None, None, "space", None),
            P("space", None),
            P(),
        ),
        out_specs=(P("freq", None, None, "space", None), P("freq", None, None)),
        check_vma=False,
    )
```

```python
from functools import partial
import math

import jax
import jax.numpy as jnp
from jax import lax
from jax.experimental import pallas as pl
from jax.experimental.pallas import tpu as pltpu
from jax.sharding import PartitionSpec as P

K = 64
FIELDS = 5
NT = 16
F = 8
STEP_DT = 0.25
VISCOSITY = 0.5
LANES = 2 * K
HALF = 4
SPACE = ("chip", "core")
RH = 2
VMEM_LIMIT = 28 * 1024 * 1024


def xor_sum(value, axis, masks):
    count = lax.axis_size(axis)
    for other in [lax.ppermute(value, axis, [(i, i ^ m) for i in range(count)]) for m in masks]:
        value = value + other
    return value


def spread_body(sketch_ref, out_ref, rows_ref, turned_ref):
    groups = out_ref.shape[0]
    radial = sketch_ref.shape[4]
    per = radial // groups
    rows_ref[...] = sketch_ref[...].astype(jnp.float32).reshape(LANES * 8, radial)
    edge = jnp.zeros((RH * HALF, LANES), jnp.float32)
    for half in range(2):
        turned_ref[half, 0 : RH * HALF, :] = edge
        turned_ref[half, (radial + RH) * HALF :, :] = edge
    for x in range(8):
        block = rows_ref[pl.ds(x, LANES, stride=8), :]
        turned_ref[x // HALF, pl.ds(RH * HALF + x % HALF, radial, stride=HALF), :] = block.T
    count = (per + 2 * RH) * HALF
    for half in range(2):
        for group in range(groups):
            start = group * per * HALF
            out_ref[group, half] = turned_ref[half, start : start + count, :].astype(jnp.bfloat16)


def spread(sketch, groups):
    radial = sketch.shape[4]
    rows = (radial // groups + 2 * RH) * HALF
    return pl.pallas_call(
        spread_body,
        grid=(FIELDS,),
        in_specs=[pl.BlockSpec((2, K, 1, 8, radial), lambda i: (0, 0, i, 0, 0))],
        out_specs=pl.BlockSpec((groups, 2, rows, LANES), lambda i: (0, 0, i, 0)),
        out_shape=jax.ShapeDtypeStruct((groups, 2, FIELDS * rows, LANES), jnp.bfloat16),
        scratch_shapes=[
            pltpu.VMEM((LANES * 8, radial), jnp.float32),
            pltpu.VMEM((2, (radial + 2 * RH) * HALF, LANES), jnp.float32),
        ],
        compiler_params=pltpu.CompilerParams(vmem_limit_bytes=VMEM_LIMIT),
        name="spread",
    )(sketch)


def fourier_body(parity_ref, one_ref, two_ref, table_ref, z_one, z_two, pair_ref):
    size = pair_ref.shape[2]
    first = lax.broadcasted_iota(jnp.int32, (8, LANES), 1) < K
    for rows_ref, z_ref in ((one_ref, z_one), (two_ref, z_two)):

        @pl.loop(0, rows_ref.shape[2] // size)
        def _(step):
            start = pl.multiple_of(step * size, size)
            for d in range(4):
                a = rows_ref[d, 0, pl.ds(start, size), :].astype(jnp.float32)
                b = rows_ref[d + 4, 0, pl.ds(start, size), :].astype(jnp.float32)
                pair_ref[0, d] = a + b
                pair_ref[1, d] = a - b
            for f in range(F):
                parity = parity_ref[f]
                wave = [[jnp.broadcast_to(table_ref[f, c, d : d + 1], (8, LANES)) for d in range(4)] for c in range(2)]
                for line in range(0, size, 8):
                    p = [pair_ref[parity, d, line : line + 8] for d in range(4)]
                    u = (p[0] * wave[0][0] + p[1] * wave[0][1]) + (p[2] * wave[0][2] + p[3] * wave[0][3])
                    v = (p[0] * wave[1][0] + p[1] * wave[1][1]) + (p[2] * wave[1][2] + p[3] * wave[1][3])
                    z_ref[f, pl.ds(start + line, 8), :] = jnp.where(first, u, v) + pltpu.roll(
                        jnp.where(first, v, u), K, 1
                    )


def fourier(parity, one, two, table, parts):
    slots, _, count, _ = one.shape
    size = count // FIELDS
    z_spec = pl.BlockSpec((F, count, LANES), lambda i: (0, 0, 0))
    z_shape = jax.ShapeDtypeStruct((F, count, LANES), jnp.float32)
    return pl.pallas_call(
        fourier_body,
        grid=(1,),
        in_specs=[
            pl.BlockSpec(memory_space=pltpu.SMEM),
            pl.BlockSpec((slots, 1, count, LANES), lambda i: (0, parts[0], 0, 0)),
            pl.BlockSpec((slots, 1, count, LANES), lambda i: (0, parts[1], 0, 0)),
            pl.BlockSpec(table.shape, lambda i: (0, 0, 0, 0)),
        ],
        out_specs=[z_spec, z_spec],
        out_shape=[z_shape, z_shape],
        scratch_shapes=[pltpu.VMEM((2, 4, size, LANES), jnp.float32)],
        compiler_params=pltpu.CompilerParams(vmem_limit_bytes=VMEM_LIMIT),
        name="fourier",
    )(parity, one, two, table)


CODE = 8388000.0


def encode(block, scale):
    number = jnp.round(block * (CODE / scale)).astype(jnp.int32)
    half = block.shape[0] // 2
    low = number & 255
    both = (low[:half] << 8) + low[half:] - 32768
    return (number >> 8).astype(jnp.int16), both.astype(jnp.int16)


HALF_ROWS = K // 2 + 8


def pack(gram, scale, ref, n):
    line = lax.broadcasted_iota(jnp.int32, (K, LANES), 0)
    lane = lax.broadcasted_iota(jnp.int32, (K, LANES), 1)
    last = pltpu.roll(gram[K:], K, 1)
    both = jnp.where(lane >= line, gram[:K], last)
    diagonal = jnp.sum(jnp.where(lane == line, last, 0.0), axis=0, keepdims=True)
    sub = lax.broadcasted_iota(jnp.int32, (8, LANES), 0)
    for h in range(2):
        ref[n, h, 0 : K // 2, :] = both[h * K // 2 : (h + 1) * K // 2]
        ref[n, h, K // 2 :, :] = jnp.where(sub == 0, diagonal, scale)


def unpack(one, two):
    line = lax.broadcasted_iota(jnp.int32, (K, LANES), 0)
    lane = lax.broadcasted_iota(jnp.int32, (K, LANES), 1)
    top = jnp.concatenate([one[: K // 2], two[: K // 2]], axis=0)
    last = pltpu.roll(jnp.where(lane < line, top, 0.0), K, 1)
    half = jnp.concatenate([jnp.where(lane >= line, top, 0.0), last], axis=0)
    diagonal = pltpu.roll(jnp.broadcast_to(one[K // 2 : K // 2 + 1], (8, LANES)), K, 1)
    diagonal = jnp.concatenate([top] + [diagonal] * (K // 8), axis=0)
    line = lax.broadcasted_iota(jnp.int32, (LANES, LANES), 0)
    lane = lax.broadcasted_iota(jnp.int32, (LANES, LANES), 1)
    return jnp.where(line == lane, diagonal, half + half.T)


def evolve_body(order_ref, *refs):
    layers, (coef_ref, mask_ref, turn_a, turn_b, code_ref, gram_ref, z_ref, s_ref, out_ref) = refs[:8], refs[8:]
    wide = z_ref.shape[2]
    per = wide - 2 * RH
    sub = lax.broadcasted_iota(jnp.int32, (8, LANES), 0)

    @pl.loop(0, layers[0].shape[1] // 8, unroll=5)
    def _(step):
        here = pl.ds(pl.multiple_of(step * 8, 8), 8)
        line = step * 2
        field = line // wide
        cell = line % wide
        for n in range(2):
            for tile in range(2):
                a = layers[4 * n + 2 * tile][0, here, :]
                b = layers[4 * n + 2 * tile + 1][0, here, :]
                z_ref[n, field, cell, tile] = jnp.where(sub < HALF, a, pltpu.roll(b, HALF, 0))
                z_ref[n, field, cell + 1, tile] = jnp.where(sub < HALF, pltpu.roll(a, HALF, 0), b)

    turns = [turn_a[0], turn_b[0]]

    def shifted(tiles, shift, t):
        keep = (sub < 8 - shift) if shift > 0 else (sub >= -shift)
        turned = [pltpu.roll(v, (-shift) % 8, 0) for v in tiles]
        return jnp.where(keep, turned[t], turned[1 - t])

    def advance(ref, r, place, t, store):
        q = [[ref[n, j, r, t] for j in range(FIELDS)] for n in range(2)]
        for i in range(FIELDS):
            coupled = [coef_ref[j * FIELDS + i, place, t] for j in range(FIELDS)]
            moves = [coef_ref[FIELDS * FIELDS + m, place, t] for m in range(4)]
            for n in range(2):
                value = coupled[0] * q[n][0]
                for j in range(1, FIELDS):
                    value = value + coupled[j] * q[n][j]
                pair = [None, None]
                pair[t] = q[n][i]
                pair[1 - t] = ref[n, i, r, 1 - t]
                for m, shift in enumerate((1, -1, 2, -2)):
                    value = value + moves[m] * shifted(pair, shift, t)
                value = value + (STEP_DT * VISCOSITY) * (ref[n, i, r - 1, t] + ref[n, i, r + 1, t])
                store(n, i, value + turns[n] * pltpu.roll(q[n][i], K, 1))

    @pl.loop(0, per + 2)
    def _(r):
        for t in range(2):
            mask = mask_ref[r, t]

            def store(n, i, value):
                s_ref[n, i, r, t] = value * mask

            advance(z_ref, r + 1, r, t, store)

    @pl.loop(0, per, unroll=2)
    def _(r):
        def store(n, i, value):
            out_ref[n, pl.ds(i * 8 * per + r, 8, stride=per), :] = value

        advance(s_ref, r + 1, r + 1, 0, store)

    for n in range(2):
        block = out_ref[n]
        gram = lax.dot_general(
            block, block, (((0,), (0,)), ((), ())),
            precision=lax.Precision.HIGHEST, preferred_element_type=jnp.float32,
        )
        scale = jnp.maximum(jnp.max(jnp.abs(block), axis=0, keepdims=True), 1e-30)
        pack(gram, scale, gram_ref, n)
        count = block.shape[0]
        code_ref[n, 0:count, :], code_ref[n, count : count + count // 2, :] = encode(block, scale)


def evolve(order, low, high, right, left, coef, mask, turn):
    count = order.shape[0]
    per = coef.shape[1] - 2
    rows = low.shape[1]
    whole = lambda shape: pl.BlockSpec(shape, lambda i, order: (0,) * len(shape))
    pick = lambda shape, n: pl.BlockSpec((1,) + shape, lambda i, order: (order[2 * i + n], 0, 0))
    layers = [pick((rows, LANES), n) for n in range(2) for _ in range(4)]
    return pl.pallas_call(
        evolve_body,
        grid_spec=pltpu.PrefetchScalarGridSpec(
            num_scalar_prefetch=1,
            grid=(count // 2,),
            in_specs=layers
            + [whole(coef.shape), whole(mask.shape), pick((8, LANES), 0), pick((8, LANES), 1)],
            out_specs=[
                pl.BlockSpec((2, FIELDS * 12 * per, LANES), lambda i, order: (i, 0, 0)),
                pl.BlockSpec((2, 2, HALF_ROWS, LANES), lambda i, order: (i, 0, 0, 0)),
            ],
            scratch_shapes=[
                pltpu.VMEM((2, FIELDS, per + 2 * RH, 2, 8, LANES), jnp.float32),
                pltpu.VMEM((2, FIELDS, per + 2, 2, 8, LANES), jnp.float32),
                pltpu.VMEM((2, FIELDS * 8 * per, LANES), jnp.float32),
            ],
        ),
        out_shape=[
            jax.ShapeDtypeStruct((count, FIELDS * 12 * per, LANES), jnp.int16),
            jax.ShapeDtypeStruct((count, 2, HALF_ROWS, LANES), jnp.float32),
        ],
        compiler_params=pltpu.CompilerParams(vmem_limit_bytes=VMEM_LIMIT),
        name="evolve",
    )(order, *([low, high, right, left] * 2), coef, mask, turn, turn)


def factor_body(scale, *refs):
    parts = refs[:-2]
    inverse_ref, factor_ref = refs[-2:]
    blocks = LANES // 8
    lane = lax.broadcasted_iota(jnp.int32, (8, LANES), 1)
    sub = lax.broadcasted_iota(jnp.int32, (8, LANES), 0)
    gram = unpack(parts[0][...], parts[1][...])
    w = [gram[8 * b : 8 * b + 8] for b in range(blocks)]
    full = lambda v: jnp.broadcast_to(v, (8, LANES))
    for b in range(blocks):
        columns = [[full(w[i][:, 8 * b + k : 8 * b + k + 1]) for k in range(8)] for i in range(b, blocks)]
        rows = [full(w[b][k : k + 1, :]) for k in range(8)]
        a = [[full(columns[0][k][i : i + 1, :]) for k in range(i + 1)] for i in range(8)]
        low = [[None] * 8 for _ in range(8)]
        m = [[None] * 8 for _ in range(8)]
        for j in range(8):
            root = lax.rsqrt(a[j][j])
            root = root * (1.5 - 0.5 * (a[j][j] * root) * root)
            m[j][j] = root
            for i in range(j + 1, 8):
                low[i][j] = a[i][j] * root
            for i in range(j + 1, 8):
                for k in range(j + 1, i + 1):
                    a[i][k] = a[i][k] - low[i][j] * low[k][j]
            for k in range(j):
                total = low[j][k] * m[k][k]
                for n in range(k + 1, j):
                    total = total + low[j][n] * m[n][k]
                m[j][k] = -(total * root)
        inside = (lane >= 8 * b) & (lane < 8 * b + 8)
        ones = [jnp.where(inside, jnp.where(lane == 8 * b + k, 1.0, 0.0), rows[k]) for k in range(8)]
        final = [None] * 8
        upper = None
        lower = None
        for i in range(8):
            top = m[i][0] * rows[0]
            final[i] = m[i][0] * ones[0]
            for k in range(1, i + 1):
                top = top + m[i][k] * rows[k]
                final[i] = final[i] + m[i][k] * ones[k]
            upper = top if i == 0 else jnp.where(sub == i, top, upper)
            lower = final[i] if i == 0 else jnp.where(sub == i, final[i], lower)
        inverse_ref[8 * b : 8 * b + 8, :] = jnp.where(lane <= sub + 8 * b, lower * scale, 0.0)
        factor_ref[8 * b : 8 * b + 8, :] = jnp.where(lane >= sub + 8 * b, upper * (1.0 / scale), 0.0)
        if b + 1 < blocks:
            solved = []
            for k in range(8):
                total = m[k][k] * final[k]
                for i in range(k + 1, 8):
                    total = total + m[i][k] * final[i]
                solved.append(total)
            for i in range(b + 1, blocks):
                c = columns[i - b]
                products = [c[k] * solved[k] for k in range(8)]
                while len(products) > 1:
                    products = [products[n] + products[n + 1] for n in range(0, len(products), 2)]
                w[i] = jnp.where(inside, 0.0, w[i]) - products[0]
    factor_ref[...] = factor_ref[...].T


def factorize(parts, scale):
    vmem = pl.BlockSpec(memory_space=pltpu.VMEM)
    shape = jax.ShapeDtypeStruct((LANES, LANES), jnp.float32)
    return pl.pallas_call(
        partial(factor_body, scale),
        in_specs=[vmem] * len(parts),
        out_specs=[vmem, vmem],
        out_shape=[shape, shape],
        name="factorize",
    )(*parts)


def split(value):
    one = value.astype(jnp.bfloat16)
    rest = value - one.astype(jnp.float32)
    two = rest.astype(jnp.bfloat16)
    three = (rest - two.astype(jnp.float32)).astype(jnp.bfloat16)
    return one, two, three


def apply_body(inverse_ref, scale_ref, code_ref, out_ref, rows_ref, all_ref):
    per = code_ref.shape[1] // (12 * FIELDS)
    total = 8 * FIELDS * per
    field = pl.program_id(0)
    one, two, three = split(inverse_ref[...].T)
    main = jnp.concatenate([jnp.concatenate([one, two], axis=1)] * 2, axis=0)
    rest = jnp.concatenate([one, three], axis=0)
    for x in range(8):
        line = (field * 8 + x) * per
        late = line >= total // 2
        other = jnp.where(late, line - total // 2, line)
        shift = jnp.where(late, 0, 8)
        for d in range(F):
            high = code_ref[d, pl.ds(pl.multiple_of(line, 16), per), :].astype(jnp.int32)
            low = code_ref[d, pl.ds(pl.multiple_of(total + other, 16), per), :].astype(jnp.int32) + 32768
            low = lax.shift_right_logical(low, jnp.full(low.shape, shift, jnp.int32)) & 255
            value = ((high << 8) + low).astype(jnp.float32) * (scale_ref[d : d + 1, :] * (1.0 / CODE))
            all_ref[x, d * per : (d + 1) * per, :] = value
    for x in range(8):
        a, b, c = split(all_ref[x])
        wide = jnp.dot(jnp.concatenate([a, b], axis=1), main, preferred_element_type=jnp.float32)
        tail = jnp.dot(jnp.concatenate([c, a], axis=1), rest, preferred_element_type=jnp.float32)
        value = wide[:, :LANES] + (wide[:, LANES:] + tail)
        rows_ref[pl.ds(x, LANES, stride=8), :] = value.T
    out_ref[...] = rows_ref[...].reshape(out_ref.shape)


def apply(inverse, scales, columns):
    per = columns.shape[1] // (12 * FIELDS)
    radial = per * F
    vmem = pl.BlockSpec(memory_space=pltpu.VMEM)
    return pl.pallas_call(
        apply_body,
        grid=(FIELDS,),
        in_specs=[vmem, vmem, vmem],
        out_specs=pl.BlockSpec((1, LANES, 1, 8, radial), lambda i: (0, 0, i, 0, 0)),
        out_shape=jax.ShapeDtypeStruct((1, LANES, FIELDS, 8, radial), jnp.float32),
        scratch_shapes=[
            pltpu.VMEM((LANES * 8, radial), jnp.float32),
            pltpu.VMEM((8, radial, LANES), jnp.float32),
        ],
        compiler_params=pltpu.CompilerParams(vmem_limit_bytes=VMEM_LIMIT),
        name="apply",
    )(inverse, scales, columns)


def make_table(indices, slots):
    times = jnp.arange(slots, dtype=jnp.int32)
    phases = indices[:, None] * times[None, :] % slots
    angles = phases.astype(jnp.float32) * (2.0 * math.pi / slots)
    return jnp.stack([jnp.cos(angles), -jnp.sin(angles)], axis=1)


def stencil_body(place_ref, coupling_ref, velocity_ref, right_ref, left_ref, coef_ref, mask_ref):
    cells, radial = coef_ref.shape[1], velocity_ref.shape[1]
    start = place_ref[0]
    turn = lax.rem(radial + 1 - start, radial)
    sub = lax.broadcasted_iota(jnp.int32, (8, LANES), 0)

    def tiles(index, own):
        gap = jnp.zeros((4, radial), jnp.float32)
        other = jnp.concatenate([right_ref[index], gap, left_ref[index]], axis=0)
        return [pltpu.roll(value, turn, 1) for value in (own, other)]

    def spread_lanes(index, t, value):
        for r in range(cells):
            coef_ref[index, r, t] = jnp.broadcast_to(value[:, r : r + 1], (8, LANES))

    centre = 1.0 - STEP_DT * VISCOSITY * (30.0 / 12.0 + 2.0)

    @pl.loop(0, FIELDS * FIELDS)
    def _(index):
        diagonal = jnp.where(lax.rem(index, FIELDS + 1) == 0, centre, 0.0)
        for t, value in enumerate(tiles(index, coupling_ref[index])):
            spread_lanes(index, t, STEP_DT * value + diagonal)

    near_d, near_c = STEP_DT * 8.0 / 12.0, STEP_DT * VISCOSITY * 16.0 / 12.0
    far_d, far_c = STEP_DT / 12.0, STEP_DT * VISCOSITY / 12.0
    for t, speed in enumerate(tiles(FIELDS * FIELDS, velocity_ref[...])):
        spread_lanes(FIELDS * FIELDS, t, near_d * speed + near_c)
        spread_lanes(FIELDS * FIELDS + 1, t, near_c - near_d * speed)
        spread_lanes(FIELDS * FIELDS + 2, t, -far_d * speed - far_c)
        spread_lanes(FIELDS * FIELDS + 3, t, far_d * speed - far_c)
    sides = jnp.where(sub < HALF, place_ref[2], place_ref[1])
    for r in range(cells):
        here = start - 1 + r
        inside = jnp.where((here >= 0) & (here < radial), 1, 0)
        mask_ref[r, 0] = jnp.full((8, LANES), inside, jnp.int32).astype(jnp.float32)
        mask_ref[r, 1] = (sides * inside).astype(jnp.float32)


def stencil(coupling, velocity, per):
    count = lax.axis_size(SPACE)
    mine = lax.axis_index(SPACE)
    radial = velocity.shape[1]
    up = [(i, i + 1) for i in range(count - 1)]
    down = [(i + 1, i) for i in range(count - 1)]
    coupling = coupling.reshape(FIELDS * FIELDS, 8, radial)
    edges = [jnp.concatenate([coupling[:, s], velocity[None, s]], axis=0) for s in (slice(0, 2), slice(6, 8))]
    right = lax.ppermute(edges[0], SPACE, down)
    left = lax.ppermute(edges[1], SPACE, up)
    place = jnp.stack([lax.axis_index("freq") * per, (mine > 0).astype(jnp.int32), (mine < count - 1).astype(jnp.int32)])
    vmem = pl.BlockSpec(memory_space=pltpu.VMEM)
    return pl.pallas_call(
        stencil_body,
        in_specs=[pl.BlockSpec(memory_space=pltpu.SMEM)] + [vmem] * 4,
        out_specs=[vmem, vmem],
        out_shape=[
            jax.ShapeDtypeStruct((FIELDS * FIELDS + 4, per + 2, 2, 8, LANES), jnp.float32),
            jax.ShapeDtypeStruct((per + 2, 2, 8, LANES), jnp.float32),
        ],
        compiler_params=pltpu.CompilerParams(vmem_limit_bytes=VMEM_LIMIT),
        name="stencil",
    )(place, coupling, velocity, right, left)


def local(sketch, coupling, velocity, freq_index):
    groups = lax.axis_size("freq")
    count = lax.axis_size(SPACE)
    radial = sketch.shape[4]
    per = radial // groups
    mine = lax.axis_index("freq")

    rows = spread(sketch, groups)
    coupling, velocity, rows = lax.optimization_barrier((coupling, velocity, rows))
    rows = lax.all_to_all(rows, "freq", split_axis=0, concat_axis=0, tiled=True)

    parity = freq_index % 2
    waves = make_table(freq_index, NT)[:, :, : NT // 2].reshape(F, 2, 4, 2)
    waves = jnp.repeat(waves, K, axis=3)
    angular = math.pi / NT * STEP_DT * freq_index.astype(jnp.float32)
    sign = jnp.where(jnp.arange(LANES) < K, 1.0, -1.0).astype(jnp.float32)
    turn = jnp.broadcast_to((angular[:, None] * sign)[:, None, :], (F, 8, LANES))
    coef, mask = stencil(coupling, velocity, per)

    rows, coef, mask, turn, waves, parity = lax.optimization_barrier((rows, coef, mask, turn, waves, parity))
    right = lax.ppermute(rows[:, 0], SPACE, [(i + 1, i) for i in range(count - 1)])
    left = lax.ppermute(rows[:, 1], SPACE, [(i, i + 1) for i in range(count - 1)])
    low, high = fourier(parity, rows, rows, waves, (0, 1))
    right, left = fourier(parity, right[:, None], left[:, None], waves, (0, 0))

    columns, grams = evolve(jnp.arange(F, dtype=jnp.int32), low, high, right, left, coef, mask, turn)
    core = lax.axis_index("core")
    grams = grams.reshape(groups * 2, HALF_ROWS, LANES)
    parts = lax.all_to_all(grams, ("freq", "core"), split_axis=0, concat_axis=0, tiled=True)
    gram = jnp.sum(parts, axis=0)
    parts = parts.reshape(groups, 2, HALF_ROWS, LANES)[:, :, K // 2 + 1]
    scales = jnp.where(core == 0, parts[:, 0], parts[:, 1])
    columns, gram = lax.optimization_barrier((columns, gram))
    columns = lax.all_to_all(columns, "freq", split_axis=0, concat_axis=0, tiled=True)
    gram = xor_sum(gram, "chip", (16, 8, 24))
    gram = xor_sum(gram, "chip", (2, 1, 3))
    gram = xor_sum(gram, "chip", (4,))
    other = lax.ppermute(gram, "core", [(0, 1), (1, 0)])
    parts = [jnp.where(core == 0, gram, other), jnp.where(core == 0, other, gram)]
    row_scale = math.sqrt(FIELDS * 8 * count * radial)
    inverse, factor = factorize(parts, row_scale)
    return apply(inverse, scales, columns), factor[None]


def solution(mesh):
    devices = mesh.devices
    split_mesh = jax.sharding.Mesh(
        devices.reshape(devices.shape[0] // 2, 2, devices.shape[1]), ("chip", "core", "freq")
    )
    return jax.shard_map(
        local,
        mesh=split_mesh,
        in_specs=(
            P("freq", None, None, SPACE, None),
            P(None, None, SPACE, None),
            P(SPACE, None),
            P(),
        ),
        out_specs=(P("freq", None, None, SPACE, None), P("freq", None, None)),
        check_vma=False,
    )
```

```python
from functools import partial
import math

import jax
import jax.numpy as jnp
from jax import lax
from jax.experimental import pallas as pl
from jax.experimental.pallas import tpu as pltpu
from jax.sharding import PartitionSpec as P

K = 64
FIELDS = 5
NT = 16
F = 8
STEP_DT = 0.25
VISCOSITY = 0.5
LANES = 2 * K
HALF = 4
SPACE = ("chip", "core")
RH = 2
PITCH = 24
TOGETHER = 4
VMEM_LIMIT = 28 * 1024 * 1024


def xor_sum(value, axis, masks):
    count = lax.axis_size(axis)
    for other in [lax.ppermute(value, axis, [(i, i ^ m) for i in range(count)]) for m in masks]:
        value = value + other
    return value


def spread_body(sketch_ref, out_ref, rows_ref, turned_ref):
    groups = out_ref.shape[0]
    radial = sketch_ref.shape[4]
    per = radial // groups
    rows_ref[...] = sketch_ref[...].astype(jnp.float32).reshape(LANES * 8, radial)
    edge = jnp.zeros((RH * HALF, LANES), jnp.float32)
    for half in range(2):
        turned_ref[half, 0 : RH * HALF, :] = edge
        turned_ref[half, (radial + RH) * HALF :, :] = edge
    for x in range(8):
        block = rows_ref[pl.ds(x, LANES, stride=8), :]
        turned_ref[x // HALF, pl.ds(RH * HALF + x % HALF, radial, stride=HALF), :] = block.T
    count = (per + 2 * RH) * HALF
    for half in range(2):
        for group in range(groups):
            start = group * per * HALF
            out_ref[group, half] = turned_ref[half, start : start + count, :].astype(jnp.bfloat16)


def spread(sketch, groups):
    radial = sketch.shape[4]
    rows = (radial // groups + 2 * RH) * HALF
    return pl.pallas_call(
        spread_body,
        grid=(FIELDS,),
        in_specs=[pl.BlockSpec((2, K, 1, 8, radial), lambda i: (0, 0, i, 0, 0))],
        out_specs=pl.BlockSpec((groups, 2, rows, LANES), lambda i: (0, 0, i, 0)),
        out_shape=jax.ShapeDtypeStruct((groups, 2, FIELDS * rows, LANES), jnp.bfloat16),
        scratch_shapes=[
            pltpu.VMEM((LANES * 8, radial), jnp.float32),
            pltpu.VMEM((2, (radial + 2 * RH) * HALF, LANES), jnp.float32),
        ],
        compiler_params=pltpu.CompilerParams(vmem_limit_bytes=2 * VMEM_LIMIT),
        name="spread",
    )(sketch)


def fourier_body(parity_ref, one_ref, two_ref, table_ref, z_one, z_two, pair_ref):
    size = pair_ref.shape[2]
    first = lax.broadcasted_iota(jnp.int32, (8, LANES), 1) < K
    for rows_ref, z_ref in ((one_ref, z_one), (two_ref, z_two)):

        @pl.loop(0, rows_ref.shape[2] // size)
        def _(step):
            start = pl.multiple_of(step * size, size)
            for d in range(4):
                a = rows_ref[d, 0, pl.ds(start, size), :].astype(jnp.float32)
                b = rows_ref[d + 4, 0, pl.ds(start, size), :].astype(jnp.float32)
                pair_ref[0, d] = a + b
                pair_ref[1, d] = a - b
            for f in range(F):
                parity = parity_ref[f]
                wave = [[jnp.broadcast_to(table_ref[f, c, d : d + 1], (8, LANES)) for d in range(4)] for c in range(2)]
                for line in range(0, size, 8):
                    p = [pair_ref[parity, d, line : line + 8] for d in range(4)]
                    u = (p[0] * wave[0][0] + p[1] * wave[0][1]) + (p[2] * wave[0][2] + p[3] * wave[0][3])
                    v = (p[0] * wave[1][0] + p[1] * wave[1][1]) + (p[2] * wave[1][2] + p[3] * wave[1][3])
                    z_ref[f, pl.ds(start + line, 8), :] = jnp.where(first, u, v) + pltpu.roll(
                        jnp.where(first, v, u), K, 1
                    )


def fourier(parity, one, two, table, parts):
    slots, _, count, _ = one.shape
    size = count // FIELDS
    z_spec = pl.BlockSpec((F, count, LANES), lambda i: (0, 0, 0))
    z_shape = jax.ShapeDtypeStruct((F, count, LANES), jnp.float32)
    return pl.pallas_call(
        fourier_body,
        grid=(1,),
        in_specs=[
            pl.BlockSpec(memory_space=pltpu.SMEM),
            pl.BlockSpec((slots, 1, count, LANES), lambda i: (0, parts[0], 0, 0)),
            pl.BlockSpec((slots, 1, count, LANES), lambda i: (0, parts[1], 0, 0)),
            pl.BlockSpec(table.shape, lambda i: (0, 0, 0, 0)),
        ],
        out_specs=[z_spec, z_spec],
        out_shape=[z_shape, z_shape],
        scratch_shapes=[pltpu.VMEM((2, 4, size, LANES), jnp.float32)],
        compiler_params=pltpu.CompilerParams(vmem_limit_bytes=VMEM_LIMIT),
        name="fourier",
    )(parity, one, two, table)


def split(value):
    one = value.astype(jnp.bfloat16)
    rest = value - one.astype(jnp.float32)
    two = rest.astype(jnp.bfloat16)
    three = (rest - two.astype(jnp.float32)).astype(jnp.bfloat16)
    return one, two, three


CODE = 8388000.0


def encode(block, scale):
    number = jnp.round(block * (CODE / scale)).astype(jnp.int32)
    half = block.shape[0] // 2
    low = number & 255
    both = (low[:half] << 8) + low[half:] - 32768
    return (number >> 8).astype(jnp.int16), both.astype(jnp.int16)


HALF_ROWS = K // 2 + 8


def pack(gram, scale, ref, n):
    line = lax.broadcasted_iota(jnp.int32, (K, LANES), 0)
    lane = lax.broadcasted_iota(jnp.int32, (K, LANES), 1)
    last = pltpu.roll(gram[K:], K, 1)
    both = jnp.where(lane >= line, gram[:K], last)
    diagonal = jnp.sum(jnp.where(lane == line, last, 0.0), axis=0, keepdims=True)
    sub = lax.broadcasted_iota(jnp.int32, (8, LANES), 0)
    for h in range(2):
        ref[n, h, 0 : K // 2, :] = both[h * K // 2 : (h + 1) * K // 2]
        ref[n, h, K // 2 :, :] = jnp.where(sub == 0, diagonal, scale)


def unpack(one, two):
    line = lax.broadcasted_iota(jnp.int32, (K, LANES), 0)
    lane = lax.broadcasted_iota(jnp.int32, (K, LANES), 1)
    top = jnp.concatenate([one[: K // 2], two[: K // 2]], axis=0)
    last = pltpu.roll(jnp.where(lane < line, top, 0.0), K, 1)
    half = jnp.concatenate([jnp.where(lane >= line, top, 0.0), last], axis=0)
    diagonal = pltpu.roll(jnp.broadcast_to(one[K // 2 : K // 2 + 1], (8, LANES)), K, 1)
    diagonal = jnp.concatenate([top] + [diagonal] * (K // 8), axis=0)
    line = lax.broadcasted_iota(jnp.int32, (LANES, LANES), 0)
    lane = lax.broadcasted_iota(jnp.int32, (LANES, LANES), 1)
    return jnp.where(line == lane, diagonal, half + half.T)


def evolve_body(order_ref, *refs):
    layers, turn_refs = refs[: 4 * TOGETHER], refs[4 * TOGETHER : 5 * TOGETHER]
    coef_ref, mask_ref, code_ref, gram_ref, z_ref, s_ref, out_ref = refs[5 * TOGETHER :]
    per = out_ref.shape[1] // (8 * FIELDS)
    wide = per + 2 * RH

    for n in range(TOGETHER):
        low, high, right, left = layers[4 * n : 4 * n + 4]

        @pl.loop(0, FIELDS)
        def _(field):
            for group, ref in enumerate((left, low, high, right)):
                for x in range(HALF):
                    source = field * wide * HALF + x
                    target = 8 + PITCH * (group * HALF + x)
                    z_ref[n, field, target - RH : target, :] = ref[0, pl.ds(source, RH, stride=HALF), :]
                    for r in range(0, per, 8):
                        z_ref[n, field, target + r : target + r + 8, :] = ref[
                            0, pl.ds(source + (r + RH) * HALF, 8, stride=HALF), :
                        ]
                    z_ref[n, field, target + per : target + per + RH, :] = ref[
                        0, pl.ds(source + (per + RH) * HALF, RH, stride=HALF), :
                    ]

    turns = [ref[0] for ref in turn_refs]

    def advance(ref, line, place, store):
        q = [[ref[n, j, pl.ds(line, 8), :] for j in range(FIELDS)] for n in range(TOGETHER)]
        for i in range(FIELDS):
            coupled = [coef_ref[j * FIELDS + i, pl.ds(place, 8), :] for j in range(FIELDS)]
            moves = [coef_ref[FIELDS * FIELDS + m, pl.ds(place, 8), :] for m in range(4)]
            for n in range(TOGETHER):
                value = coupled[0] * q[n][0]
                for j in range(1, FIELDS):
                    value = value + coupled[j] * q[n][j]
                for m, shift in enumerate((1, -1, 2, -2)):
                    value = value + moves[m] * ref[n, i, pl.ds(line + PITCH * shift, 8), :]
                side = ref[n, i, pl.ds(line - 1, 8), :] + ref[n, i, pl.ds(line + 1, 8), :]
                value = value + (STEP_DT * VISCOSITY) * side
                store(n, i, value + turns[n] * pltpu.roll(q[n][i], K, 1))

    def first_step(place):
        mask = mask_ref[pl.ds(place, 8), :]

        def store(n, i, value):
            s_ref[n, i, pl.ds(place, 8), :] = value * mask

        advance(z_ref, pl.multiple_of(place + 2 * PITCH, 8), place, store)

    @pl.loop(0, 12)
    def _(x):
        for r in range(0, per, 8):
            first_step(pl.multiple_of(8 + PITCH * x + r, 8))

    @pl.loop(1, 10)
    def _(x):
        first_step(pl.multiple_of(8 + PITCH * x + per, 8))

    @pl.loop(0, 8)
    def _(x):
        for r in range(0, per, 8):
            line = pl.multiple_of(8 + PITCH * (x + 2) + r, 8)

            def store(n, i, value):
                out_ref[n, pl.ds(pl.multiple_of((i * 8 + x) * per + r, 8), 8), :] = value

            advance(s_ref, line, line, store)

    for n in range(TOGETHER):
        block = out_ref[n]
        one, two, three = split(block)
        pair = jnp.concatenate([one, two], axis=1)
        contract = (((0,), (0,)), ((), ()))
        wide = lax.dot_general(pair, pair, contract, preferred_element_type=jnp.float32)
        thin = lax.dot_general(one, three, contract, preferred_element_type=jnp.float32)
        cross = wide[:LANES, LANES:] + thin
        gram = wide[:LANES, :LANES] + (cross + cross.T + wide[LANES:, LANES:])
        scale = jnp.maximum(jnp.max(jnp.abs(block), axis=0, keepdims=True), 1e-30)
        pack(gram, scale, gram_ref, n)
        count = block.shape[0]
        code_ref[n, 0:count, :], code_ref[n, count : count + count // 2, :] = encode(block, scale)


def evolve(order, low, high, right, left, coef, mask, turn):
    count = order.shape[0]
    rows = low.shape[1]
    per = rows // (FIELDS * HALF) - 2 * RH
    whole = lambda shape: pl.BlockSpec(shape, lambda i, order: (0,) * len(shape))
    pick = lambda shape, n: pl.BlockSpec((1,) + shape, lambda i, order: (order[TOGETHER * i + n], 0, 0))
    layers = [pick((rows, LANES), n) for n in range(TOGETHER) for _ in range(4)]
    return pl.pallas_call(
        evolve_body,
        grid_spec=pltpu.PrefetchScalarGridSpec(
            num_scalar_prefetch=1,
            grid=(count // TOGETHER,),
            in_specs=layers
            + [pick((8, LANES), n) for n in range(TOGETHER)]
            + [whole(coef.shape), whole(mask.shape)],
            out_specs=[
                pl.BlockSpec((TOGETHER, FIELDS * 12 * per, LANES), lambda i, order: (i, 0, 0)),
                pl.BlockSpec((TOGETHER, 2, HALF_ROWS, LANES), lambda i, order: (i, 0, 0, 0)),
            ],
            scratch_shapes=[
                pltpu.VMEM((TOGETHER, FIELDS, 16 + 16 * PITCH, LANES), jnp.float32),
                pltpu.VMEM((TOGETHER, FIELDS, 16 + 12 * PITCH, LANES), jnp.float32),
                pltpu.VMEM((TOGETHER, FIELDS * 8 * per, LANES), jnp.float32),
            ],
        ),
        out_shape=[
            jax.ShapeDtypeStruct((count, FIELDS * 12 * per, LANES), jnp.int16),
            jax.ShapeDtypeStruct((count, 2, HALF_ROWS, LANES), jnp.float32),
        ],
        compiler_params=pltpu.CompilerParams(vmem_limit_bytes=VMEM_LIMIT),
        name="evolve",
    )(order, *([low, high, right, left] * TOGETHER), *([turn] * TOGETHER), coef, mask)


def factor_body(scale, *refs):
    parts = refs[:-2]
    inverse_ref, factor_ref = refs[-2:]
    blocks = LANES // 8
    lane = lax.broadcasted_iota(jnp.int32, (8, LANES), 1)
    sub = lax.broadcasted_iota(jnp.int32, (8, LANES), 0)
    gram = unpack(parts[0][...], parts[1][...])
    w = [gram[8 * b : 8 * b + 8] for b in range(blocks)]
    full = lambda v: jnp.broadcast_to(v, (8, LANES))
    for b in range(blocks):
        columns = [[full(w[i][:, 8 * b + k : 8 * b + k + 1]) for k in range(8)] for i in range(b, blocks)]
        rows = [full(w[b][k : k + 1, :]) for k in range(8)]
        a = [[full(columns[0][k][i : i + 1, :]) for k in range(i + 1)] for i in range(8)]
        low = [[None] * 8 for _ in range(8)]
        m = [[None] * 8 for _ in range(8)]
        for j in range(8):
            root = lax.rsqrt(a[j][j])
            root = root * (1.5 - 0.5 * (a[j][j] * root) * root)
            m[j][j] = root
            for i in range(j + 1, 8):
                low[i][j] = a[i][j] * root
            for i in range(j + 1, 8):
                for k in range(j + 1, i + 1):
                    a[i][k] = a[i][k] - low[i][j] * low[k][j]
            for k in range(j):
                total = low[j][k] * m[k][k]
                for n in range(k + 1, j):
                    total = total + low[j][n] * m[n][k]
                m[j][k] = -(total * root)
        inside = (lane >= 8 * b) & (lane < 8 * b + 8)
        ones = [jnp.where(inside, jnp.where(lane == 8 * b + k, 1.0, 0.0), rows[k]) for k in range(8)]
        final = [None] * 8
        upper = None
        lower = None
        for i in range(8):
            top = m[i][0] * rows[0]
            final[i] = m[i][0] * ones[0]
            for k in range(1, i + 1):
                top = top + m[i][k] * rows[k]
                final[i] = final[i] + m[i][k] * ones[k]
            upper = top if i == 0 else jnp.where(sub == i, top, upper)
            lower = final[i] if i == 0 else jnp.where(sub == i, final[i], lower)
        inverse_ref[8 * b : 8 * b + 8, :] = jnp.where(lane <= sub + 8 * b, lower * scale, 0.0)
        factor_ref[8 * b : 8 * b + 8, :] = jnp.where(lane >= sub + 8 * b, upper * (1.0 / scale), 0.0)
        if b + 1 < blocks:
            solved = []
            for k in range(8):
                total = m[k][k] * final[k]
                for i in range(k + 1, 8):
                    total = total + m[i][k] * final[i]
                solved.append(total)
            for i in range(b + 1, blocks):
                c = columns[i - b]
                products = [c[k] * solved[k] for k in range(8)]
                while len(products) > 1:
                    products = [products[n] + products[n + 1] for n in range(0, len(products), 2)]
                w[i] = jnp.where(inside, 0.0, w[i]) - products[0]
    factor_ref[...] = factor_ref[...].T


def factorize(parts, scale):
    vmem = pl.BlockSpec(memory_space=pltpu.VMEM)
    shape = jax.ShapeDtypeStruct((LANES, LANES), jnp.float32)
    return pl.pallas_call(
        partial(factor_body, scale),
        in_specs=[vmem] * len(parts),
        out_specs=[vmem, vmem],
        out_shape=[shape, shape],
        name="factorize",
    )(*parts)


def apply_body(inverse_ref, scale_ref, code_ref, out_ref, rows_ref, all_ref):
    per = code_ref.shape[1] // (12 * FIELDS)
    total = 8 * FIELDS * per
    field = pl.program_id(0)
    one, two, three = split(inverse_ref[...].T)
    main = jnp.concatenate([jnp.concatenate([one, two], axis=1)] * 2, axis=0)
    rest = jnp.concatenate([one, three], axis=0)
    for x in range(8):
        line = (field * 8 + x) * per
        late = line >= total // 2
        other = jnp.where(late, line - total // 2, line)
        shift = jnp.where(late, 0, 8)
        for d in range(F):
            high = code_ref[d, pl.ds(pl.multiple_of(line, 16), per), :].astype(jnp.int32)
            low = code_ref[d, pl.ds(pl.multiple_of(total + other, 16), per), :].astype(jnp.int32) + 32768
            low = lax.shift_right_logical(low, jnp.full(low.shape, shift, jnp.int32)) & 255
            value = ((high << 8) + low).astype(jnp.float32) * (scale_ref[d : d + 1, :] * (1.0 / CODE))
            all_ref[x, d * per : (d + 1) * per, :] = value
    for x in range(8):
        a, b, c = split(all_ref[x])
        wide = jnp.dot(jnp.concatenate([a, b], axis=1), main, preferred_element_type=jnp.float32)
        tail = jnp.dot(jnp.concatenate([c, a], axis=1), rest, preferred_element_type=jnp.float32)
        value = wide[:, :LANES] + (wide[:, LANES:] + tail)
        rows_ref[pl.ds(x, LANES, stride=8), :] = value.T
    out_ref[...] = rows_ref[...].reshape(out_ref.shape)


def apply(inverse, scales, columns):
    per = columns.shape[1] // (12 * FIELDS)
    radial = per * F
    vmem = pl.BlockSpec(memory_space=pltpu.VMEM)
    return pl.pallas_call(
        apply_body,
        grid=(FIELDS,),
        in_specs=[vmem, vmem, vmem],
        out_specs=pl.BlockSpec((1, LANES, 1, 8, radial), lambda i: (0, 0, i, 0, 0)),
        out_shape=jax.ShapeDtypeStruct((1, LANES, FIELDS, 8, radial), jnp.float32),
        scratch_shapes=[
            pltpu.VMEM((LANES * 8, radial), jnp.float32),
            pltpu.VMEM((8, radial, LANES), jnp.float32),
        ],
        compiler_params=pltpu.CompilerParams(vmem_limit_bytes=VMEM_LIMIT),
        name="apply",
    )(inverse, scales, columns)


def make_table(indices, slots):
    times = jnp.arange(slots, dtype=jnp.int32)
    phases = indices[:, None] * times[None, :] % slots
    angles = phases.astype(jnp.float32) * (2.0 * math.pi / slots)
    return jnp.stack([jnp.cos(angles), -jnp.sin(angles)], axis=1)


def stencil_body(place_ref, coupling_ref, velocity_ref, right_ref, left_ref, coef_ref, mask_ref):
    radial = velocity_ref.shape[1]
    cells = radial // F + 2
    start = place_ref[0]
    turn = lax.rem(radial + 1 - start, radial)

    def tiles(index, own):
        gap = jnp.zeros((4, radial), jnp.float32)
        other = jnp.concatenate([right_ref[index], gap, left_ref[index]], axis=0)
        return [pltpu.roll(value, turn, 1) for value in (own, other)]

    def put(ref, lead, t, r, value):
        line = 8 + r - 1
        if t == 0:
            ref[lead + (pl.ds(line + 2 * PITCH, 8, stride=PITCH),)] = value
        elif 1 <= r <= cells - 2:
            ref[lead + (pl.ds(line + 10 * PITCH, 2, stride=PITCH),)] = value[0:2]
            ref[lead + (pl.ds(line, 2, stride=PITCH),)] = value[6:8]

    def spread_lanes(index, t, value):
        for r in range(cells):
            put(coef_ref, (index,), t, r, jnp.broadcast_to(value[:, r : r + 1], (8, LANES)))

    centre = 1.0 - STEP_DT * VISCOSITY * (30.0 / 12.0 + 2.0)

    @pl.loop(0, FIELDS * FIELDS)
    def _(index):
        diagonal = jnp.where(lax.rem(index, FIELDS + 1) == 0, centre, 0.0)
        for t, value in enumerate(tiles(index, coupling_ref[index])):
            spread_lanes(index, t, STEP_DT * value + diagonal)

    near_d, near_c = STEP_DT * 8.0 / 12.0, STEP_DT * VISCOSITY * 16.0 / 12.0
    far_d, far_c = STEP_DT / 12.0, STEP_DT * VISCOSITY / 12.0
    for t, speed in enumerate(tiles(FIELDS * FIELDS, velocity_ref[...])):
        spread_lanes(FIELDS * FIELDS, t, near_d * speed + near_c)
        spread_lanes(FIELDS * FIELDS + 1, t, near_c - near_d * speed)
        spread_lanes(FIELDS * FIELDS + 2, t, -far_d * speed - far_c)
        spread_lanes(FIELDS * FIELDS + 3, t, far_d * speed - far_c)
    sub = lax.broadcasted_iota(jnp.int32, (8, LANES), 0)
    sides = jnp.where(sub < HALF, place_ref[2], place_ref[1])
    for r in range(cells):
        here = start - 1 + r
        inside = jnp.where((here >= 0) & (here < radial), 1, 0)
        put(mask_ref, (), 0, r, jnp.full((8, LANES), inside, jnp.int32).astype(jnp.float32))
        put(mask_ref, (), 1, r, (sides * inside).astype(jnp.float32))


def stencil(coupling, velocity, per):
    count = lax.axis_size(SPACE)
    mine = lax.axis_index(SPACE)
    radial = velocity.shape[1]
    up = [(i, i + 1) for i in range(count - 1)]
    down = [(i + 1, i) for i in range(count - 1)]
    coupling = coupling.reshape(FIELDS * FIELDS, 8, radial)
    edges = [jnp.concatenate([coupling[:, s], velocity[None, s]], axis=0) for s in (slice(0, 2), slice(6, 8))]
    right = lax.ppermute(edges[0], SPACE, down)
    left = lax.ppermute(edges[1], SPACE, up)
    place = jnp.stack([lax.axis_index("freq") * per, (mine > 0).astype(jnp.int32), (mine < count - 1).astype(jnp.int32)])
    vmem = pl.BlockSpec(memory_space=pltpu.VMEM)
    return pl.pallas_call(
        stencil_body,
        in_specs=[pl.BlockSpec(memory_space=pltpu.SMEM)] + [vmem] * 4,
        out_specs=[vmem, vmem],
        out_shape=[
            jax.ShapeDtypeStruct((FIELDS * FIELDS + 4, 16 + 12 * PITCH, LANES), jnp.float32),
            jax.ShapeDtypeStruct((16 + 12 * PITCH, LANES), jnp.float32),
        ],
        compiler_params=pltpu.CompilerParams(vmem_limit_bytes=VMEM_LIMIT),
        name="stencil",
    )(place, coupling, velocity, right, left)


def local(sketch, coupling, velocity, freq_index):
    groups = lax.axis_size("freq")
    count = lax.axis_size(SPACE)
    radial = sketch.shape[4]
    per = radial // groups
    mine = lax.axis_index("freq")

    rows = spread(sketch, groups)
    coupling, velocity, rows = lax.optimization_barrier((coupling, velocity, rows))
    rows = lax.all_to_all(rows, "freq", split_axis=0, concat_axis=0, tiled=True)

    parity = freq_index % 2
    waves = make_table(freq_index, NT)[:, :, : NT // 2].reshape(F, 2, 4, 2)
    waves = jnp.repeat(waves, K, axis=3)
    angular = math.pi / NT * STEP_DT * freq_index.astype(jnp.float32)
    sign = jnp.where(jnp.arange(LANES) < K, 1.0, -1.0).astype(jnp.float32)
    turn = jnp.broadcast_to((angular[:, None] * sign)[:, None, :], (F, 8, LANES))
    coef, mask = stencil(coupling, velocity, per)

    rows, coef, mask, turn, waves, parity = lax.optimization_barrier((rows, coef, mask, turn, waves, parity))
    right = lax.ppermute(rows[:, 0], SPACE, [(i + 1, i) for i in range(count - 1)])
    left = lax.ppermute(rows[:, 1], SPACE, [(i, i + 1) for i in range(count - 1)])
    low, high = fourier(parity, rows, rows, waves, (0, 1))
    right, left = fourier(parity, right[:, None], left[:, None], waves, (0, 0))

    columns, grams = evolve(jnp.arange(F, dtype=jnp.int32), low, high, right, left, coef, mask, turn)
    core = lax.axis_index("core")
    grams = grams.reshape(groups * 2, HALF_ROWS, LANES)
    parts = lax.all_to_all(grams, ("freq", "core"), split_axis=0, concat_axis=0, tiled=True)
    gram = jnp.sum(parts, axis=0)
    parts = parts.reshape(groups, 2, HALF_ROWS, LANES)[:, :, K // 2 + 1]
    scales = jnp.where(core == 0, parts[:, 0], parts[:, 1])
    columns, gram = lax.optimization_barrier((columns, gram))
    columns = lax.all_to_all(columns, "freq", split_axis=0, concat_axis=0, tiled=True)
    gram = xor_sum(gram, "chip", (16, 8, 24))
    gram = xor_sum(gram, "chip", (2, 1, 3))
    gram = xor_sum(gram, "chip", (4,))
    other = lax.ppermute(gram, "core", [(0, 1), (1, 0)])
    parts = [jnp.where(core == 0, gram, other), jnp.where(core == 0, other, gram)]
    row_scale = math.sqrt(FIELDS * 8 * count * radial)
    inverse, factor = factorize(parts, row_scale)
    return apply(inverse, scales, columns), factor[None]


def solution(mesh):
    devices = mesh.devices
    split_mesh = jax.sharding.Mesh(
        devices.reshape(devices.shape[0] // 2, 2, devices.shape[1]), ("chip", "core", "freq")
    )
    return jax.shard_map(
        local,
        mesh=split_mesh,
        in_specs=(
            P("freq", None, None, SPACE, None),
            P(None, None, SPACE, None),
            P(SPACE, None),
            P(),
        ),
        out_specs=(P("freq", None, None, SPACE, None), P("freq", None, None)),
        check_vma=False,
    )
```

```python
from functools import partial
import math

import jax
import jax.numpy as jnp
from jax import lax
from jax.experimental import pallas as pl
from jax.experimental.pallas import tpu as pltpu
from jax.sharding import PartitionSpec as P

K = 64
FIELDS = 5
NT = 16
F = 8
STEP_DT = 0.25
VISCOSITY = 0.5
LANES = 2 * K
HALF = 4
SPACE = ("chip", "core")
RH = 2
PITCH = 24
TOGETHER = 4
VMEM_LIMIT = 28 * 1024 * 1024


def swap(value, axis, mask):
    count = lax.axis_size(axis)
    return lax.ppermute(value, axis, [(i, i ^ mask) for i in range(count)])


def quad_sum(value, axis, one, two):
    near, far, both = [swap(value, axis, mask) for mask in (one, two, one ^ two)]
    return (value + near) + (far + both)


def spread_body(sketch_ref, out_ref, rows_ref, turned_ref):
    groups = out_ref.shape[0]
    radial = sketch_ref.shape[4]
    per = radial // groups
    rows_ref[...] = sketch_ref[...].astype(jnp.float32).reshape(LANES * 8, radial)
    edge = jnp.zeros((RH * HALF, LANES), jnp.float32)
    for half in range(2):
        turned_ref[half, 0 : RH * HALF, :] = edge
        turned_ref[half, (radial + RH) * HALF :, :] = edge
    for x in range(8):
        block = rows_ref[pl.ds(x, LANES, stride=8), :]
        turned_ref[x // HALF, pl.ds(RH * HALF + x % HALF, radial, stride=HALF), :] = block.T
    count = (per + 2 * RH) * HALF
    for half in range(2):
        for group in range(groups):
            start = group * per * HALF
            out_ref[group, half] = turned_ref[half, start : start + count, :].astype(jnp.bfloat16)


def spread(sketch, groups):
    radial = sketch.shape[4]
    rows = (radial // groups + 2 * RH) * HALF
    return pl.pallas_call(
        spread_body,
        grid=(FIELDS,),
        in_specs=[pl.BlockSpec((2, K, 1, 8, radial), lambda i: (0, 0, i, 0, 0))],
        out_specs=pl.BlockSpec((groups, 2, rows, LANES), lambda i: (0, 0, i, 0)),
        out_shape=jax.ShapeDtypeStruct((groups, 2, FIELDS * rows, LANES), jnp.bfloat16),
        scratch_shapes=[
            pltpu.VMEM((LANES * 8, radial), jnp.float32),
            pltpu.VMEM((2, (radial + 2 * RH) * HALF, LANES), jnp.float32),
        ],
        compiler_params=pltpu.CompilerParams(vmem_limit_bytes=2 * VMEM_LIMIT),
        name="spread",
    )(sketch)


def fourier_body(parity_ref, table_ref, *refs):
    pair_ref = refs[-1]
    groups = len(refs) // 2
    size = pair_ref.shape[2]
    first = lax.broadcasted_iota(jnp.int32, (8, LANES), 1) < K
    for rows_ref, z_ref in zip(refs[:groups], refs[groups : 2 * groups]):

        @pl.loop(0, rows_ref.shape[2] // size)
        def _(step):
            start = pl.multiple_of(step * size, size)
            for d in range(4):
                a = rows_ref[d, 0, pl.ds(start, size), :].astype(jnp.float32)
                b = rows_ref[d + 4, 0, pl.ds(start, size), :].astype(jnp.float32)
                pair_ref[0, d] = a + b
                pair_ref[1, d] = a - b
            for f in range(F):
                parity = parity_ref[f]
                wave = [[jnp.broadcast_to(table_ref[f, c, d : d + 1], (8, LANES)) for d in range(4)] for c in range(2)]
                for line in range(0, size, 8):
                    p = [pair_ref[parity, d, line : line + 8] for d in range(4)]
                    u = (p[0] * wave[0][0] + p[1] * wave[0][1]) + (p[2] * wave[0][2] + p[3] * wave[0][3])
                    v = (p[0] * wave[1][0] + p[1] * wave[1][1]) + (p[2] * wave[1][2] + p[3] * wave[1][3])
                    z_ref[f, pl.ds(start + line, 8), :] = jnp.where(first, u, v) + pltpu.roll(
                        jnp.where(first, v, u), K, 1
                    )


def fourier(parity, rows, parts, table):
    slots, _, count, _ = rows[0].shape
    size = count // FIELDS
    block = lambda part: pl.BlockSpec((slots, 1, count, LANES), lambda i: (0, part, 0, 0))
    return pl.pallas_call(
        fourier_body,
        grid=(1,),
        in_specs=[pl.BlockSpec(memory_space=pltpu.SMEM), pl.BlockSpec(table.shape, lambda i: (0, 0, 0, 0))]
        + [block(part) for part in parts],
        out_specs=[pl.BlockSpec((F, count, LANES), lambda i: (0, 0, 0))] * len(rows),
        out_shape=[jax.ShapeDtypeStruct((F, count, LANES), jnp.float32)] * len(rows),
        scratch_shapes=[pltpu.VMEM((2, 4, size, LANES), jnp.float32)],
        compiler_params=pltpu.CompilerParams(vmem_limit_bytes=VMEM_LIMIT),
        name="fourier",
    )(parity, table, *rows)


def split(value):
    one = value.astype(jnp.bfloat16)
    rest = value - one.astype(jnp.float32)
    two = rest.astype(jnp.bfloat16)
    three = (rest - two.astype(jnp.float32)).astype(jnp.bfloat16)
    return one, two, three


CODE = 8388000.0


def encode(block, scale):
    number = jnp.round(block * (CODE / scale)).astype(jnp.int32)
    half = block.shape[0] // 2
    low = number & 255
    both = (low[:half] << 8) + low[half:] - 32768
    return (number >> 8).astype(jnp.int16), both.astype(jnp.int16)


HALF_ROWS = K // 2 + 8


def pack(gram, scale, ref, n):
    line = lax.broadcasted_iota(jnp.int32, (K, LANES), 0)
    lane = lax.broadcasted_iota(jnp.int32, (K, LANES), 1)
    last = pltpu.roll(gram[K:], K, 1)
    both = jnp.where(lane >= line, gram[:K], last)
    diagonal = jnp.sum(jnp.where(lane == line, last, 0.0), axis=0, keepdims=True)
    sub = lax.broadcasted_iota(jnp.int32, (8, LANES), 0)
    for h in range(2):
        ref[n, h, 0 : K // 2, :] = both[h * K // 2 : (h + 1) * K // 2]
        ref[n, h, K // 2 :, :] = jnp.where(sub == 0, diagonal, scale)


def unpack(one, two):
    line = lax.broadcasted_iota(jnp.int32, (K, LANES), 0)
    lane = lax.broadcasted_iota(jnp.int32, (K, LANES), 1)
    top = jnp.concatenate([one[: K // 2], two[: K // 2]], axis=0)
    last = pltpu.roll(jnp.where(lane < line, top, 0.0), K, 1)
    half = jnp.concatenate([jnp.where(lane >= line, top, 0.0), last], axis=0)
    diagonal = pltpu.roll(jnp.broadcast_to(one[K // 2 : K // 2 + 1], (8, LANES)), K, 1)
    diagonal = jnp.concatenate([top] + [diagonal] * (K // 8), axis=0)
    line = lax.broadcasted_iota(jnp.int32, (LANES, LANES), 0)
    lane = lax.broadcasted_iota(jnp.int32, (LANES, LANES), 1)
    return jnp.where(line == lane, diagonal, half + half.T)


def evolve_body(order_ref, *refs):
    layers, turn_refs = refs[: 4 * TOGETHER], refs[4 * TOGETHER : 5 * TOGETHER]
    coef_ref, mask_ref, code_ref, gram_ref, z_ref, s_ref, out_ref = refs[5 * TOGETHER :]
    per = out_ref.shape[1] // (8 * FIELDS)
    wide = per + 2 * RH

    for n in range(TOGETHER):
        low, high, inner, outer = layers[4 * n : 4 * n + 4]
        core = order_ref[F]

        @pl.loop(0, FIELDS)
        def _(field):
            for group, ref in ((1, low), (2, high), (3 - 3 * core, inner), (3 * core, outer)):
                for x in range(HALF):
                    source = field * wide * HALF + x
                    target = pl.multiple_of(8 + PITCH * (group * HALF + x), 8)
                    z_ref[n, field, pl.ds(target - RH, RH), :] = ref[0, pl.ds(source, RH, stride=HALF), :]
                    for r in range(0, per, 8):
                        z_ref[n, field, pl.ds(target + r, 8), :] = ref[
                            0, pl.ds(source + (r + RH) * HALF, 8, stride=HALF), :
                        ]
                    z_ref[n, field, pl.ds(target + per, RH), :] = ref[
                        0, pl.ds(source + (per + RH) * HALF, RH, stride=HALF), :
                    ]

    turns = [ref[0] for ref in turn_refs]

    def advance(ref, line, place, store):
        q = [[ref[n, j, pl.ds(line, 8), :] for j in range(FIELDS)] for n in range(TOGETHER)]
        for i in range(FIELDS):
            coupled = [coef_ref[j * FIELDS + i, pl.ds(place, 8), :] for j in range(FIELDS)]
            moves = [coef_ref[FIELDS * FIELDS + m, pl.ds(place, 8), :] for m in range(4)]
            for n in range(TOGETHER):
                value = coupled[0] * q[n][0]
                for j in range(1, FIELDS):
                    value = value + coupled[j] * q[n][j]
                for m, shift in enumerate((1, -1, 2, -2)):
                    value = value + moves[m] * ref[n, i, pl.ds(line + PITCH * shift, 8), :]
                side = ref[n, i, pl.ds(line - 1, 8), :] + ref[n, i, pl.ds(line + 1, 8), :]
                value = value + (STEP_DT * VISCOSITY) * side
                store(n, i, value + turns[n] * pltpu.roll(q[n][i], K, 1))

    def first_step(place):
        mask = mask_ref[pl.ds(place, 8), :]

        def store(n, i, value):
            s_ref[n, i, pl.ds(place, 8), :] = value * mask

        advance(z_ref, pl.multiple_of(place + 2 * PITCH, 8), place, store)

    @pl.loop(0, 12)
    def _(x):
        for r in range(0, per, 8):
            first_step(pl.multiple_of(8 + PITCH * x + r, 8))

    @pl.loop(1, 10)
    def _(x):
        first_step(pl.multiple_of(8 + PITCH * x + per, 8))

    @pl.loop(0, 8)
    def _(x):
        for r in range(0, per, 8):
            line = pl.multiple_of(8 + PITCH * (x + 2) + r, 8)

            def store(n, i, value):
                out_ref[n, pl.ds(pl.multiple_of((i * 8 + x) * per + r, 8), 8), :] = value

            advance(s_ref, line, line, store)

    for n in range(TOGETHER):
        block = out_ref[n]
        one, two, three = split(block)
        pair = jnp.concatenate([one, two], axis=1)
        contract = (((0,), (0,)), ((), ()))
        wide = lax.dot_general(pair, pair, contract, preferred_element_type=jnp.float32)
        thin = lax.dot_general(one, three, contract, preferred_element_type=jnp.float32)
        cross = wide[:LANES, LANES:] + thin
        gram = wide[:LANES, :LANES] + (cross + cross.T + wide[LANES:, LANES:])
        scale = jnp.maximum(jnp.max(jnp.abs(block), axis=0, keepdims=True), 1e-30)
        pack(gram, scale, gram_ref, n)
        count = block.shape[0]
        code_ref[n, 0:count, :], code_ref[n, count : count + count // 2, :] = encode(block, scale)


def evolve(order, low, high, inner, outer, coef, mask, turn):
    count = order.shape[0] - 1
    rows = low.shape[1]
    per = rows // (FIELDS * HALF) - 2 * RH
    whole = lambda shape: pl.BlockSpec(shape, lambda i, order: (0,) * len(shape))
    pick = lambda shape, n: pl.BlockSpec((1,) + shape, lambda i, order: (order[TOGETHER * i + n], 0, 0))
    layers = [pick((rows, LANES), n) for n in range(TOGETHER) for _ in range(4)]
    return pl.pallas_call(
        evolve_body,
        grid_spec=pltpu.PrefetchScalarGridSpec(
            num_scalar_prefetch=1,
            grid=(count // TOGETHER,),
            in_specs=layers
            + [pick((8, LANES), n) for n in range(TOGETHER)]
            + [whole(coef.shape), whole(mask.shape)],
            out_specs=[
                pl.BlockSpec((TOGETHER, FIELDS * 12 * per, LANES), lambda i, order: (i, 0, 0)),
                pl.BlockSpec((TOGETHER, 2, HALF_ROWS, LANES), lambda i, order: (i, 0, 0, 0)),
            ],
            scratch_shapes=[
                pltpu.VMEM((TOGETHER, FIELDS, 16 + 16 * PITCH, LANES), jnp.float32),
                pltpu.VMEM((TOGETHER, FIELDS, 16 + 12 * PITCH, LANES), jnp.float32),
                pltpu.VMEM((TOGETHER, FIELDS * 8 * per, LANES), jnp.float32),
            ],
        ),
        out_shape=[
            jax.ShapeDtypeStruct((count, FIELDS * 12 * per, LANES), jnp.int16),
            jax.ShapeDtypeStruct((count, 2, HALF_ROWS, LANES), jnp.float32),
        ],
        compiler_params=pltpu.CompilerParams(vmem_limit_bytes=VMEM_LIMIT),
        name="evolve",
    )(order, *([low, high, inner, outer] * TOGETHER), *([turn] * TOGETHER), coef, mask)


def factor_body(scale, core_ref, *refs):
    parts = refs[:-2]
    inverse_ref, factor_ref = refs[-2:]
    blocks = LANES // 8
    lane = lax.broadcasted_iota(jnp.int32, (8, LANES), 1)
    sub = lax.broadcasted_iota(jnp.int32, (8, LANES), 0)
    mine, other = parts[0][...] + parts[1][...], parts[2][...] + parts[3][...]
    lower = jnp.full(mine.shape, core_ref[0], jnp.int32) == 0
    gram = unpack(jnp.where(lower, mine, other), jnp.where(lower, other, mine))
    w = [gram[8 * b : 8 * b + 8] for b in range(blocks)]
    full = lambda v: jnp.broadcast_to(v, (8, LANES))
    for b in range(blocks):
        columns = [[full(w[i][:, 8 * b + k : 8 * b + k + 1]) for k in range(8)] for i in range(b, blocks)]
        rows = [full(w[b][k : k + 1, :]) for k in range(8)]
        a = [[full(columns[0][k][i : i + 1, :]) for k in range(i + 1)] for i in range(8)]
        low = [[None] * 8 for _ in range(8)]
        m = [[None] * 8 for _ in range(8)]
        for j in range(8):
            root = lax.rsqrt(a[j][j])
            root = root * (1.5 - 0.5 * (a[j][j] * root) * root)
            m[j][j] = root
            for i in range(j + 1, 8):
                low[i][j] = a[i][j] * root
            for i in range(j + 1, 8):
                for k in range(j + 1, i + 1):
                    a[i][k] = a[i][k] - low[i][j] * low[k][j]
            for k in range(j):
                total = low[j][k] * m[k][k]
                for n in range(k + 1, j):
                    total = total + low[j][n] * m[n][k]
                m[j][k] = -(total * root)
        inside = (lane >= 8 * b) & (lane < 8 * b + 8)
        ones = [jnp.where(inside, jnp.where(lane == 8 * b + k, 1.0, 0.0), rows[k]) for k in range(8)]
        final = [None] * 8
        upper = None
        lower = None
        for i in range(8):
            top = m[i][0] * rows[0]
            final[i] = m[i][0] * ones[0]
            for k in range(1, i + 1):
                top = top + m[i][k] * rows[k]
                final[i] = final[i] + m[i][k] * ones[k]
            upper = top if i == 0 else jnp.where(sub == i, top, upper)
            lower = final[i] if i == 0 else jnp.where(sub == i, final[i], lower)
        inverse_ref[8 * b : 8 * b + 8, :] = jnp.where(lane <= sub + 8 * b, lower * scale, 0.0)
        factor_ref[8 * b : 8 * b + 8, :] = jnp.where(lane >= sub + 8 * b, upper * (1.0 / scale), 0.0)
        if b + 1 < blocks:
            solved = []
            for k in range(8):
                total = m[k][k] * final[k]
                for i in range(k + 1, 8):
                    total = total + m[i][k] * final[i]
                solved.append(total)
            for i in range(b + 1, blocks):
                c = columns[i - b]
                products = [c[k] * solved[k] for k in range(8)]
                while len(products) > 1:
                    products = [products[n] + products[n + 1] for n in range(0, len(products), 2)]
                w[i] = jnp.where(inside, 0.0, w[i]) - products[0]
    factor_ref[...] = factor_ref[...].T


def factorize(core, parts, scale):
    vmem = pl.BlockSpec(memory_space=pltpu.VMEM)
    shape = jax.ShapeDtypeStruct((LANES, LANES), jnp.float32)
    return pl.pallas_call(
        partial(factor_body, scale),
        in_specs=[pl.BlockSpec(memory_space=pltpu.SMEM)] + [vmem] * len(parts),
        out_specs=[vmem, vmem],
        out_shape=[shape, shape],
        name="factorize",
    )(core[None], *parts)


def apply_body(inverse_ref, scale_ref, code_ref, out_ref, rows_ref, all_ref):
    per = code_ref.shape[1] // (12 * FIELDS)
    total = 8 * FIELDS * per
    field = pl.program_id(0)
    one, two, three = split(inverse_ref[...].T)
    main = jnp.concatenate([jnp.concatenate([one, two], axis=1)] * 2, axis=0)
    rest = jnp.concatenate([one, three], axis=0)
    for x in range(8):
        line = (field * 8 + x) * per
        late = line >= total // 2
        other = jnp.where(late, line - total // 2, line)
        shift = jnp.where(late, 0, 8)
        for d in range(F):
            high = code_ref[d, pl.ds(pl.multiple_of(line, 16), per), :].astype(jnp.int32)
            low = code_ref[d, pl.ds(pl.multiple_of(total + other, 16), per), :].astype(jnp.int32) + 32768
            low = lax.shift_right_logical(low, jnp.full(low.shape, shift, jnp.int32)) & 255
            value = ((high << 8) + low).astype(jnp.float32) * (scale_ref[d : d + 1, :] * (1.0 / CODE))
            all_ref[x, d * per : (d + 1) * per, :] = value
    for x in range(8):
        a, b, c = split(all_ref[x])
        wide = jnp.dot(jnp.concatenate([a, b], axis=1), main, preferred_element_type=jnp.float32)
        tail = jnp.dot(jnp.concatenate([c, a], axis=1), rest, preferred_element_type=jnp.float32)
        value = wide[:, :LANES] + (wide[:, LANES:] + tail)
        rows_ref[pl.ds(x, LANES, stride=8), :] = value.T
    out_ref[...] = rows_ref[...].reshape(out_ref.shape)


def apply(inverse, scales, columns):
    per = columns.shape[1] // (12 * FIELDS)
    radial = per * F
    vmem = pl.BlockSpec(memory_space=pltpu.VMEM)
    return pl.pallas_call(
        apply_body,
        grid=(FIELDS,),
        in_specs=[vmem, vmem, vmem],
        out_specs=pl.BlockSpec((1, LANES, 1, 8, radial), lambda i: (0, 0, i, 0, 0)),
        out_shape=jax.ShapeDtypeStruct((1, LANES, FIELDS, 8, radial), jnp.float32),
        scratch_shapes=[
            pltpu.VMEM((LANES * 8, radial), jnp.float32),
            pltpu.VMEM((8, radial, LANES), jnp.float32),
        ],
        compiler_params=pltpu.CompilerParams(vmem_limit_bytes=VMEM_LIMIT),
        name="apply",
    )(inverse, scales, columns)


def make_table(indices, slots):
    times = jnp.arange(slots, dtype=jnp.int32)
    phases = indices[:, None] * times[None, :] % slots
    angles = phases.astype(jnp.float32) * (2.0 * math.pi / slots)
    return jnp.stack([jnp.cos(angles), -jnp.sin(angles)], axis=1)


def stencil_body(place_ref, coupling_ref, velocity_ref, right_ref, left_ref, coef_ref, mask_ref):
    radial = velocity_ref.shape[1]
    cells = radial // F + 2
    start = place_ref[0]
    turn = lax.rem(radial + 1 - start, radial)

    def tiles(index, own):
        gap = jnp.zeros((4, radial), jnp.float32)
        other = jnp.concatenate([right_ref[index], gap, left_ref[index]], axis=0)
        return [pltpu.roll(value, turn, 1) for value in (own, other)]

    def put(ref, lead, t, r, value):
        line = 8 + r - 1
        if t == 0:
            ref[lead + (pl.ds(line + 2 * PITCH, 8, stride=PITCH),)] = value
        elif 1 <= r <= cells - 2:
            ref[lead + (pl.ds(line + 10 * PITCH, 2, stride=PITCH),)] = value[0:2]
            ref[lead + (pl.ds(line, 2, stride=PITCH),)] = value[6:8]

    def spread_lanes(index, t, value):
        for r in range(cells):
            put(coef_ref, (index,), t, r, jnp.broadcast_to(value[:, r : r + 1], (8, LANES)))

    centre = 1.0 - STEP_DT * VISCOSITY * (30.0 / 12.0 + 2.0)

    @pl.loop(0, FIELDS * FIELDS)
    def _(index):
        diagonal = jnp.where(lax.rem(index, FIELDS + 1) == 0, centre, 0.0)
        for t, value in enumerate(tiles(index, coupling_ref[index])):
            spread_lanes(index, t, STEP_DT * value + diagonal)

    near_d, near_c = STEP_DT * 8.0 / 12.0, STEP_DT * VISCOSITY * 16.0 / 12.0
    far_d, far_c = STEP_DT / 12.0, STEP_DT * VISCOSITY / 12.0
    for t, speed in enumerate(tiles(FIELDS * FIELDS, velocity_ref[...])):
        spread_lanes(FIELDS * FIELDS, t, near_d * speed + near_c)
        spread_lanes(FIELDS * FIELDS + 1, t, near_c - near_d * speed)
        spread_lanes(FIELDS * FIELDS + 2, t, -far_d * speed - far_c)
        spread_lanes(FIELDS * FIELDS + 3, t, far_d * speed - far_c)
    sub = lax.broadcasted_iota(jnp.int32, (8, LANES), 0)
    sides = jnp.where(sub < HALF, place_ref[2], place_ref[1])
    for r in range(cells):
        here = start - 1 + r
        inside = jnp.where((here >= 0) & (here < radial), 1, 0)
        put(mask_ref, (), 0, r, jnp.full((8, LANES), inside, jnp.int32).astype(jnp.float32))
        put(mask_ref, (), 1, r, (sides * inside).astype(jnp.float32))


def stencil(coupling, velocity, per):
    count = lax.axis_size(SPACE)
    mine = lax.axis_index(SPACE)
    radial = velocity.shape[1]
    up = [(i, i + 1) for i in range(count - 1)]
    down = [(i + 1, i) for i in range(count - 1)]
    coupling = coupling.reshape(FIELDS * FIELDS, 8, radial)
    edges = [jnp.concatenate([coupling[:, s], velocity[None, s]], axis=0) for s in (slice(0, 2), slice(6, 8))]
    right = lax.ppermute(edges[0], SPACE, down)
    left = lax.ppermute(edges[1], SPACE, up)
    place = jnp.stack([lax.axis_index("freq") * per, (mine > 0).astype(jnp.int32), (mine < count - 1).astype(jnp.int32)])
    vmem = pl.BlockSpec(memory_space=pltpu.VMEM)
    return pl.pallas_call(
        stencil_body,
        in_specs=[pl.BlockSpec(memory_space=pltpu.SMEM)] + [vmem] * 4,
        out_specs=[vmem, vmem],
        out_shape=[
            jax.ShapeDtypeStruct((FIELDS * FIELDS + 4, 16 + 12 * PITCH, LANES), jnp.float32),
            jax.ShapeDtypeStruct((16 + 12 * PITCH, LANES), jnp.float32),
        ],
        compiler_params=pltpu.CompilerParams(vmem_limit_bytes=VMEM_LIMIT),
        name="stencil",
    )(place, coupling, velocity, right, left)


def local(sketch, coupling, velocity, freq_index):
    groups = lax.axis_size("freq")
    count = lax.axis_size(SPACE)
    radial = sketch.shape[4]
    per = radial // groups
    mine = lax.axis_index("freq")

    rows = spread(sketch, groups)
    coupling, velocity, rows = lax.optimization_barrier((coupling, velocity, rows))
    rows = lax.all_to_all(rows, "freq", split_axis=0, concat_axis=0, tiled=True)

    parity = freq_index % 2
    waves = make_table(freq_index, NT)[:, :, : NT // 2].reshape(F, 2, 4, 2)
    waves = jnp.repeat(waves, K, axis=3)
    angular = math.pi / NT * STEP_DT * freq_index.astype(jnp.float32)
    sign = jnp.where(jnp.arange(LANES) < K, 1.0, -1.0).astype(jnp.float32)
    turn = jnp.broadcast_to((angular[:, None] * sign)[:, None, :], (F, 8, LANES))
    coef, mask = stencil(coupling, velocity, per)

    rows, coef, mask, turn, waves, parity = lax.optimization_barrier((rows, coef, mask, turn, waves, parity))
    core = lax.axis_index("core")
    outer = lax.dynamic_index_in_dim(rows, core, 1, keepdims=False)
    inner = lax.dynamic_index_in_dim(rows, 1 - core, 1, keepdims=False)
    outer = lax.ppermute(outer, SPACE, [(i, i + 1 if i % 2 else i - 1) for i in range(1, count - 1)])
    inner = swap(inner, "core", 1)
    low, high = fourier(parity, [rows, rows], [0, 1], waves)
    (inner,) = fourier(parity, [inner[:, None]], [0], waves)
    (outer,) = fourier(parity, [outer[:, None]], [0], waves)
    order = jnp.concatenate([jnp.arange(F, dtype=jnp.int32), core[None]])

    columns, grams = evolve(order, low, high, inner, outer, coef, mask, turn)
    grams = grams.reshape(groups * 2, HALF_ROWS, LANES)
    parts = lax.all_to_all(grams, ("freq", "core"), split_axis=0, concat_axis=0, tiled=True)
    gram = jnp.sum(parts, axis=0)
    parts = parts.reshape(groups, 2, HALF_ROWS, LANES)[:, :, K // 2 + 1]
    scales = jnp.where(core == 0, parts[:, 0], parts[:, 1])
    columns, gram = lax.optimization_barrier((columns, gram))
    columns = lax.all_to_all(columns, "freq", split_axis=0, concat_axis=0, tiled=True)
    gram = quad_sum(gram, "chip", 16, 8)
    gram = quad_sum(gram, "chip", 2, 1)
    parts = [gram] + [swap(gram, ("chip", "core"), mask) for mask in (8, 1, 9)]
    row_scale = math.sqrt(FIELDS * 8 * count * radial)
    inverse, factor = factorize(core, parts, row_scale)
    return apply(inverse, scales, columns), factor[None]


def solution(mesh):
    devices = mesh.devices
    split_mesh = jax.sharding.Mesh(
        devices.reshape(devices.shape[0] // 2, 2, devices.shape[1]), ("chip", "core", "freq")
    )
    return jax.shard_map(
        local,
        mesh=split_mesh,
        in_specs=(
            P("freq", None, None, SPACE, None),
            P(None, None, SPACE, None),
            P(SPACE, None),
            P(),
        ),
        out_specs=(P("freq", None, None, SPACE, None), P("freq", None, None)),
        check_vma=False,
    )
```

```python
from functools import partial
import math

import jax
import jax.numpy as jnp
from jax import lax
from jax.experimental import pallas as pl
from jax.experimental.pallas import tpu as pltpu
from jax.sharding import PartitionSpec as P

K = 64
FIELDS = 5
NT = 16
F = 8
STEP_DT = 0.25
VISCOSITY = 0.5
LANES = 2 * K
HALF = 4
SPACE = ("chip", "core")
RH = 2
PITCH = 24
TOGETHER = 4
VMEM_LIMIT = 28 * 1024 * 1024


def swap(value, axis, mask):
    count = lax.axis_size(axis)
    return lax.ppermute(value, axis, [(i, i ^ mask) for i in range(count)])


def quad_sum(value, axis, one, two):
    near, far, both = [swap(value, axis, mask) for mask in (one, two, one ^ two)]
    return (value + near) + (far + both)


def spread_body(sketch_ref, out_ref, rows_ref, turned_ref):
    groups = out_ref.shape[0]
    radial = sketch_ref.shape[4]
    per = radial // groups
    rows_ref[...] = sketch_ref[...].astype(jnp.float32).reshape(LANES * 8, radial)
    edge = jnp.zeros((RH * HALF, LANES), jnp.float32)
    for half in range(2):
        turned_ref[half, 0 : RH * HALF, :] = edge
        turned_ref[half, (radial + RH) * HALF :, :] = edge
    for x in range(8):
        block = rows_ref[pl.ds(x, LANES, stride=8), :]
        turned_ref[x // HALF, pl.ds(RH * HALF + x % HALF, radial, stride=HALF), :] = block.T
    count = (per + 2 * RH) * HALF
    for half in range(2):
        for group in range(groups):
            start = group * per * HALF
            out_ref[group, half] = turned_ref[half, start : start + count, :].astype(jnp.bfloat16)


def spread(sketch, groups):
    radial = sketch.shape[4]
    rows = (radial // groups + 2 * RH) * HALF
    return pl.pallas_call(
        spread_body,
        grid=(FIELDS,),
        in_specs=[pl.BlockSpec((2, K, 1, 8, radial), lambda i: (0, 0, i, 0, 0))],
        out_specs=pl.BlockSpec((groups, 2, rows, LANES), lambda i: (0, 0, i, 0)),
        out_shape=jax.ShapeDtypeStruct((groups, 2, FIELDS * rows, LANES), jnp.bfloat16),
        scratch_shapes=[
            pltpu.VMEM((LANES * 8, radial), jnp.float32),
            pltpu.VMEM((2, (radial + 2 * RH) * HALF, LANES), jnp.float32),
        ],
        compiler_params=pltpu.CompilerParams(vmem_limit_bytes=2 * VMEM_LIMIT),
        name="spread",
    )(sketch)


def fourier_body(parity_ref, table_ref, *refs):
    pair_ref = refs[-1]
    groups = len(refs) // 2
    size = pair_ref.shape[2]
    first = lax.broadcasted_iota(jnp.int32, (8, LANES), 1) < K
    for rows_ref, z_ref in zip(refs[:groups], refs[groups : 2 * groups]):

        @pl.loop(0, rows_ref.shape[2] // size)
        def _(step):
            start = pl.multiple_of(step * size, size)
            for d in range(4):
                a = rows_ref[d, 0, pl.ds(start, size), :].astype(jnp.float32)
                b = rows_ref[d + 4, 0, pl.ds(start, size), :].astype(jnp.float32)
                pair_ref[0, d] = a + b
                pair_ref[1, d] = a - b
            for f in range(F):
                parity = parity_ref[f]
                wave = [[jnp.broadcast_to(table_ref[f, c, d : d + 1], (8, LANES)) for d in range(4)] for c in range(2)]
                for line in range(0, size, 8):
                    p = [pair_ref[parity, d, line : line + 8] for d in range(4)]
                    u = (p[0] * wave[0][0] + p[1] * wave[0][1]) + (p[2] * wave[0][2] + p[3] * wave[0][3])
                    v = (p[0] * wave[1][0] + p[1] * wave[1][1]) + (p[2] * wave[1][2] + p[3] * wave[1][3])
                    z_ref[f, pl.ds(start + line, 8), :] = jnp.where(first, u, v) + pltpu.roll(
                        jnp.where(first, v, u), K, 1
                    )


def fourier(parity, rows, parts, table):
    slots, _, count, _ = rows[0].shape
    size = count // FIELDS
    block = lambda part: pl.BlockSpec((slots, 1, count, LANES), lambda i: (0, part, 0, 0))
    return pl.pallas_call(
        fourier_body,
        grid=(1,),
        in_specs=[pl.BlockSpec(memory_space=pltpu.SMEM), pl.BlockSpec(table.shape, lambda i: (0, 0, 0, 0))]
        + [block(part) for part in parts],
        out_specs=[pl.BlockSpec((F, count, LANES), lambda i: (0, 0, 0))] * len(rows),
        out_shape=[jax.ShapeDtypeStruct((F, count, LANES), jnp.float32)] * len(rows),
        scratch_shapes=[pltpu.VMEM((2, 4, size, LANES), jnp.float32)],
        compiler_params=pltpu.CompilerParams(vmem_limit_bytes=VMEM_LIMIT),
        name="fourier",
    )(parity, table, *rows)


def split(value):
    one = value.astype(jnp.bfloat16)
    rest = value - one.astype(jnp.float32)
    two = rest.astype(jnp.bfloat16)
    three = (rest - two.astype(jnp.float32)).astype(jnp.bfloat16)
    return one, two, three


CODE = 524200.0


def encode(block, scale, ref, n):
    total = block.shape[0]
    size = total // FIELDS
    part = size // 4
    for i in range(FIELDS):
        number = jnp.round(block[i * size : (i + 1) * size] * (CODE / scale)).astype(jnp.int32)
        ref[n, i * size : (i + 1) * size, :] = (number >> 4).astype(jnp.int16)
        low = number & 15
        both = (low[:part] << 12) + (low[part : 2 * part] << 8)
        both = both + (low[2 * part : 3 * part] << 4) + low[3 * part :] - 32768
        ref[n, total + i * part : total + (i + 1) * part, :] = both.astype(jnp.int16)


HALF_ROWS = K // 2 + 8


def pack(gram, scale, ref, n):
    line = lax.broadcasted_iota(jnp.int32, (K, LANES), 0)
    lane = lax.broadcasted_iota(jnp.int32, (K, LANES), 1)
    last = pltpu.roll(gram[K:], K, 1)
    both = jnp.where(lane >= line, gram[:K], last)
    diagonal = jnp.sum(jnp.where(lane == line, last, 0.0), axis=0, keepdims=True)
    sub = lax.broadcasted_iota(jnp.int32, (8, LANES), 0)
    for h in range(2):
        ref[n, h, 0 : K // 2, :] = both[h * K // 2 : (h + 1) * K // 2]
        ref[n, h, K // 2 :, :] = jnp.where(sub == 0, diagonal, scale)


def unpack(one, two):
    line = lax.broadcasted_iota(jnp.int32, (K, LANES), 0)
    lane = lax.broadcasted_iota(jnp.int32, (K, LANES), 1)
    top = jnp.concatenate([one[: K // 2], two[: K // 2]], axis=0)
    last = pltpu.roll(jnp.where(lane < line, top, 0.0), K, 1)
    half = jnp.concatenate([jnp.where(lane >= line, top, 0.0), last], axis=0)
    diagonal = pltpu.roll(jnp.broadcast_to(one[K // 2 : K // 2 + 1], (8, LANES)), K, 1)
    diagonal = jnp.concatenate([top] + [diagonal] * (K // 8), axis=0)
    line = lax.broadcasted_iota(jnp.int32, (LANES, LANES), 0)
    lane = lax.broadcasted_iota(jnp.int32, (LANES, LANES), 1)
    return jnp.where(line == lane, diagonal, half + half.T)


def evolve_body(order_ref, *refs):
    layers, turn_refs = refs[: 4 * TOGETHER], refs[4 * TOGETHER : 5 * TOGETHER]
    coef_ref, mask_ref, sent_ref, gram_ref, z_ref, s_ref, out_ref, code_ref, sems = refs[5 * TOGETHER :]
    per = out_ref.shape[1] // (8 * FIELDS)
    wide = per + 2 * RH

    for n in range(TOGETHER):
        low, high, inner, outer = layers[4 * n : 4 * n + 4]
        core = order_ref[F]

        @pl.loop(0, FIELDS)
        def _(field):
            for group, ref in ((1, low), (2, high), (3 - 3 * core, inner), (3 * core, outer)):
                for x in range(HALF):
                    source = field * wide * HALF + x
                    target = pl.multiple_of(8 + PITCH * (group * HALF + x), 8)
                    z_ref[n, field, pl.ds(target - RH, RH), :] = ref[0, pl.ds(source, RH, stride=HALF), :]
                    for r in range(0, per, 8):
                        z_ref[n, field, pl.ds(target + r, 8), :] = ref[
                            0, pl.ds(source + (r + RH) * HALF, 8, stride=HALF), :
                        ]
                    z_ref[n, field, pl.ds(target + per, RH), :] = ref[
                        0, pl.ds(source + (per + RH) * HALF, RH, stride=HALF), :
                    ]

    turns = [ref[0] for ref in turn_refs]

    def advance(ref, line, place, store):
        q = [[ref[n, j, pl.ds(line, 8), :] for j in range(FIELDS)] for n in range(TOGETHER)]
        for i in range(FIELDS):
            coupled = [coef_ref[j * FIELDS + i, pl.ds(place, 8), :] for j in range(FIELDS)]
            moves = [coef_ref[FIELDS * FIELDS + m, pl.ds(place, 8), :] for m in range(4)]
            for n in range(TOGETHER):
                value = coupled[0] * q[n][0]
                for j in range(1, FIELDS):
                    value = value + coupled[j] * q[n][j]
                for m, shift in enumerate((1, -1, 2, -2)):
                    value = value + moves[m] * ref[n, i, pl.ds(line + PITCH * shift, 8), :]
                side = ref[n, i, pl.ds(line - 1, 8), :] + ref[n, i, pl.ds(line + 1, 8), :]
                value = value + (STEP_DT * VISCOSITY) * side
                store(n, i, value + turns[n] * pltpu.roll(q[n][i], K, 1))

    def first_step(place):
        mask = mask_ref[pl.ds(place, 8), :]

        def store(n, i, value):
            s_ref[n, i, pl.ds(place, 8), :] = value * mask

        advance(z_ref, pl.multiple_of(place + 2 * PITCH, 8), place, store)

    @pl.loop(0, 12)
    def _(x):
        for r in range(0, per, 8):
            first_step(pl.multiple_of(8 + PITCH * x + r, 8))

    @pl.loop(1, 10)
    def _(x):
        first_step(pl.multiple_of(8 + PITCH * x + per, 8))

    @pl.loop(0, 8)
    def _(x):
        for r in range(0, per, 8):
            line = pl.multiple_of(8 + PITCH * (x + 2) + r, 8)

            def store(n, i, value):
                out_ref[n, pl.ds(pl.multiple_of((i * 8 + x) * per + r, 8), 8), :] = value

            advance(s_ref, line, line, store)

    copies = []
    for n in range(TOGETHER):
        block = out_ref[n]
        one, two, three = split(block)
        pair = jnp.concatenate([one, two], axis=1)
        contract = (((0,), (0,)), ((), ()))
        wide = lax.dot_general(pair, pair, contract, preferred_element_type=jnp.float32)
        thin = lax.dot_general(one, three, contract, preferred_element_type=jnp.float32)
        cross = wide[:LANES, LANES:] + thin
        gram = wide[:LANES, :LANES] + (cross + cross.T + wide[LANES:, LANES:])
        scale = jnp.maximum(jnp.max(jnp.abs(block), axis=0, keepdims=True), 1e-30)
        pack(gram, scale, gram_ref, n)
        encode(block, scale, code_ref, n)
        copies.append(pltpu.make_async_copy(code_ref.at[n], sent_ref.at[pl.program_id(0) * TOGETHER + n], sems.at[n]))
        copies[n].start()
    for copy in copies:
        copy.wait()


def evolve(order, low, high, inner, outer, coef, mask, turn):
    count = order.shape[0] - 1
    rows = low.shape[1]
    per = rows // (FIELDS * HALF) - 2 * RH
    whole = lambda shape: pl.BlockSpec(shape, lambda i, order: (0,) * len(shape))
    pick = lambda shape, n: pl.BlockSpec((1,) + shape, lambda i, order: (order[TOGETHER * i + n], 0, 0))
    layers = [pick((rows, LANES), n) for n in range(TOGETHER) for _ in range(4)]
    return pl.pallas_call(
        evolve_body,
        grid_spec=pltpu.PrefetchScalarGridSpec(
            num_scalar_prefetch=1,
            grid=(count // TOGETHER,),
            in_specs=layers
            + [pick((8, LANES), n) for n in range(TOGETHER)]
            + [whole(coef.shape), whole(mask.shape)],
            out_specs=[
                pl.BlockSpec(memory_space=pltpu.HBM),
                pl.BlockSpec((TOGETHER, 2, HALF_ROWS, LANES), lambda i, order: (i, 0, 0, 0)),
            ],
            scratch_shapes=[
                pltpu.VMEM((TOGETHER, FIELDS, 16 + 16 * PITCH, LANES), jnp.float32),
                pltpu.VMEM((TOGETHER, FIELDS, 16 + 12 * PITCH, LANES), jnp.float32),
                pltpu.VMEM((TOGETHER, FIELDS * 8 * per, LANES), jnp.float32),
                pltpu.VMEM((TOGETHER, FIELDS * 10 * per, LANES), jnp.int16),
                pltpu.SemaphoreType.DMA((TOGETHER,)),
            ],
        ),
        out_shape=[
            jax.ShapeDtypeStruct((count, FIELDS * 10 * per, LANES), jnp.int16),
            jax.ShapeDtypeStruct((count, 2, HALF_ROWS, LANES), jnp.float32),
        ],
        compiler_params=pltpu.CompilerParams(vmem_limit_bytes=VMEM_LIMIT),
        name="evolve",
    )(order, *([low, high, inner, outer] * TOGETHER), *([turn] * TOGETHER), coef, mask)


def factor_body(scale, core_ref, *refs):
    parts = refs[:-2]
    inverse_ref, factor_ref = refs[-2:]
    blocks = LANES // 8
    lane = lax.broadcasted_iota(jnp.int32, (8, LANES), 1)
    sub = lax.broadcasted_iota(jnp.int32, (8, LANES), 0)
    mine, other = parts[0][...], parts[1][...]
    lower = jnp.full(mine.shape, core_ref[0], jnp.int32) == 0
    gram = unpack(jnp.where(lower, mine, other), jnp.where(lower, other, mine))
    w = [gram[8 * b : 8 * b + 8] for b in range(blocks)]
    full = lambda v: jnp.broadcast_to(v, (8, LANES))
    for b in range(blocks):
        columns = [[full(w[i][:, 8 * b + k : 8 * b + k + 1]) for k in range(8)] for i in range(b, blocks)]
        rows = [full(w[b][k : k + 1, :]) for k in range(8)]
        a = [[full(columns[0][k][i : i + 1, :]) for k in range(i + 1)] for i in range(8)]
        low = [[None] * 8 for _ in range(8)]
        m = [[None] * 8 for _ in range(8)]
        for j in range(8):
            root = lax.rsqrt(a[j][j])
            root = root * (1.5 - 0.5 * (a[j][j] * root) * root)
            m[j][j] = root
            for i in range(j + 1, 8):
                low[i][j] = a[i][j] * root
            for i in range(j + 1, 8):
                for k in range(j + 1, i + 1):
                    a[i][k] = a[i][k] - low[i][j] * low[k][j]
            for k in range(j):
                total = low[j][k] * m[k][k]
                for n in range(k + 1, j):
                    total = total + low[j][n] * m[n][k]
                m[j][k] = -(total * root)
        inside = (lane >= 8 * b) & (lane < 8 * b + 8)
        ones = [jnp.where(inside, jnp.where(lane == 8 * b + k, 1.0, 0.0), rows[k]) for k in range(8)]
        final = [None] * 8
        upper = None
        lower = None
        for i in range(8):
            top = m[i][0] * rows[0]
            final[i] = m[i][0] * ones[0]
            for k in range(1, i + 1):
                top = top + m[i][k] * rows[k]
                final[i] = final[i] + m[i][k] * ones[k]
            upper = top if i == 0 else jnp.where(sub == i, top, upper)
            lower = final[i] if i == 0 else jnp.where(sub == i, final[i], lower)
        inverse_ref[8 * b : 8 * b + 8, :] = jnp.where(lane <= sub + 8 * b, lower * scale, 0.0)
        factor_ref[8 * b : 8 * b + 8, :] = jnp.where(lane >= sub + 8 * b, upper * (1.0 / scale), 0.0)
        if b + 1 < blocks:
            solved = []
            for k in range(8):
                total = m[k][k] * final[k]
                for i in range(k + 1, 8):
                    total = total + m[i][k] * final[i]
                solved.append(total)
            for i in range(b + 1, blocks):
                c = columns[i - b]
                products = [c[k] * solved[k] for k in range(8)]
                while len(products) > 1:
                    products = [products[n] + products[n + 1] for n in range(0, len(products), 2)]
                w[i] = jnp.where(inside, 0.0, w[i]) - products[0]
    factor_ref[...] = factor_ref[...].T


def factorize(core, parts, scale):
    vmem = pl.BlockSpec(memory_space=pltpu.VMEM)
    shape = jax.ShapeDtypeStruct((LANES, LANES), jnp.float32)
    return pl.pallas_call(
        partial(factor_body, scale),
        in_specs=[pl.BlockSpec(memory_space=pltpu.SMEM)] + [vmem] * len(parts),
        out_specs=[vmem, vmem],
        out_shape=[shape, shape],
        compiler_params=pltpu.CompilerParams(vmem_limit_bytes=8 * 1024 * 1024),
        name="factorize",
    )(core[None], *parts)


def apply_body(inverse_ref, scale_ref, high_ref, low_ref, out_ref, rows_ref, all_ref):
    per = high_ref.shape[1] // 8
    one, two, three = split(inverse_ref[...].T)
    main = jnp.concatenate([jnp.concatenate([one, two], axis=1)] * 2, axis=0)
    rest = jnp.concatenate([one, three], axis=0)
    for x in range(8):
        shift, half = 12 - 4 * (x // 2), x % 2
        for d in range(F):
            high = high_ref[d, x * per : (x + 1) * per, :].astype(jnp.int32)
            low = low_ref[d, half * per : (half + 1) * per, :].astype(jnp.int32) + 32768
            number = (high << 4) + ((low >> shift) & 15)
            all_ref[x, d * per : (d + 1) * per, :] = number.astype(jnp.float32) * (
                scale_ref[d : d + 1, :] * (1.0 / CODE)
            )
    for x in range(8):
        a, b, c = split(all_ref[x])
        wide = jnp.dot(jnp.concatenate([a, b], axis=1), main, preferred_element_type=jnp.float32)
        tail = jnp.dot(jnp.concatenate([c, a], axis=1), rest, preferred_element_type=jnp.float32)
        value = wide[:, :LANES] + (wide[:, LANES:] + tail)
        rows_ref[pl.ds(x, LANES, stride=8), :] = value.T
    out_ref[...] = rows_ref[...].reshape(out_ref.shape)


def apply(inverse, scales, columns):
    per = columns.shape[1] // (10 * FIELDS)
    radial = per * F
    first_low = 8 * FIELDS * per // (2 * per)
    vmem = pl.BlockSpec(memory_space=pltpu.VMEM)
    return pl.pallas_call(
        apply_body,
        grid=(FIELDS,),
        in_specs=[
            vmem,
            vmem,
            pl.BlockSpec((F, 8 * per, LANES), lambda i: (0, i, 0)),
            pl.BlockSpec((F, 2 * per, LANES), lambda i: (0, first_low + i, 0)),
        ],
        out_specs=pl.BlockSpec((1, LANES, 1, 8, radial), lambda i: (0, 0, i, 0, 0)),
        out_shape=jax.ShapeDtypeStruct((1, LANES, FIELDS, 8, radial), jnp.float32),
        scratch_shapes=[
            pltpu.VMEM((LANES * 8, radial), jnp.float32),
            pltpu.VMEM((8, radial, LANES), jnp.float32),
        ],
        compiler_params=pltpu.CompilerParams(vmem_limit_bytes=VMEM_LIMIT),
        name="apply",
    )(inverse, scales, columns, columns)


def make_table(indices, slots):
    times = jnp.arange(slots, dtype=jnp.int32)
    phases = indices[:, None] * times[None, :] % slots
    angles = phases.astype(jnp.float32) * (2.0 * math.pi / slots)
    return jnp.stack([jnp.cos(angles), -jnp.sin(angles)], axis=1)


def stencil_body(place_ref, coupling_ref, velocity_ref, right_ref, left_ref, coef_ref, mask_ref):
    radial = velocity_ref.shape[1]
    cells = radial // F + 2
    start = place_ref[0]
    turn = lax.rem(radial + 1 - start, radial)

    def tiles(index, own):
        gap = jnp.zeros((4, radial), jnp.float32)
        other = jnp.concatenate([right_ref[index], gap, left_ref[index]], axis=0)
        return [pltpu.roll(value, turn, 1) for value in (own, other)]

    def put(ref, lead, t, r, value):
        line = 8 + r - 1
        if t == 0:
            ref[lead + (pl.ds(line + 2 * PITCH, 8, stride=PITCH),)] = value
        elif 1 <= r <= cells - 2:
            ref[lead + (pl.ds(line + 10 * PITCH, 2, stride=PITCH),)] = value[0:2]
            ref[lead + (pl.ds(line, 2, stride=PITCH),)] = value[6:8]

    def spread_lanes(index, t, value):
        for r in range(cells):
            put(coef_ref, (index,), t, r, jnp.broadcast_to(value[:, r : r + 1], (8, LANES)))

    centre = 1.0 - STEP_DT * VISCOSITY * (30.0 / 12.0 + 2.0)

    @pl.loop(0, FIELDS * FIELDS)
    def _(index):
        diagonal = jnp.where(lax.rem(index, FIELDS + 1) == 0, centre, 0.0)
        for t, value in enumerate(tiles(index, coupling_ref[index])):
            spread_lanes(index, t, STEP_DT * value + diagonal)

    near_d, near_c = STEP_DT * 8.0 / 12.0, STEP_DT * VISCOSITY * 16.0 / 12.0
    far_d, far_c = STEP_DT / 12.0, STEP_DT * VISCOSITY / 12.0
    for t, speed in enumerate(tiles(FIELDS * FIELDS, velocity_ref[...])):
        spread_lanes(FIELDS * FIELDS, t, near_d * speed + near_c)
        spread_lanes(FIELDS * FIELDS + 1, t, near_c - near_d * speed)
        spread_lanes(FIELDS * FIELDS + 2, t, -far_d * speed - far_c)
        spread_lanes(FIELDS * FIELDS + 3, t, far_d * speed - far_c)
    sub = lax.broadcasted_iota(jnp.int32, (8, LANES), 0)
    sides = jnp.where(sub < HALF, place_ref[2], place_ref[1])
    for r in range(cells):
        here = start - 1 + r
        inside = jnp.where((here >= 0) & (here < radial), 1, 0)
        put(mask_ref, (), 0, r, jnp.full((8, LANES), inside, jnp.int32).astype(jnp.float32))
        put(mask_ref, (), 1, r, (sides * inside).astype(jnp.float32))


def stencil(coupling, velocity, per):
    count = lax.axis_size(SPACE)
    mine = lax.axis_index(SPACE)
    radial = velocity.shape[1]
    up = [(i, i + 1) for i in range(count - 1)]
    down = [(i + 1, i) for i in range(count - 1)]
    coupling = coupling.reshape(FIELDS * FIELDS, 8, radial)
    edges = [jnp.concatenate([coupling[:, s], velocity[None, s]], axis=0) for s in (slice(0, 2), slice(6, 8))]
    right = lax.ppermute(edges[0], SPACE, down)
    left = lax.ppermute(edges[1], SPACE, up)
    place = jnp.stack([lax.axis_index("freq") * per, (mine > 0).astype(jnp.int32), (mine < count - 1).astype(jnp.int32)])
    vmem = pl.BlockSpec(memory_space=pltpu.VMEM)
    return pl.pallas_call(
        stencil_body,
        in_specs=[pl.BlockSpec(memory_space=pltpu.SMEM)] + [vmem] * 4,
        out_specs=[vmem, vmem],
        out_shape=[
            jax.ShapeDtypeStruct((FIELDS * FIELDS + 4, 16 + 12 * PITCH, LANES), jnp.float32),
            jax.ShapeDtypeStruct((16 + 12 * PITCH, LANES), jnp.float32),
        ],
        compiler_params=pltpu.CompilerParams(vmem_limit_bytes=VMEM_LIMIT),
        name="stencil",
    )(place, coupling, velocity, right, left)


def local(sketch, coupling, velocity, freq_index):
    groups = lax.axis_size("freq")
    count = lax.axis_size(SPACE)
    radial = sketch.shape[4]
    per = radial // groups
    mine = lax.axis_index("freq")

    rows = spread(sketch, groups)
    coupling, velocity, rows = lax.optimization_barrier((coupling, velocity, rows))
    rows = lax.all_to_all(rows, "freq", split_axis=0, concat_axis=0, tiled=True)

    parity = freq_index % 2
    waves = make_table(freq_index, NT)[:, :, : NT // 2].reshape(F, 2, 4, 2)
    waves = jnp.repeat(waves, K, axis=3)
    angular = math.pi / NT * STEP_DT * freq_index.astype(jnp.float32)
    sign = jnp.where(jnp.arange(LANES) < K, 1.0, -1.0).astype(jnp.float32)
    turn = jnp.broadcast_to((angular[:, None] * sign)[:, None, :], (F, 8, LANES))
    coef, mask = stencil(coupling, velocity, per)

    rows, coef, mask, turn, waves, parity = lax.optimization_barrier((rows, coef, mask, turn, waves, parity))
    core = lax.axis_index("core")
    outer = lax.dynamic_index_in_dim(rows, core, 1, keepdims=False)
    inner = lax.dynamic_index_in_dim(rows, 1 - core, 1, keepdims=False)
    outer = lax.ppermute(outer, SPACE, [(i, i + 1 if i % 2 else i - 1) for i in range(1, count - 1)])
    inner = swap(inner, "core", 1)
    low, high = fourier(parity, [rows, rows], [0, 1], waves)
    (inner,) = fourier(parity, [inner[:, None]], [0], waves)
    (outer,) = fourier(parity, [outer[:, None]], [0], waves)
    order = jnp.concatenate([jnp.arange(F, dtype=jnp.int32), core[None]])

    columns, grams = evolve(order, low, high, inner, outer, coef, mask, turn)
    grams = grams.reshape(groups * 2, HALF_ROWS, LANES)
    parts = lax.all_to_all(grams, ("freq", "core"), split_axis=0, concat_axis=0, tiled=True)
    gram = jnp.sum(parts, axis=0)
    parts = parts.reshape(groups, 2, HALF_ROWS, LANES)[:, :, K // 2 + 1]
    scales = jnp.where(core == 0, parts[:, 0], parts[:, 1])
    columns, gram = lax.optimization_barrier((columns, gram))
    columns = lax.all_to_all(columns, "freq", split_axis=0, concat_axis=0, tiled=True)
    gram = quad_sum(gram, "chip", 16, 8)
    gram = quad_sum(gram, "chip", 2, 1)
    gram = gram + swap(gram, "chip", 4)
    parts = [gram, swap(gram, "core", 1)]
    row_scale = math.sqrt(FIELDS * 8 * count * radial)
    inverse, factor = factorize(core, parts, row_scale)
    return apply(inverse, scales, columns), factor[None]


def solution(mesh):
    devices = mesh.devices
    split_mesh = jax.sharding.Mesh(
        devices.reshape(devices.shape[0] // 2, 2, devices.shape[1]), ("chip", "core", "freq")
    )
    return jax.shard_map(
        local,
        mesh=split_mesh,
        in_specs=(
            P("freq", None, None, SPACE, None),
            P(None, None, SPACE, None),
            P(SPACE, None),
            P(),
        ),
        out_specs=(P("freq", None, None, SPACE, None), P("freq", None, None)),
        check_vma=False,
    )
```

```python
from functools import partial
import math

import jax
import jax.numpy as jnp
from jax import lax
from jax.experimental import pallas as pl
from jax.experimental.pallas import tpu as pltpu
from jax.sharding import PartitionSpec as P

K = 64
FIELDS = 5
NT = 16
F = 8
STEP_DT = 0.25
VISCOSITY = 0.5
LANES = 2 * K
HALF = 4
SPACE = ("chip", "core")
RH = 2
PITCH = 24
TOGETHER = 4
VMEM_LIMIT = 28 * 1024 * 1024


def swap(value, axis, mask):
    count = lax.axis_size(axis)
    return lax.ppermute(value, axis, [(i, i ^ mask) for i in range(count)])


def quad_sum(value, axis, one, two):
    near, far, both = [swap(value, axis, mask) for mask in (one, two, one ^ two)]
    return (value + near) + (far + both)


def spread_body(sketch_ref, out_ref, rows_ref, turned_ref):
    groups = out_ref.shape[0]
    radial = sketch_ref.shape[4]
    per = radial // groups
    rows_ref[...] = sketch_ref[...].astype(jnp.float32).reshape(LANES * 8, radial)
    edge = jnp.zeros((RH * HALF, LANES), jnp.float32)
    for half in range(2):
        turned_ref[half, 0 : RH * HALF, :] = edge
        turned_ref[half, (radial + RH) * HALF :, :] = edge
    for x in range(8):
        block = rows_ref[pl.ds(x, LANES, stride=8), :]
        turned_ref[x // HALF, pl.ds(RH * HALF + x % HALF, radial, stride=HALF), :] = block.T
    count = (per + 2 * RH) * HALF
    for half in range(2):
        for group in range(groups):
            start = group * per * HALF
            out_ref[group, half] = turned_ref[half, start : start + count, :].astype(jnp.bfloat16)


def spread(sketch, groups):
    radial = sketch.shape[4]
    rows = (radial // groups + 2 * RH) * HALF
    return pl.pallas_call(
        spread_body,
        grid=(FIELDS,),
        in_specs=[pl.BlockSpec((2, K, 1, 8, radial), lambda i: (0, 0, i, 0, 0))],
        out_specs=pl.BlockSpec((groups, 2, rows, LANES), lambda i: (0, 0, i, 0)),
        out_shape=jax.ShapeDtypeStruct((groups, 2, FIELDS * rows, LANES), jnp.bfloat16),
        scratch_shapes=[
            pltpu.VMEM((LANES * 8, radial), jnp.float32),
            pltpu.VMEM((2, (radial + 2 * RH) * HALF, LANES), jnp.float32),
        ],
        compiler_params=pltpu.CompilerParams(vmem_limit_bytes=2 * VMEM_LIMIT),
        name="spread",
    )(sketch)


def fourier_body(parity_ref, table_ref, *refs):
    pair_ref = refs[-1]
    groups = len(refs) // 2
    size = pair_ref.shape[2]
    first = lax.broadcasted_iota(jnp.int32, (8, LANES), 1) < K
    for rows_ref, z_ref in zip(refs[:groups], refs[groups : 2 * groups]):

        @pl.loop(0, rows_ref.shape[2] // size)
        def _(step):
            start = pl.multiple_of(step * size, size)
            for d in range(4):
                a = rows_ref[d, 0, pl.ds(start, size), :].astype(jnp.float32)
                b = rows_ref[d + 4, 0, pl.ds(start, size), :].astype(jnp.float32)
                pair_ref[0, d] = a + b
                pair_ref[1, d] = a - b
            for f in range(F):
                parity = parity_ref[f]
                wave = [[jnp.broadcast_to(table_ref[f, c, d : d + 1], (8, LANES)) for d in range(4)] for c in range(2)]
                for line in range(0, size, 8):
                    p = [pair_ref[parity, d, line : line + 8] for d in range(4)]
                    u = (p[0] * wave[0][0] + p[1] * wave[0][1]) + (p[2] * wave[0][2] + p[3] * wave[0][3])
                    v = (p[0] * wave[1][0] + p[1] * wave[1][1]) + (p[2] * wave[1][2] + p[3] * wave[1][3])
                    z_ref[f, pl.ds(start + line, 8), :] = jnp.where(first, u, v) + pltpu.roll(
                        jnp.where(first, v, u), K, 1
                    )


def fourier(parity, rows, parts, table):
    slots, _, count, _ = rows[0].shape
    size = count // FIELDS
    block = lambda part: pl.BlockSpec((slots, 1, count, LANES), lambda i: (0, part, 0, 0))
    return pl.pallas_call(
        fourier_body,
        grid=(1,),
        in_specs=[pl.BlockSpec(memory_space=pltpu.SMEM), pl.BlockSpec(table.shape, lambda i: (0, 0, 0, 0))]
        + [block(part) for part in parts],
        out_specs=[pl.BlockSpec((F, count, LANES), lambda i: (0, 0, 0))] * len(rows),
        out_shape=[jax.ShapeDtypeStruct((F, count, LANES), jnp.float32)] * len(rows),
        scratch_shapes=[pltpu.VMEM((2, 4, size, LANES), jnp.float32)],
        compiler_params=pltpu.CompilerParams(vmem_limit_bytes=VMEM_LIMIT),
        name="fourier",
    )(parity, table, *rows)


def split(value):
    one = value.astype(jnp.bfloat16)
    rest = value - one.astype(jnp.float32)
    two = rest.astype(jnp.bfloat16)
    three = (rest - two.astype(jnp.float32)).astype(jnp.bfloat16)
    return one, two, three


CODE = 524200.0


def encode(block, scale, ref, n):
    total = block.shape[0]
    size = total // FIELDS
    part = size // 4
    for i in range(FIELDS):
        number = jnp.round(block[i * size : (i + 1) * size] * (CODE / scale)).astype(jnp.int32)
        ref[n, i * size : (i + 1) * size, :] = (number >> 4).astype(jnp.int16)
        low = number & 15
        both = (low[:part] << 12) + (low[part : 2 * part] << 8)
        both = both + (low[2 * part : 3 * part] << 4) + low[3 * part :] - 32768
        ref[n, total + i * part : total + (i + 1) * part, :] = both.astype(jnp.int16)


HALF_ROWS = K // 2 + 8


def pack(gram, scale, ref, n):
    line = lax.broadcasted_iota(jnp.int32, (K, LANES), 0)
    lane = lax.broadcasted_iota(jnp.int32, (K, LANES), 1)
    last = pltpu.roll(gram[K:], K, 1)
    both = jnp.where(lane >= line, gram[:K], last)
    diagonal = jnp.sum(jnp.where(lane == line, last, 0.0), axis=0, keepdims=True)
    sub = lax.broadcasted_iota(jnp.int32, (8, LANES), 0)
    for h in range(2):
        ref[n, h, 0 : K // 2, :] = both[h * K // 2 : (h + 1) * K // 2]
        ref[n, h, K // 2 :, :] = jnp.where(sub == 0, diagonal, scale)


def unpack(one, two):
    line = lax.broadcasted_iota(jnp.int32, (K, LANES), 0)
    lane = lax.broadcasted_iota(jnp.int32, (K, LANES), 1)
    top = jnp.concatenate([one[: K // 2], two[: K // 2]], axis=0)
    last = pltpu.roll(jnp.where(lane < line, top, 0.0), K, 1)
    half = jnp.concatenate([jnp.where(lane >= line, top, 0.0), last], axis=0)
    diagonal = pltpu.roll(jnp.broadcast_to(one[K // 2 : K // 2 + 1], (8, LANES)), K, 1)
    diagonal = jnp.concatenate([top] + [diagonal] * (K // 8), axis=0)
    line = lax.broadcasted_iota(jnp.int32, (LANES, LANES), 0)
    lane = lax.broadcasted_iota(jnp.int32, (LANES, LANES), 1)
    return jnp.where(line == lane, diagonal, half + half.T)


def evolve_body(order_ref, *refs):
    layers, turn_refs = refs[: 4 * TOGETHER], refs[4 * TOGETHER : 5 * TOGETHER]
    coef_ref, mask_ref, sent_ref, gram_ref, z_ref, s_ref, out_ref, code_ref, sems = refs[5 * TOGETHER :]
    per = out_ref.shape[1] // (8 * FIELDS)
    wide = per + 2 * RH

    for n in range(TOGETHER):
        low, high, inner, outer = layers[4 * n : 4 * n + 4]
        core = order_ref[F]

        @pl.loop(0, FIELDS)
        def _(field):
            for group, ref in ((1, low), (2, high), (3 - 3 * core, inner), (3 * core, outer)):
                for x in range(HALF):
                    source = field * wide * HALF + x
                    target = pl.multiple_of(8 + PITCH * (group * HALF + x), 8)
                    z_ref[n, field, pl.ds(target - RH, RH), :] = ref[0, pl.ds(source, RH, stride=HALF), :]
                    for r in range(0, per, 8):
                        z_ref[n, field, pl.ds(target + r, 8), :] = ref[
                            0, pl.ds(source + (r + RH) * HALF, 8, stride=HALF), :
                        ]
                    z_ref[n, field, pl.ds(target + per, RH), :] = ref[
                        0, pl.ds(source + (per + RH) * HALF, RH, stride=HALF), :
                    ]

    turns = [ref[0] for ref in turn_refs]

    def advance(ref, line, place, store):
        q = [[ref[n, j, pl.ds(line, 8), :] for j in range(FIELDS)] for n in range(TOGETHER)]
        for i in range(FIELDS):
            coupled = [coef_ref[j * FIELDS + i, pl.ds(place, 8), :] for j in range(FIELDS)]
            moves = [coef_ref[FIELDS * FIELDS + m, pl.ds(place, 8), :] for m in range(4)]
            for n in range(TOGETHER):
                value = coupled[0] * q[n][0]
                for j in range(1, FIELDS):
                    value = value + coupled[j] * q[n][j]
                for m, shift in enumerate((1, -1, 2, -2)):
                    value = value + moves[m] * ref[n, i, pl.ds(line + PITCH * shift, 8), :]
                side = ref[n, i, pl.ds(line - 1, 8), :] + ref[n, i, pl.ds(line + 1, 8), :]
                value = value + (STEP_DT * VISCOSITY) * side
                store(n, i, value + turns[n] * pltpu.roll(q[n][i], K, 1))

    def first_step(place):
        mask = mask_ref[pl.ds(place, 8), :]

        def store(n, i, value):
            s_ref[n, i, pl.ds(place, 8), :] = value * mask

        advance(z_ref, pl.multiple_of(place + 2 * PITCH, 8), place, store)

    @pl.loop(0, 12)
    def _(x):
        for r in range(0, per, 8):
            first_step(pl.multiple_of(8 + PITCH * x + r, 8))

    @pl.loop(1, 10)
    def _(x):
        first_step(pl.multiple_of(8 + PITCH * x + per, 8))

    @pl.loop(0, 8)
    def _(x):
        for r in range(0, per, 8):
            line = pl.multiple_of(8 + PITCH * (x + 2) + r, 8)

            def store(n, i, value):
                out_ref[n, pl.ds(pl.multiple_of((i * 8 + x) * per + r, 8), 8), :] = value

            advance(s_ref, line, line, store)

    step = pl.program_id(0)
    copy = lambda step, n: pltpu.make_async_copy(code_ref.at[n], sent_ref.at[step * TOGETHER + n], sems.at[n])

    @pl.when(step > 0)
    def _():
        for n in range(TOGETHER):
            copy(step - 1, n).wait()

    scales = []
    for n in range(TOGETHER):
        block = out_ref[n]
        scales.append(jnp.maximum(jnp.max(jnp.abs(block), axis=0, keepdims=True), 1e-30))
        encode(block, scales[n], code_ref, n)
        copy(step, n).start()
    for n in range(TOGETHER):
        one, two, three = split(out_ref[n])
        pair = jnp.concatenate([one, two], axis=1)
        contract = (((0,), (0,)), ((), ()))
        wide = lax.dot_general(pair, pair, contract, preferred_element_type=jnp.float32)
        thin = lax.dot_general(one, three, contract, preferred_element_type=jnp.float32)
        cross = wide[:LANES, LANES:] + thin
        gram = wide[:LANES, :LANES] + (cross + cross.T + wide[LANES:, LANES:])
        pack(gram, scales[n], gram_ref, n)

    @pl.when(step == pl.num_programs(0) - 1)
    def _():
        for n in range(TOGETHER):
            copy(step, n).wait()


def evolve(order, low, high, inner, outer, coef, mask, turn):
    count = order.shape[0] - 1
    rows = low.shape[1]
    per = rows // (FIELDS * HALF) - 2 * RH
    whole = lambda shape: pl.BlockSpec(shape, lambda i, order: (0,) * len(shape))
    pick = lambda shape, n: pl.BlockSpec((1,) + shape, lambda i, order: (order[TOGETHER * i + n], 0, 0))
    layers = [pick((rows, LANES), n) for n in range(TOGETHER) for _ in range(4)]
    return pl.pallas_call(
        evolve_body,
        grid_spec=pltpu.PrefetchScalarGridSpec(
            num_scalar_prefetch=1,
            grid=(count // TOGETHER,),
            in_specs=layers
            + [pick((8, LANES), n) for n in range(TOGETHER)]
            + [whole(coef.shape), whole(mask.shape)],
            out_specs=[
                pl.BlockSpec(memory_space=pltpu.HBM),
                pl.BlockSpec((TOGETHER, 2, HALF_ROWS, LANES), lambda i, order: (i, 0, 0, 0)),
            ],
            scratch_shapes=[
                pltpu.VMEM((TOGETHER, FIELDS, 16 + 16 * PITCH, LANES), jnp.float32),
                pltpu.VMEM((TOGETHER, FIELDS, 16 + 12 * PITCH, LANES), jnp.float32),
                pltpu.VMEM((TOGETHER, FIELDS * 8 * per, LANES), jnp.float32),
                pltpu.VMEM((TOGETHER, FIELDS * 10 * per, LANES), jnp.int16),
                pltpu.SemaphoreType.DMA((TOGETHER,)),
            ],
        ),
        out_shape=[
            jax.ShapeDtypeStruct((count, FIELDS * 10 * per, LANES), jnp.int16),
            jax.ShapeDtypeStruct((count, 2, HALF_ROWS, LANES), jnp.float32),
        ],
        compiler_params=pltpu.CompilerParams(vmem_limit_bytes=VMEM_LIMIT),
        name="evolve",
    )(order, *([low, high, inner, outer] * TOGETHER), *([turn] * TOGETHER), coef, mask)


def factor_body(scale, core_ref, *refs):
    parts = refs[:-2]
    inverse_ref, factor_ref = refs[-2:]
    blocks = LANES // 8
    lane = lax.broadcasted_iota(jnp.int32, (8, LANES), 1)
    sub = lax.broadcasted_iota(jnp.int32, (8, LANES), 0)
    mine, other = parts[0][...], parts[1][...]
    lower = jnp.full(mine.shape, core_ref[0], jnp.int32) == 0
    gram = unpack(jnp.where(lower, mine, other), jnp.where(lower, other, mine))
    w = [gram[8 * b : 8 * b + 8] for b in range(blocks)]
    full = lambda v: jnp.broadcast_to(v, (8, LANES))
    for b in range(blocks):
        columns = [[full(w[i][:, 8 * b + k : 8 * b + k + 1]) for k in range(8)] for i in range(b, blocks)]
        rows = [full(w[b][k : k + 1, :]) for k in range(8)]
        a = [[full(columns[0][k][i : i + 1, :]) for k in range(i + 1)] for i in range(8)]
        low = [[None] * 8 for _ in range(8)]
        m = [[None] * 8 for _ in range(8)]
        for j in range(8):
            root = lax.rsqrt(a[j][j])
            root = root * (1.5 - 0.5 * (a[j][j] * root) * root)
            m[j][j] = root
            for i in range(j + 1, 8):
                low[i][j] = a[i][j] * root
            for i in range(j + 1, 8):
                for k in range(j + 1, i + 1):
                    a[i][k] = a[i][k] - low[i][j] * low[k][j]
            for k in range(j):
                total = low[j][k] * m[k][k]
                for n in range(k + 1, j):
                    total = total + low[j][n] * m[n][k]
                m[j][k] = -(total * root)
        inside = (lane >= 8 * b) & (lane < 8 * b + 8)
        ones = [jnp.where(inside, jnp.where(lane == 8 * b + k, 1.0, 0.0), rows[k]) for k in range(8)]
        final = [None] * 8
        upper = None
        lower = None
        for i in range(8):
            top = m[i][0] * rows[0]
            final[i] = m[i][0] * ones[0]
            for k in range(1, i + 1):
                top = top + m[i][k] * rows[k]
                final[i] = final[i] + m[i][k] * ones[k]
            upper = top if i == 0 else jnp.where(sub == i, top, upper)
            lower = final[i] if i == 0 else jnp.where(sub == i, final[i], lower)
        inverse_ref[8 * b : 8 * b + 8, :] = jnp.where(lane <= sub + 8 * b, lower * scale, 0.0)
        factor_ref[8 * b : 8 * b + 8, :] = jnp.where(lane >= sub + 8 * b, upper * (1.0 / scale), 0.0)
        if b + 1 < blocks:
            solved = []
            for k in range(8):
                total = m[k][k] * final[k]
                for i in range(k + 1, 8):
                    total = total + m[i][k] * final[i]
                solved.append(total)
            for i in range(b + 1, blocks):
                c = columns[i - b]
                products = [c[k] * solved[k] for k in range(8)]
                while len(products) > 1:
                    products = [products[n] + products[n + 1] for n in range(0, len(products), 2)]
                w[i] = jnp.where(inside, 0.0, w[i]) - products[0]
    factor_ref[...] = factor_ref[...].T


def factorize(core, parts, scale):
    vmem = pl.BlockSpec(memory_space=pltpu.VMEM)
    shape = jax.ShapeDtypeStruct((LANES, LANES), jnp.float32)
    return pl.pallas_call(
        partial(factor_body, scale),
        in_specs=[pl.BlockSpec(memory_space=pltpu.SMEM)] + [vmem] * len(parts),
        out_specs=[vmem, vmem],
        out_shape=[shape, shape],
        compiler_params=pltpu.CompilerParams(vmem_limit_bytes=8 * 1024 * 1024),
        name="factorize",
    )(core[None], *parts)


def apply_body(inverse_ref, scale_ref, high_ref, low_ref, out_ref, rows_ref):
    per = high_ref.shape[1] // 8
    one, two, three = split(inverse_ref[...].T)
    main = jnp.concatenate([jnp.concatenate([one, two], axis=1)] * 2, axis=0)
    rest = jnp.concatenate([one, three], axis=0)
    for x in range(8):
        shift, half = 12 - 4 * (x // 2), x % 2
        lines = []
        for d in range(F):
            high = high_ref[d, x * per : (x + 1) * per, :].astype(jnp.int32)
            low = low_ref[d, half * per : (half + 1) * per, :].astype(jnp.int32) + 32768
            number = (high << 4) + ((low >> shift) & 15)
            lines.append(number.astype(jnp.float32) * (scale_ref[d : d + 1, :] * (1.0 / CODE)))
        a, b, c = split(jnp.concatenate(lines, axis=0))
        wide = jnp.dot(jnp.concatenate([a, b], axis=1), main, preferred_element_type=jnp.float32)
        tail = jnp.dot(jnp.concatenate([c, a], axis=1), rest, preferred_element_type=jnp.float32)
        value = wide[:, :LANES] + (wide[:, LANES:] + tail)
        rows_ref[pl.ds(x, LANES, stride=8), :] = value.T
    out_ref[...] = rows_ref[...].reshape(out_ref.shape)


def apply(inverse, scales, columns):
    per = columns.shape[1] // (10 * FIELDS)
    radial = per * F
    first_low = 8 * FIELDS * per // (2 * per)
    vmem = pl.BlockSpec(memory_space=pltpu.VMEM)
    return pl.pallas_call(
        apply_body,
        grid=(FIELDS,),
        in_specs=[
            vmem,
            vmem,
            pl.BlockSpec((F, 8 * per, LANES), lambda i: (0, i, 0)),
            pl.BlockSpec((F, 2 * per, LANES), lambda i: (0, first_low + i, 0)),
        ],
        out_specs=pl.BlockSpec((1, LANES, 1, 8, radial), lambda i: (0, 0, i, 0, 0)),
        out_shape=jax.ShapeDtypeStruct((1, LANES, FIELDS, 8, radial), jnp.float32),
        scratch_shapes=[
            pltpu.VMEM((LANES * 8, radial), jnp.float32),
        ],
        compiler_params=pltpu.CompilerParams(vmem_limit_bytes=VMEM_LIMIT),
        name="apply",
    )(inverse, scales, columns, columns)


def make_table(indices, slots):
    times = jnp.arange(slots, dtype=jnp.int32)
    phases = indices[:, None] * times[None, :] % slots
    angles = phases.astype(jnp.float32) * (2.0 * math.pi / slots)
    return jnp.stack([jnp.cos(angles), -jnp.sin(angles)], axis=1)


def stencil_body(place_ref, coupling_ref, velocity_ref, right_ref, left_ref, coef_ref, mask_ref):
    radial = velocity_ref.shape[1]
    cells = radial // F + 2
    start = place_ref[0]
    turn = lax.rem(radial + 1 - start, radial)

    def tiles(index, own):
        gap = jnp.zeros((4, radial), jnp.float32)
        other = jnp.concatenate([right_ref[index], gap, left_ref[index]], axis=0)
        return [pltpu.roll(value, turn, 1) for value in (own, other)]

    def put(ref, lead, t, r, value):
        line = 8 + r - 1
        if t == 0:
            ref[lead + (pl.ds(line + 2 * PITCH, 8, stride=PITCH),)] = value
        elif 1 <= r <= cells - 2:
            ref[lead + (pl.ds(line + 10 * PITCH, 2, stride=PITCH),)] = value[0:2]
            ref[lead + (pl.ds(line, 2, stride=PITCH),)] = value[6:8]

    def spread_lanes(index, t, value):
        for r in range(cells):
            put(coef_ref, (index,), t, r, jnp.broadcast_to(value[:, r : r + 1], (8, LANES)))

    centre = 1.0 - STEP_DT * VISCOSITY * (30.0 / 12.0 + 2.0)

    @pl.loop(0, FIELDS * FIELDS)
    def _(index):
        diagonal = jnp.where(lax.rem(index, FIELDS + 1) == 0, centre, 0.0)
        for t, value in enumerate(tiles(index, coupling_ref[index])):
            spread_lanes(index, t, STEP_DT * value + diagonal)

    near_d, near_c = STEP_DT * 8.0 / 12.0, STEP_DT * VISCOSITY * 16.0 / 12.0
    far_d, far_c = STEP_DT / 12.0, STEP_DT * VISCOSITY / 12.0
    for t, speed in enumerate(tiles(FIELDS * FIELDS, velocity_ref[...])):
        spread_lanes(FIELDS * FIELDS, t, near_d * speed + near_c)
        spread_lanes(FIELDS * FIELDS + 1, t, near_c - near_d * speed)
        spread_lanes(FIELDS * FIELDS + 2, t, -far_d * speed - far_c)
        spread_lanes(FIELDS * FIELDS + 3, t, far_d * speed - far_c)
    sub = lax.broadcasted_iota(jnp.int32, (8, LANES), 0)
    sides = jnp.where(sub < HALF, place_ref[2], place_ref[1])
    for r in range(cells):
        here = start - 1 + r
        inside = jnp.where((here >= 0) & (here < radial), 1, 0)
        put(mask_ref, (), 0, r, jnp.full((8, LANES), inside, jnp.int32).astype(jnp.float32))
        put(mask_ref, (), 1, r, (sides * inside).astype(jnp.float32))


def stencil(coupling, velocity, per):
    count = lax.axis_size(SPACE)
    mine = lax.axis_index(SPACE)
    radial = velocity.shape[1]
    up = [(i, i + 1) for i in range(count - 1)]
    down = [(i + 1, i) for i in range(count - 1)]
    coupling = coupling.reshape(FIELDS * FIELDS, 8, radial)
    edges = [jnp.concatenate([coupling[:, s], velocity[None, s]], axis=0) for s in (slice(0, 2), slice(6, 8))]
    right = lax.ppermute(edges[0], SPACE, down)
    left = lax.ppermute(edges[1], SPACE, up)
    place = jnp.stack([lax.axis_index("freq") * per, (mine > 0).astype(jnp.int32), (mine < count - 1).astype(jnp.int32)])
    vmem = pl.BlockSpec(memory_space=pltpu.VMEM)
    return pl.pallas_call(
        stencil_body,
        in_specs=[pl.BlockSpec(memory_space=pltpu.SMEM)] + [vmem] * 4,
        out_specs=[vmem, vmem],
        out_shape=[
            jax.ShapeDtypeStruct((FIELDS * FIELDS + 4, 16 + 12 * PITCH, LANES), jnp.float32),
            jax.ShapeDtypeStruct((16 + 12 * PITCH, LANES), jnp.float32),
        ],
        compiler_params=pltpu.CompilerParams(vmem_limit_bytes=VMEM_LIMIT),
        name="stencil",
    )(place, coupling, velocity, right, left)


def local(sketch, coupling, velocity, freq_index):
    groups = lax.axis_size("freq")
    count = lax.axis_size(SPACE)
    radial = sketch.shape[4]
    per = radial // groups
    mine = lax.axis_index("freq")

    rows = spread(sketch, groups)
    coupling, velocity, rows = lax.optimization_barrier((coupling, velocity, rows))
    rows = lax.all_to_all(rows, "freq", split_axis=0, concat_axis=0, tiled=True)

    parity = freq_index % 2
    waves = make_table(freq_index, NT)[:, :, : NT // 2].reshape(F, 2, 4, 2)
    waves = jnp.repeat(waves, K, axis=3)
    angular = math.pi / NT * STEP_DT * freq_index.astype(jnp.float32)
    sign = jnp.where(jnp.arange(LANES) < K, 1.0, -1.0).astype(jnp.float32)
    turn = jnp.broadcast_to((angular[:, None] * sign)[:, None, :], (F, 8, LANES))
    coef, mask = stencil(coupling, velocity, per)

    rows, coef, mask, turn, waves, parity = lax.optimization_barrier((rows, coef, mask, turn, waves, parity))
    core = lax.axis_index("core")
    outer = lax.dynamic_index_in_dim(rows, core, 1, keepdims=False)
    inner = lax.dynamic_index_in_dim(rows, 1 - core, 1, keepdims=False)
    outer = lax.ppermute(outer, SPACE, [(i, i + 1 if i % 2 else i - 1) for i in range(1, count - 1)])
    inner = swap(inner, "core", 1)
    low, high, inner = fourier(parity, [rows, rows, inner[:, None]], [0, 1, 0], waves)
    (outer,) = fourier(parity, [outer[:, None]], [0], waves)
    order = jnp.concatenate([jnp.arange(F, dtype=jnp.int32), core[None]])

    columns, grams = evolve(order, low, high, inner, outer, coef, mask, turn)
    grams = grams.reshape(groups * 2, HALF_ROWS, LANES)
    parts = lax.all_to_all(grams, ("freq", "core"), split_axis=0, concat_axis=0, tiled=True)
    gram = jnp.sum(parts, axis=0)
    parts = parts.reshape(groups, 2, HALF_ROWS, LANES)[:, :, K // 2 + 1]
    scales = jnp.where(core == 0, parts[:, 0], parts[:, 1])
    columns, gram = lax.optimization_barrier((columns, gram))
    columns = lax.all_to_all(columns, "freq", split_axis=0, concat_axis=0, tiled=True)
    gram = quad_sum(gram, "chip", 16, 8)
    gram = quad_sum(gram, "chip", 2, 1)
    gram = gram + swap(gram, "chip", 4)
    parts = [gram, swap(gram, "core", 1)]
    row_scale = math.sqrt(FIELDS * 8 * count * radial)
    inverse, factor = factorize(core, parts, row_scale)
    return apply(inverse, scales, columns), factor[None]


def solution(mesh):
    devices = mesh.devices
    split_mesh = jax.sharding.Mesh(
        devices.reshape(devices.shape[0] // 2, 2, devices.shape[1]), ("chip", "core", "freq")
    )
    return jax.shard_map(
        local,
        mesh=split_mesh,
        in_specs=(
            P("freq", None, None, SPACE, None),
            P(None, None, SPACE, None),
            P(SPACE, None),
            P(),
        ),
        out_specs=(P("freq", None, None, SPACE, None), P("freq", None, None)),
        check_vma=False,
    )
```

```python
from functools import partial
import math

import jax
import jax.numpy as jnp
from jax import lax
from jax.experimental import pallas as pl
from jax.experimental.pallas import tpu as pltpu
from jax.sharding import PartitionSpec as P

K = 64
FIELDS = 5
NT = 16
F = 8
STEP_DT = 0.25
VISCOSITY = 0.5
LANES = 2 * K
HALF = 4
SPACE = ("chip", "core")
RH = 2
PITCH = 24
TOGETHER = 4
VMEM_LIMIT = 28 * 1024 * 1024


def swap(value, axis, mask):
    count = lax.axis_size(axis)
    return lax.ppermute(value, axis, [(i, i ^ mask) for i in range(count)])


def quad_sum(value, axis, one, two):
    near, far, both = [swap(value, axis, mask) for mask in (one, two, one ^ two)]
    return (value + near) + (far + both)


def eight_sum(value, axis):
    far = {mask: swap(value, axis, mask) for mask in (4, 7, 3, 5, 2, 6, 1)}
    return ((value + far[1]) + (far[2] + far[3])) + ((far[4] + far[5]) + (far[6] + far[7]))


def spread_body(sketch_ref, out_ref, rows_ref, turned_ref):
    groups = out_ref.shape[0]
    radial = sketch_ref.shape[4]
    per = radial // groups
    rows_ref[...] = sketch_ref[...].astype(jnp.float32).reshape(LANES * 8, radial)
    edge = jnp.zeros((RH * HALF, LANES), jnp.float32)
    for half in range(2):
        turned_ref[half, 0 : RH * HALF, :] = edge
        turned_ref[half, (radial + RH) * HALF :, :] = edge
    for x in range(8):
        block = rows_ref[pl.ds(x, LANES, stride=8), :]
        turned_ref[x // HALF, pl.ds(RH * HALF + x % HALF, radial, stride=HALF), :] = block.T
    count = (per + 2 * RH) * HALF
    for half in range(2):
        for group in range(groups):
            start = group * per * HALF
            out_ref[group, half] = turned_ref[half, start : start + count, :].astype(jnp.bfloat16)


def spread(sketch, groups):
    radial = sketch.shape[4]
    rows = (radial // groups + 2 * RH) * HALF
    return pl.pallas_call(
        spread_body,
        grid=(FIELDS,),
        in_specs=[pl.BlockSpec((2, K, 1, 8, radial), lambda i: (0, 0, i, 0, 0))],
        out_specs=pl.BlockSpec((groups, 2, rows, LANES), lambda i: (0, 0, i, 0)),
        out_shape=jax.ShapeDtypeStruct((groups, 2, FIELDS * rows, LANES), jnp.bfloat16),
        scratch_shapes=[
            pltpu.VMEM((LANES * 8, radial), jnp.float32),
            pltpu.VMEM((2, (radial + 2 * RH) * HALF, LANES), jnp.float32),
        ],
        compiler_params=pltpu.CompilerParams(vmem_limit_bytes=2 * VMEM_LIMIT),
        name="spread",
    )(sketch)


def fourier_body(parity_ref, table_ref, *refs):
    pair_ref = refs[-1]
    groups = len(refs) // 2
    size = pair_ref.shape[2]
    first = lax.broadcasted_iota(jnp.int32, (8, LANES), 1) < K
    for rows_ref, z_ref in zip(refs[:groups], refs[groups : 2 * groups]):

        @pl.loop(0, rows_ref.shape[2] // size)
        def _(step):
            start = pl.multiple_of(step * size, size)
            for d in range(4):
                a = rows_ref[d, 0, pl.ds(start, size), :].astype(jnp.float32)
                b = rows_ref[d + 4, 0, pl.ds(start, size), :].astype(jnp.float32)
                pair_ref[0, d] = a + b
                pair_ref[1, d] = a - b
            for f in range(F):
                parity = parity_ref[f]
                wave = [[jnp.broadcast_to(table_ref[f, c, d : d + 1], (8, LANES)) for d in range(4)] for c in range(2)]
                for line in range(0, size, 8):
                    p = [pair_ref[parity, d, line : line + 8] for d in range(4)]
                    u = (p[0] * wave[0][0] + p[1] * wave[0][1]) + (p[2] * wave[0][2] + p[3] * wave[0][3])
                    v = (p[0] * wave[1][0] + p[1] * wave[1][1]) + (p[2] * wave[1][2] + p[3] * wave[1][3])
                    z_ref[f, pl.ds(start + line, 8), :] = jnp.where(first, u, v) + pltpu.roll(
                        jnp.where(first, v, u), K, 1
                    )


def fourier(parity, rows, parts, table):
    slots, _, count, _ = rows[0].shape
    size = count // FIELDS
    block = lambda part: pl.BlockSpec((slots, 1, count, LANES), lambda i: (0, part, 0, 0))
    return pl.pallas_call(
        fourier_body,
        grid=(1,),
        in_specs=[pl.BlockSpec(memory_space=pltpu.SMEM), pl.BlockSpec(table.shape, lambda i: (0, 0, 0, 0))]
        + [block(part) for part in parts],
        out_specs=[pl.BlockSpec((F, count, LANES), lambda i: (0, 0, 0))] * len(rows),
        out_shape=[jax.ShapeDtypeStruct((F, count, LANES), jnp.float32)] * len(rows),
        scratch_shapes=[pltpu.VMEM((2, 4, size, LANES), jnp.float32)],
        compiler_params=pltpu.CompilerParams(vmem_limit_bytes=VMEM_LIMIT),
        name="fourier",
    )(parity, table, *rows)


def split(value):
    one = value.astype(jnp.bfloat16)
    rest = value - one.astype(jnp.float32)
    two = rest.astype(jnp.bfloat16)
    three = (rest - two.astype(jnp.float32)).astype(jnp.bfloat16)
    return one, two, three


CODE = 524200.0


def encode(block, scale, ref, n):
    total = block.shape[0]
    size = total // FIELDS
    part = size // 4
    for i in range(FIELDS):
        number = jnp.round(block[i * size : (i + 1) * size] * (CODE / scale)).astype(jnp.int32)
        ref[n, i * size : (i + 1) * size, :] = (number >> 4).astype(jnp.int16)
        low = number & 15
        both = (low[:part] << 12) + (low[part : 2 * part] << 8)
        both = both + (low[2 * part : 3 * part] << 4) + low[3 * part :] - 32768
        ref[n, total + i * part : total + (i + 1) * part, :] = both.astype(jnp.int16)


HALF_ROWS = K // 2 + 8


def pack(gram, scale, ref, n):
    line = lax.broadcasted_iota(jnp.int32, (K, LANES), 0)
    lane = lax.broadcasted_iota(jnp.int32, (K, LANES), 1)
    last = pltpu.roll(gram[K:], K, 1)
    both = jnp.where(lane >= line, gram[:K], last)
    diagonal = jnp.sum(jnp.where(lane == line, last, 0.0), axis=0, keepdims=True)
    sub = lax.broadcasted_iota(jnp.int32, (8, LANES), 0)
    for h in range(2):
        ref[n, h, 0 : K // 2, :] = both[h * K // 2 : (h + 1) * K // 2]
        ref[n, h, K // 2 :, :] = jnp.where(sub == 0, diagonal, scale)


def unpack(one, two):
    line = lax.broadcasted_iota(jnp.int32, (K, LANES), 0)
    lane = lax.broadcasted_iota(jnp.int32, (K, LANES), 1)
    top = jnp.concatenate([one[: K // 2], two[: K // 2]], axis=0)
    last = pltpu.roll(jnp.where(lane < line, top, 0.0), K, 1)
    half = jnp.concatenate([jnp.where(lane >= line, top, 0.0), last], axis=0)
    diagonal = pltpu.roll(jnp.broadcast_to(one[K // 2 : K // 2 + 1], (8, LANES)), K, 1)
    diagonal = jnp.concatenate([top] + [diagonal] * (K // 8), axis=0)
    line = lax.broadcasted_iota(jnp.int32, (LANES, LANES), 0)
    lane = lax.broadcasted_iota(jnp.int32, (LANES, LANES), 1)
    return jnp.where(line == lane, diagonal, half + half.T)


def evolve_body(order_ref, *refs):
    layers, turn_refs = refs[: 4 * TOGETHER], refs[4 * TOGETHER : 5 * TOGETHER]
    coef_ref, mask_ref, sent_ref, gram_ref, z_ref, s_ref, out_ref, code_ref, sems = refs[5 * TOGETHER :]
    per = out_ref.shape[1] // (8 * FIELDS)
    wide = per + 2 * RH

    for n in range(TOGETHER):
        low, high, inner, outer = layers[4 * n : 4 * n + 4]
        core = order_ref[F]

        @pl.loop(0, FIELDS)
        def _(field):
            for group, ref in ((1, low), (2, high), (3 - 3 * core, inner), (3 * core, outer)):
                for x in range(HALF):
                    source = field * wide * HALF + x
                    target = pl.multiple_of(8 + PITCH * (group * HALF + x), 8)
                    z_ref[n, field, pl.ds(target - RH, RH), :] = ref[0, pl.ds(source, RH, stride=HALF), :]
                    for r in range(0, per, 8):
                        z_ref[n, field, pl.ds(target + r, 8), :] = ref[
                            0, pl.ds(source + (r + RH) * HALF, 8, stride=HALF), :
                        ]
                    z_ref[n, field, pl.ds(target + per, RH), :] = ref[
                        0, pl.ds(source + (per + RH) * HALF, RH, stride=HALF), :
                    ]

    turns = [ref[0] for ref in turn_refs]

    def advance(ref, line, place, store):
        q = [[ref[n, j, pl.ds(line, 8), :] for j in range(FIELDS)] for n in range(TOGETHER)]
        for i in range(FIELDS):
            coupled = [coef_ref[j * FIELDS + i, pl.ds(place, 8), :] for j in range(FIELDS)]
            moves = [coef_ref[FIELDS * FIELDS + m, pl.ds(place, 8), :] for m in range(4)]
            for n in range(TOGETHER):
                value = coupled[0] * q[n][0]
                for j in range(1, FIELDS):
                    value = value + coupled[j] * q[n][j]
                for m, shift in enumerate((1, -1, 2, -2)):
                    value = value + moves[m] * ref[n, i, pl.ds(line + PITCH * shift, 8), :]
                side = ref[n, i, pl.ds(line - 1, 8), :] + ref[n, i, pl.ds(line + 1, 8), :]
                value = value + (STEP_DT * VISCOSITY) * side
                store(n, i, value + turns[n] * pltpu.roll(q[n][i], K, 1))

    def first_step(place):
        mask = mask_ref[pl.ds(place, 8), :]

        def store(n, i, value):
            s_ref[n, i, pl.ds(place, 8), :] = value * mask

        advance(z_ref, pl.multiple_of(place + 2 * PITCH, 8), place, store)

    @pl.loop(0, 12)
    def _(x):
        for r in range(0, per, 8):
            first_step(pl.multiple_of(8 + PITCH * x + r, 8))

    @pl.loop(1, 10)
    def _(x):
        first_step(pl.multiple_of(8 + PITCH * x + per, 8))

    @pl.loop(0, 8)
    def _(x):
        for r in range(0, per, 8):
            line = pl.multiple_of(8 + PITCH * (x + 2) + r, 8)

            def store(n, i, value):
                out_ref[n, pl.ds(pl.multiple_of((i * 8 + x) * per + r, 8), 8), :] = value

            advance(s_ref, line, line, store)

    step = pl.program_id(0)
    copy = lambda step, n: pltpu.make_async_copy(code_ref.at[n], sent_ref.at[step * TOGETHER + n], sems.at[n])

    @pl.when(step > 0)
    def _():
        for n in range(TOGETHER):
            copy(step - 1, n).wait()

    scales = []
    for n in range(TOGETHER):
        block = out_ref[n]
        scales.append(jnp.maximum(jnp.max(jnp.abs(block), axis=0, keepdims=True), 1e-30))
        encode(block, scales[n], code_ref, n)
        copy(step, n).start()
    for n in range(TOGETHER):
        one, two, three = split(out_ref[n])
        pair = jnp.concatenate([one, two], axis=1)
        contract = (((0,), (0,)), ((), ()))
        wide = lax.dot_general(pair, pair, contract, preferred_element_type=jnp.float32)
        thin = lax.dot_general(one, three, contract, preferred_element_type=jnp.float32)
        cross = wide[:LANES, LANES:] + thin
        gram = wide[:LANES, :LANES] + (cross + cross.T + wide[LANES:, LANES:])
        pack(gram, scales[n], gram_ref, n)

    @pl.when(step == pl.num_programs(0) - 1)
    def _():
        for n in range(TOGETHER):
            copy(step, n).wait()


def evolve(order, low, high, inner, outer, coef, mask, turn):
    count = order.shape[0] - 1
    rows = low.shape[1]
    per = rows // (FIELDS * HALF) - 2 * RH
    whole = lambda shape: pl.BlockSpec(shape, lambda i, order: (0,) * len(shape))
    pick = lambda shape, n: pl.BlockSpec((1,) + shape, lambda i, order: (order[TOGETHER * i + n], 0, 0))
    layers = [pick((rows, LANES), n) for n in range(TOGETHER) for _ in range(4)]
    return pl.pallas_call(
        evolve_body,
        grid_spec=pltpu.PrefetchScalarGridSpec(
            num_scalar_prefetch=1,
            grid=(count // TOGETHER,),
            in_specs=layers
            + [pick((8, LANES), n) for n in range(TOGETHER)]
            + [whole(coef.shape), whole(mask.shape)],
            out_specs=[
                pl.BlockSpec(memory_space=pltpu.HBM),
                pl.BlockSpec((TOGETHER, 2, HALF_ROWS, LANES), lambda i, order: (i, 0, 0, 0)),
            ],
            scratch_shapes=[
                pltpu.VMEM((TOGETHER, FIELDS, 16 + 16 * PITCH, LANES), jnp.float32),
                pltpu.VMEM((TOGETHER, FIELDS, 16 + 12 * PITCH, LANES), jnp.float32),
                pltpu.VMEM((TOGETHER, FIELDS * 8 * per, LANES), jnp.float32),
                pltpu.VMEM((TOGETHER, FIELDS * 10 * per, LANES), jnp.int16),
                pltpu.SemaphoreType.DMA((TOGETHER,)),
            ],
        ),
        out_shape=[
            jax.ShapeDtypeStruct((count, FIELDS * 10 * per, LANES), jnp.int16),
            jax.ShapeDtypeStruct((count, 2, HALF_ROWS, LANES), jnp.float32),
        ],
        compiler_params=pltpu.CompilerParams(vmem_limit_bytes=VMEM_LIMIT),
        name="evolve",
    )(order, *([low, high, inner, outer] * TOGETHER), *([turn] * TOGETHER), coef, mask)


def factor_body(scale, core_ref, *refs):
    parts = refs[:-2]
    inverse_ref, factor_ref = refs[-2:]
    blocks = LANES // 8
    lane = lax.broadcasted_iota(jnp.int32, (8, LANES), 1)
    sub = lax.broadcasted_iota(jnp.int32, (8, LANES), 0)
    mine, other = parts[0][...], parts[1][...]
    lower = jnp.full(mine.shape, core_ref[0], jnp.int32) == 0
    gram = unpack(jnp.where(lower, mine, other), jnp.where(lower, other, mine))
    w = [gram[8 * b : 8 * b + 8] for b in range(blocks)]
    full = lambda v: jnp.broadcast_to(v, (8, LANES))
    for b in range(blocks):
        columns = [[full(w[i][:, 8 * b + k : 8 * b + k + 1]) for k in range(8)] for i in range(b, blocks)]
        rows = [full(w[b][k : k + 1, :]) for k in range(8)]
        a = [[full(columns[0][k][i : i + 1, :]) for k in range(i + 1)] for i in range(8)]
        low = [[None] * 8 for _ in range(8)]
        m = [[None] * 8 for _ in range(8)]
        for j in range(8):
            root = lax.rsqrt(a[j][j])
            root = root * (1.5 - 0.5 * (a[j][j] * root) * root)
            m[j][j] = root
            for i in range(j + 1, 8):
                low[i][j] = a[i][j] * root
            for i in range(j + 1, 8):
                for k in range(j + 1, i + 1):
                    a[i][k] = a[i][k] - low[i][j] * low[k][j]
            for k in range(j):
                total = low[j][k] * m[k][k]
                for n in range(k + 1, j):
                    total = total + low[j][n] * m[n][k]
                m[j][k] = -(total * root)
        inside = (lane >= 8 * b) & (lane < 8 * b + 8)
        ones = [jnp.where(inside, jnp.where(lane == 8 * b + k, 1.0, 0.0), rows[k]) for k in range(8)]
        final = [None] * 8
        upper = None
        lower = None
        for i in range(8):
            top = m[i][0] * rows[0]
            final[i] = m[i][0] * ones[0]
            for k in range(1, i + 1):
                top = top + m[i][k] * rows[k]
                final[i] = final[i] + m[i][k] * ones[k]
            upper = top if i == 0 else jnp.where(sub == i, top, upper)
            lower = final[i] if i == 0 else jnp.where(sub == i, final[i], lower)
        inverse_ref[8 * b : 8 * b + 8, :] = jnp.where(lane <= sub + 8 * b, lower * scale, 0.0)
        factor_ref[8 * b : 8 * b + 8, :] = jnp.where(lane >= sub + 8 * b, upper * (1.0 / scale), 0.0)
        if b + 1 < blocks:
            solved = []
            for k in range(8):
                total = m[k][k] * final[k]
                for i in range(k + 1, 8):
                    total = total + m[i][k] * final[i]
                solved.append(total)
            for i in range(b + 1, blocks):
                c = columns[i - b]
                products = [c[k] * solved[k] for k in range(8)]
                while len(products) > 1:
                    products = [products[n] + products[n + 1] for n in range(0, len(products), 2)]
                w[i] = jnp.where(inside, 0.0, w[i]) - products[0]
    factor_ref[...] = factor_ref[...].T


def factorize(core, parts, scale):
    vmem = pl.BlockSpec(memory_space=pltpu.VMEM)
    shape = jax.ShapeDtypeStruct((LANES, LANES), jnp.float32)
    return pl.pallas_call(
        partial(factor_body, scale),
        in_specs=[pl.BlockSpec(memory_space=pltpu.SMEM)] + [vmem] * len(parts),
        out_specs=[vmem, vmem],
        out_shape=[shape, shape],
        compiler_params=pltpu.CompilerParams(vmem_limit_bytes=8 * 1024 * 1024),
        name="factorize",
    )(core[None], *parts)


def apply_body(inverse_ref, scale_ref, high_ref, low_ref, out_ref, rows_ref, main_ref, rest_ref):
    per = high_ref.shape[1] // 8

    @pl.when(pl.program_id(0) == 0)
    def _():
        one, two, three = split(inverse_ref[...].T)
        main_ref[...] = jnp.concatenate([jnp.concatenate([one, two], axis=1)] * 2, axis=0)
        rest_ref[...] = jnp.concatenate([one, three], axis=0)

    main, rest = main_ref[...], rest_ref[...]
    for x in range(8):
        shift, half = 12 - 4 * (x // 2), x % 2
        lines = []
        for d in range(F):
            high = high_ref[d, x * per : (x + 1) * per, :].astype(jnp.int32)
            low = low_ref[d, half * per : (half + 1) * per, :].astype(jnp.int32) + 32768
            number = (high << 4) + ((low >> shift) & 15)
            lines.append(number.astype(jnp.float32) * (scale_ref[d : d + 1, :] * (1.0 / CODE)))
        a, b, c = split(jnp.concatenate(lines, axis=0))
        wide = jnp.dot(jnp.concatenate([a, b], axis=1), main, preferred_element_type=jnp.float32)
        tail = jnp.dot(jnp.concatenate([c, a], axis=1), rest, preferred_element_type=jnp.float32)
        value = wide[:, :LANES] + (wide[:, LANES:] + tail)
        rows_ref[pl.ds(x, LANES, stride=8), :] = value.T
    out_ref[...] = rows_ref[...].reshape(out_ref.shape)


def apply(inverse, scales, columns):
    per = columns.shape[1] // (10 * FIELDS)
    radial = per * F
    first_low = 8 * FIELDS * per // (2 * per)
    vmem = pl.BlockSpec(memory_space=pltpu.VMEM)
    return pl.pallas_call(
        apply_body,
        grid=(FIELDS,),
        in_specs=[
            vmem,
            vmem,
            pl.BlockSpec((F, 8 * per, LANES), lambda i: (0, i, 0)),
            pl.BlockSpec((F, 2 * per, LANES), lambda i: (0, first_low + i, 0)),
        ],
        out_specs=pl.BlockSpec((1, LANES, 1, 8, radial), lambda i: (0, 0, i, 0, 0)),
        out_shape=jax.ShapeDtypeStruct((1, LANES, FIELDS, 8, radial), jnp.float32),
        scratch_shapes=[
            pltpu.VMEM((LANES * 8, radial), jnp.float32),
            pltpu.VMEM((2 * LANES, 2 * LANES), jnp.bfloat16),
            pltpu.VMEM((2 * LANES, LANES), jnp.bfloat16),
        ],
        compiler_params=pltpu.CompilerParams(vmem_limit_bytes=VMEM_LIMIT),
        name="apply",
    )(inverse, scales, columns, columns)


def make_table(indices, slots):
    times = jnp.arange(slots, dtype=jnp.int32)
    phases = indices[:, None] * times[None, :] % slots
    angles = phases.astype(jnp.float32) * (2.0 * math.pi / slots)
    return jnp.stack([jnp.cos(angles), -jnp.sin(angles)], axis=1)


def stencil_body(place_ref, coupling_ref, velocity_ref, right_ref, left_ref, coef_ref, mask_ref):
    radial = velocity_ref.shape[1]
    cells = radial // F + 2
    start = place_ref[0]
    turn = lax.rem(radial + 1 - start, radial)

    def tiles(index, own):
        gap = jnp.zeros((4, radial), jnp.float32)
        other = jnp.concatenate([right_ref[index], gap, left_ref[index]], axis=0)
        return [pltpu.roll(value, turn, 1) for value in (own, other)]

    def put(ref, lead, t, r, value):
        line = 8 + r - 1
        if t == 0:
            ref[lead + (pl.ds(line + 2 * PITCH, 8, stride=PITCH),)] = value
        elif 1 <= r <= cells - 2:
            ref[lead + (pl.ds(line + 10 * PITCH, 2, stride=PITCH),)] = value[0:2]
            ref[lead + (pl.ds(line, 2, stride=PITCH),)] = value[6:8]

    def spread_lanes(index, t, value):
        for r in range(cells):
            put(coef_ref, (index,), t, r, jnp.broadcast_to(value[:, r : r + 1], (8, LANES)))

    centre = 1.0 - STEP_DT * VISCOSITY * (30.0 / 12.0 + 2.0)

    @pl.loop(0, FIELDS * FIELDS)
    def _(index):
        diagonal = jnp.where(lax.rem(index, FIELDS + 1) == 0, centre, 0.0)
        for t, value in enumerate(tiles(index, coupling_ref[index])):
            spread_lanes(index, t, STEP_DT * value + diagonal)

    near_d, near_c = STEP_DT * 8.0 / 12.0, STEP_DT * VISCOSITY * 16.0 / 12.0
    far_d, far_c = STEP_DT / 12.0, STEP_DT * VISCOSITY / 12.0
    for t, speed in enumerate(tiles(FIELDS * FIELDS, velocity_ref[...])):
        spread_lanes(FIELDS * FIELDS, t, near_d * speed + near_c)
        spread_lanes(FIELDS * FIELDS + 1, t, near_c - near_d * speed)
        spread_lanes(FIELDS * FIELDS + 2, t, -far_d * speed - far_c)
        spread_lanes(FIELDS * FIELDS + 3, t, far_d * speed - far_c)
    sub = lax.broadcasted_iota(jnp.int32, (8, LANES), 0)
    sides = jnp.where(sub < HALF, place_ref[2], place_ref[1])
    for r in range(cells):
        here = start - 1 + r
        inside = jnp.where((here >= 0) & (here < radial), 1, 0)
        put(mask_ref, (), 0, r, jnp.full((8, LANES), inside, jnp.int32).astype(jnp.float32))
        put(mask_ref, (), 1, r, (sides * inside).astype(jnp.float32))


def stencil(coupling, velocity, per):
    count = lax.axis_size(SPACE)
    mine = lax.axis_index(SPACE)
    radial = velocity.shape[1]
    up = [(i, i + 1) for i in range(count - 1)]
    down = [(i + 1, i) for i in range(count - 1)]
    coupling = coupling.reshape(FIELDS * FIELDS, 8, radial)
    edges = [jnp.concatenate([coupling[:, s], velocity[None, s]], axis=0) for s in (slice(0, 2), slice(6, 8))]
    right = lax.ppermute(edges[0], SPACE, down)
    left = lax.ppermute(edges[1], SPACE, up)
    place = jnp.stack([lax.axis_index("freq") * per, (mine > 0).astype(jnp.int32), (mine < count - 1).astype(jnp.int32)])
    vmem = pl.BlockSpec(memory_space=pltpu.VMEM)
    return pl.pallas_call(
        stencil_body,
        in_specs=[pl.BlockSpec(memory_space=pltpu.SMEM)] + [vmem] * 4,
        out_specs=[vmem, vmem],
        out_shape=[
            jax.ShapeDtypeStruct((FIELDS * FIELDS + 4, 16 + 12 * PITCH, LANES), jnp.float32),
            jax.ShapeDtypeStruct((16 + 12 * PITCH, LANES), jnp.float32),
        ],
        compiler_params=pltpu.CompilerParams(vmem_limit_bytes=VMEM_LIMIT),
        name="stencil",
    )(place, coupling, velocity, right, left)


def local(sketch, coupling, velocity, freq_index):
    groups = lax.axis_size("freq")
    count = lax.axis_size(SPACE)
    radial = sketch.shape[4]
    per = radial // groups
    mine = lax.axis_index("freq")

    rows = spread(sketch, groups)
    coupling, velocity, rows = lax.optimization_barrier((coupling, velocity, rows))
    rows = lax.all_to_all(rows, "freq", split_axis=0, concat_axis=0, tiled=True)

    parity = freq_index % 2
    waves = make_table(freq_index, NT)[:, :, : NT // 2].reshape(F, 2, 4, 2)
    waves = jnp.repeat(waves, K, axis=3)
    angular = math.pi / NT * STEP_DT * freq_index.astype(jnp.float32)
    sign = jnp.where(jnp.arange(LANES) < K, 1.0, -1.0).astype(jnp.float32)
    turn = jnp.broadcast_to((angular[:, None] * sign)[:, None, :], (F, 8, LANES))
    coef, mask = stencil(coupling, velocity, per)

    rows, coef, mask, turn, waves, parity = lax.optimization_barrier((rows, coef, mask, turn, waves, parity))
    core = lax.axis_index("core")
    outer = lax.dynamic_index_in_dim(rows, core, 1, keepdims=False)
    inner = lax.dynamic_index_in_dim(rows, 1 - core, 1, keepdims=False)
    outer = lax.ppermute(outer, SPACE, [(i, i + 1 if i % 2 else i - 1) for i in range(1, count - 1)])
    inner = swap(inner, "core", 1)
    low, high, inner = fourier(parity, [rows, rows, inner[:, None]], [0, 1, 0], waves)
    (outer,) = fourier(parity, [outer[:, None]], [0], waves)
    order = jnp.concatenate([jnp.arange(F, dtype=jnp.int32), core[None]])

    columns, grams = evolve(order, low, high, inner, outer, coef, mask, turn)
    grams = grams.reshape(groups * 2, HALF_ROWS, LANES)
    parts = lax.all_to_all(grams, ("freq", "core"), split_axis=0, concat_axis=0, tiled=True)
    gram = jnp.sum(parts, axis=0)
    parts = parts.reshape(groups, 2, HALF_ROWS, LANES)[:, :, K // 2 + 1]
    scales = jnp.where(core == 0, parts[:, 0], parts[:, 1])
    columns, gram = lax.optimization_barrier((columns, gram))
    columns = lax.all_to_all(columns, "freq", split_axis=0, concat_axis=0, tiled=True)
    gram = quad_sum(gram, "chip", 16, 8)
    gram = eight_sum(gram, "chip")
    parts = [gram, swap(gram, "core", 1)]
    row_scale = math.sqrt(FIELDS * 8 * count * radial)
    inverse, factor = factorize(core, parts, row_scale)
    return apply(inverse, scales, columns), factor[None]


def solution(mesh):
    devices = mesh.devices
    split_mesh = jax.sharding.Mesh(
        devices.reshape(devices.shape[0] // 2, 2, devices.shape[1]), ("chip", "core", "freq")
    )
    return jax.shard_map(
        local,
        mesh=split_mesh,
        in_specs=(
            P("freq", None, None, SPACE, None),
            P(None, None, SPACE, None),
            P(SPACE, None),
            P(),
        ),
        out_specs=(P("freq", None, None, SPACE, None), P("freq", None, None)),
        check_vma=False,
    )
```
